32 devices in a mesh: fsdp: 4 (over x, core), ctx: 8 (over z, y).
Axes of the slice: x: 2, y: 2, z: 4, core: 2. Of those that a mesh axis runs over, the one named last changes fastest.
Arguments:
- tokens: bfloat16 [8192, 1024], P(('fsdp', 'ctx')), may hold values from -6 to 6
- segments: int32 [8192], P(('fsdp', 'ctx')), may hold values from 0 to 2047, as said below
- positions: int32 [8192], P(('fsdp', 'ctx')), may hold values from 0 to 4095, as said below
- cotangent: bfloat16 [8192, 1024], P(('fsdp', 'ctx')), may hold values from -12 to 12
- qkv_weight: bfloat16 [1024, 3072], P('fsdp'), may hold values from -0.1875 to 0.1875
- qkv_bias: bfloat16 [3072], P('fsdp'), may hold values from -1.75 to 1.75
- dense_weight: bfloat16 [1024, 1024], P('fsdp'), may hold values from -2 to 2
- dense_bias: bfloat16 [1024], P('fsdp'), may hold values from -1.75 to 1.75
- up_weight: bfloat16 [1024, 4096], P('fsdp'), may hold values from -0.1875 to 0.1875
- up_bias: bfloat16 [4096], P('fsdp'), may hold values from -1.75 to 1.75
- down_weight: bfloat16 [4096, 1024], P('fsdp'), may hold values from -0.09375 to 0.09375
- down_bias: bfloat16 [1024], P('fsdp'), may hold values from -1.75 to 1.75
- norm1_gain: bfloat16 [1024], P('fsdp'), may hold values from 0.25 to 1.75
- norm1_bias: bfloat16 [1024], P('fsdp'), may hold values from -1.75 to 1.75
- norm2_gain: bfloat16 [1024], P('fsdp'), may hold values from 0.25 to 1.75
- norm2_bias: bfloat16 [1024], P('fsdp'), may hold values from -1.75 to 1.75
Outputs:
- layer_out: bfloat16 [8192, 1024], P(('fsdp', 'ctx'))
- grad_tokens: bfloat16 [8192, 1024], P(('fsdp', 'ctx'))
- grad_qkv_weight: float32 [1024, 3072], P('fsdp')
- grad_qkv_bias: float32 [3072], P('fsdp')
- grad_dense_weight: float32 [1024, 1024], P('fsdp')
- grad_dense_bias: float32 [1024], P('fsdp')
- grad_up_weight: float32 [1024, 4096], P('fsdp')
- grad_up_bias: float32 [4096], P('fsdp')
- grad_down_weight: float32 [4096, 1024], P('fsdp')
- grad_down_bias: float32 [1024], P('fsdp')
- grad_norm1_gain: float32 [1024], P('fsdp')
- grad_norm1_bias: float32 [1024], P('fsdp')
- grad_norm2_gain: float32 [1024], P('fsdp')
- grad_norm2_bias: float32 [1024], P('fsdp')
The draws below stay inside these ranges and needn't reach their ends.
Inputs may be any that keep to these rules, and one draw needn't show every extreme that they name: `segments`: within each sequence (the 2048 tokens of one index of fsdp) the numbers start at 0 and never fall; one document begins within its first 256 tokens and ends within its last 256. Within a document the positions rise by one from token to token.
All inputs are finite; a program needn't handle non-finite values.
Results may differ from the reference program's by a relative error of at most 0.024.
Values may be sent and summed in bfloat16 or wider, within the bound.
A program may use at most 192 MiB of HBM per device.

```python
import math
import jax
import jax.numpy as jnp
from jax import lax

D = 1024
H = 16
HD = 64
ROT = 16
FF = 4096
TOK_DEV = 256
TOKENS = 8192
N_FSDP = 4


def document_layout(key):
    seq_len = TOKENS // N_FSDP

    def one_sequence(subkey):
        key_start, key_end, key_breaks, key_offset = jax.random.split(subkey, 4)
        long_start = jax.random.randint(key_start, (), 1, TOK_DEV)
        long_end = seq_len - jax.random.randint(key_end, (), 1, TOK_DEV)
        places = jnp.arange(seq_len, dtype=jnp.int32)
        breaks = jax.random.randint(key_breaks, (seq_len,), 0, 600) == 0
        inside = (places > long_start) & (places < long_end)
        starts = (places == long_start) | (places == long_end) | breaks & jnp.logical_not(inside) & (places > 0)
        doc_ids = jnp.cumsum(starts.astype(jnp.int32)).astype(jnp.int32)
        begins = lax.cummax(jnp.where(starts, places, 0), axis=0)
        last_begin = begins[seq_len - 1]
        doc_ids = jnp.where(places >= last_begin, seq_len - 1, doc_ids).astype(jnp.int32)
        offsets = jax.random.randint(key_offset, (seq_len,), 0, 2048)
        offsets = offsets.at[0].set(0)
        long_offset = seq_len + 2047 - (long_end - 1 - long_start)
        offsets = offsets.at[long_start].set(long_offset)
        return (doc_ids, (places - begins + offsets[begins]).astype(jnp.int32))
    doc_ids, places = jax.vmap(one_sequence)(jax.random.split(key, N_FSDP))
    return (doc_ids.reshape(-1).astype(jnp.int32), places.reshape(-1).astype(jnp.int32))


def draw_segments(key, part):
    return document_layout(key)[0]


def draw_positions(key, part):
    return document_layout(key)[1]


def raised(drawn, key, source, target, parts, factor):
    def block_of(axis_at):
        return (jnp.arange(drawn.shape[axis_at]) // (drawn.shape[axis_at] // parts)).reshape((-1,) + (1,) * (drawn.ndim - 1 - axis_at))

    one_side = jax.random.permutation(key, parts)[block_of(target)]
    far = (block_of(target) + parts // 2) % parts
    return jnp.where((block_of(source) == one_side) | (block_of(source) == far), factor * drawn, drawn)


def shard_levels(stream_key, extent, pieces, low, largest):
    factor_of = 1.0
    for axis_at, shards_of in pieces:
        heights = jax.random.uniform(jax.random.fold_in(jax.random.fold_in(stream_key, 6), axis_at), (shards_of,), jnp.float32, low / len(pieces), largest / len(pieces))
        factor_of = factor_of * jnp.repeat(jnp.exp(heights), extent[axis_at] // shards_of).reshape((-1,) + (1,) * (len(extent) - 1 - axis_at))
    return factor_of


def gaussian(rng, shape, scale, limit, cuts=(), kind=jnp.bfloat16):
    values = jax.random.normal(rng, shape, jnp.float32) * scale
    if len(cuts) > 0:
        values = shard_levels(rng, shape, cuts, -0.22, 0.18) * values
    return jnp.clip(values, min=-limit, max=limit).astype(kind)


def gaussian_with(own_key, shape, width, limit, shards, heavy, kind=jnp.bfloat16):
    array = width * jax.random.normal(own_key, shape, jnp.float32)
    if shards:
        array = array * shard_levels(own_key, shape, shards, -0.22, 0.18)
    return jnp.clip(raised(array, jax.random.fold_in(own_key, 3), *heavy), -limit, limit).astype(kind)


def setup_inputs(seed: int = 0) -> dict:
    key_of = jax.random.split(jax.random.key(seed), 17)
    tokens = gaussian(key_of[0], (TOKENS, D), 1.0, 6.0, ((0, 32),))
    segments = draw_segments(jax.random.fold_in(key_of[16], 71), 0)
    positions = draw_positions(jax.random.fold_in(key_of[16], 71), 0)
    cotangent = gaussian_with(key_of[3], (TOKENS, D), 1.0, 12.0, ((0, 32),), (0, 1, 32, 2.75))
    qkv_weight = gaussian(key_of[4], (D, 3 * D), D ** -0.5, 0.1875, ((0, 4),))
    qkv_bias = gaussian(key_of[5], (3 * D,), 0.3, 1.75, ((0, 4),))
    dense_weight = gaussian(key_of[6], (D, D), (D // 128) ** -0.5, 2.0, ((0, 4),))
    dense_bias = gaussian(key_of[7], (D,), 0.3, 1.75, ((0, 4),))
    up_weight = gaussian(key_of[8], (D, FF), D ** -0.5, 0.1875, ((0, 4),))
    up_bias = gaussian(key_of[9], (FF,), 0.3, 1.75, ((0, 4),))
    down_weight = gaussian(key_of[10], (FF, D), FF ** -0.5, 0.09375, ((0, 4),))
    down_bias = gaussian(key_of[11], (D,), 0.3, 1.75, ((0, 4),))
    norm1_gain = jnp.clip(1.0 + 0.15 * jax.random.normal(key_of[12], (D,), jnp.float32), 0.25, 1.75).astype(jnp.bfloat16)
    norm1_bias = gaussian(key_of[13], (D,), 0.3, 1.75, ((0, 4),))
    norm2_gain = jnp.clip(1.0 + 0.15 * jax.random.normal(key_of[14], (D,), jnp.float32), 0.25, 1.75).astype(jnp.bfloat16)
    norm2_bias = gaussian(key_of[15], (D,), 0.3, 1.75, ((0, 4),))
    return {"tokens": tokens, "segments": segments, "positions": positions, "cotangent": cotangent, "qkv_weight": qkv_weight, "qkv_bias": qkv_bias, "dense_weight": dense_weight, "dense_bias": dense_bias, "up_weight": up_weight, "up_bias": up_bias, "down_weight": down_weight, "down_bias": down_bias, "norm1_gain": norm1_gain, "norm1_bias": norm1_bias, "norm2_gain": norm2_gain, "norm2_bias": norm2_bias}


precise = lax.Precision.HIGHEST
masked_fill = -1e+30
norm_eps = 1e-05

@jax.custom_vjp
def low(v):
    return lax.optimization_barrier(v.astype(jnp.bfloat16)).astype(jnp.float32)

@jax.custom_vjp
def low_back(v):
    return v

def low_keep(v):
    return (low(v), None)

def low_pass(kept, grad):
    return (grad,)

def back_keep(v):
    return (v, None)

def back_low(kept, grad):
    return (low(grad),)
low.defvjp(low_keep, low_pass)
low_back.defvjp(back_keep, back_low)

def layer_norm(inputs, gain_vec, shift_vec):
    center = inputs - lax.optimization_barrier(jnp.mean(inputs, axis=-1, keepdims=True))
    spread = lax.optimization_barrier(jnp.mean(center * center, axis=-1, keepdims=True))
    return center * lax.rsqrt(spread + norm_eps) * gain_vec + shift_vec

def rotary_tables(places):
    half_rot = ROT // 2
    inverse = 10000.0 ** (-2.0 * jnp.arange(half_rot, dtype=jnp.float32) / ROT)
    angles = places.astype(jnp.float32)[:, None] * inverse[None, :]
    angles = jnp.concatenate([angles, angles], axis=1)
    return (jnp.cos(angles), jnp.sin(angles))

def rotate(head_part, cosine_table, sine_table):
    half_rot = ROT // 2
    rotated_part = head_part[..., :ROT]
    turned = jnp.concatenate([-rotated_part[..., half_rot:], rotated_part[..., :half_rot]], axis=-1)
    rotated_part = rotated_part * cosine_table[:, None, :] + turned * sine_table[:, None, :]
    return jnp.concatenate([rotated_part, head_part[..., ROT:]], axis=-1)

def attention(queries, key_rows, values, doc_ids):
    length = queries.shape[0]
    block_rows = math.gcd(length, 512)
    places = jnp.arange(length, dtype=jnp.int32)
    score_scale = 1.0 / math.sqrt(HD)

    def one_block(block_index):
        block_begin = (block_index * block_rows).astype(jnp.int32)
        query_block = lax.dynamic_slice_in_dim(queries, block_begin, block_rows, 0)
        query_place = lax.dynamic_slice_in_dim(places, block_begin, block_rows, 0)
        query_doc = lax.dynamic_slice_in_dim(doc_ids, block_begin, block_rows, 0)
        scores = jnp.einsum('qhd,khd->hqk', query_block, key_rows, precision=precise) * score_scale
        scores = low_back(scores)
        visible = ((places[None, :] <= query_place[:, None]) & (doc_ids[None, :] == query_doc[:, None]))[None]
        row_max = lax.optimization_barrier(jnp.max(jnp.where(visible, scores, masked_fill), axis=-1))
        exp_terms = jnp.where(visible, jnp.exp(jnp.where(visible, scores - row_max[..., None], 0.0)), 0.0)
        row_sum = lax.optimization_barrier(jnp.sum(exp_terms, axis=-1))
        weighted = low_back(jnp.einsum('hqk,khd->qhd', low(exp_terms), values, precision=precise))
        return weighted / jnp.transpose(row_sum)[:, :, None]
    result = lax.map(jax.checkpoint(one_block), jnp.arange(length // block_rows, dtype=jnp.int32))
    return result.reshape(length, queries.shape[1], queries.shape[2])

def forward(params, inputs, doc_ids, places):
    w_qkv, b_qkv, w_dense, b_dense, w_up, b_up, w_down, b_down, gain_one, bias_one, gain_two, bias_two = params
    length = inputs.shape[0]
    normed_one = low(layer_norm(inputs, gain_one, bias_one))
    mixed_proj = low_back(jnp.dot(normed_one, w_qkv, precision=precise) + b_qkv)
    mixed_proj = mixed_proj.reshape(length, H, 3, HD)
    cosine_table, sine_table = rotary_tables(places)
    queries = low(rotate(mixed_proj[:, :, 0], cosine_table, sine_table))
    key_rows = low(rotate(mixed_proj[:, :, 1], cosine_table, sine_table))
    values = low(mixed_proj[:, :, 2])
    context = low(attention(queries, key_rows, values, doc_ids).reshape(length, D))
    attended = jnp.dot(context, w_dense, precision=precise) + b_dense
    normed_two = low(layer_norm(inputs, gain_two, bias_two))
    up_proj = low_back(jnp.dot(normed_two, w_up, precision=precise) + b_up)
    active = low(jax.nn.gelu(up_proj, approximate=False))
    mlp_out = jnp.dot(active, w_down, precision=precise) + b_down
    return inputs + attended + mlp_out

def reference(tokens, segments, positions, cotangent, qkv_weight, qkv_bias, dense_weight, dense_bias, up_weight, up_bias, down_weight, down_bias, norm1_gain, norm1_bias, norm2_gain, norm2_bias):
    params = tuple((weight.astype(jnp.float32) for weight in (qkv_weight, qkv_bias, dense_weight, dense_bias, up_weight, up_bias, down_weight, down_bias, norm1_gain, norm1_bias, norm2_gain, norm2_bias)))
    length = TOKENS // N_FSDP
    inputs_all = tokens.astype(jnp.float32).reshape(N_FSDP, length, D)
    grads_all = cotangent.astype(jnp.float32).reshape(N_FSDP, length, D)
    docs_all = segments.reshape(N_FSDP, length).astype(jnp.int32)
    places_all = positions.reshape(N_FSDP, length).astype(jnp.int32)

    def per_sequence(running_sums, seq_items):
        inputs, doc_ids, places, grad_out = seq_items
        outputs, pull_back = jax.vjp(lambda weights, acts: forward(weights, acts, doc_ids, places), params, inputs)
        weight_grads, input_grad = pull_back(grad_out)
        running_sums = jax.tree.map(lambda running, adding: running + adding, running_sums, weight_grads)
        return (running_sums, (outputs.astype(jnp.bfloat16), input_grad.astype(jnp.bfloat16)))
    initial = tuple((jnp.zeros(weight.shape, jnp.float32) for weight in params))
    sums, (outputs, input_grads) = lax.scan(per_sequence, initial, (inputs_all, docs_all, places_all, grads_all))
    return (outputs.reshape(TOKENS, D), input_grads.reshape(TOKENS, D), sums[0], sums[1], sums[2], sums[3], sums[4], sums[5], sums[6], sums[7], sums[8], sums[9], sums[10], sums[11])
```

```python
import functools
import math

import numpy as np
import jax, jax.numpy as jnp
from jax import lax
from jax.experimental import pallas as pl
from jax.experimental.pallas import tpu as pltpu
from jax.sharding import PartitionSpec as P

HD, ROT = 64, 16
f32, bf16 = jnp.float32, jnp.bfloat16
MESH = pl.DeviceIdType.MESH
vmem = pl.BlockSpec(memory_space=pltpu.VMEM)
hbm = pl.BlockSpec(memory_space=pl.ANY)
norm_eps = 1e-5
masked_fill = -1e30


def nn(a, b):
    return jnp.dot(a, b, preferred_element_type=f32)


def nt(a, b):
    return lax.dot_general(a, b, (((1,), (1,)), ((), ())), preferred_element_type=f32)


def tn(a, b):
    return lax.dot_general(a, b, (((0,), (0,)), ((), ())), preferred_element_type=f32)


def flipped(a, d, n):
    out, bit = 0, 1
    while bit < n:
        out = out + bit * ((a // bit + d // bit) % 2)
        bit *= 2
    return out


def kernel_p(pos, seg, g1, b1, g2, b2, dense, down, qkv, up, pk, vec):
    half, rows = ROT // 2, pos.shape[0]
    row = lax.broadcasted_iota(jnp.int32, (ROT, rows), 0)
    rate = jnp.zeros((ROT, rows), f32)
    for j in range(half):
        rate = jnp.where(row % half == j, float(np.float32(10000.0) ** np.float32(-2.0 * j / ROT)), rate)
    angle = rate * jnp.broadcast_to(pos[...].astype(f32).reshape(1, rows), (ROT, rows))
    pk[0:ROT, :] = jnp.where(row < half, jnp.cos(angle), jnp.sin(angle))
    pk[ROT:, :] = jnp.zeros((8, rows), f32)
    vec[...] = jnp.zeros_like(vec)

    def line(ref):
        return ref[...].astype(f32).reshape(1, ref.shape[0])

    for i, ref in enumerate((g1, b1, g2, b2, seg)):
        pk[ROT + i : ROT + i + 1, :] = line(ref)
    pk[ROT + 5 : ROT + 6, :] = line(dense) + line(down)
    vec[0:1, 0 : qkv.shape[0]] = line(qkv)
    vec[1:2, 0 : up.shape[0]] = line(up)


def call_p(pos, seg, g1, b1, g2, b2, dense, down, qkv, up):
    n = max(qkv.shape[0], up.shape[0])
    return pl.pallas_call(
        kernel_p,
        out_shape=(jax.ShapeDtypeStruct((24, pos.shape[0]), f32), jax.ShapeDtypeStruct((8, n), f32)),
        name="pack",
    )(pos, seg, g1, b1, g2, b2, dense, down, qkv, up)


def rotary_terms(pk):
    rest = pk[0:ROT, :]
    terms = []
    for _ in range(3):
        part = rest.astype(bf16)
        terms.append(part)
        rest = rest - part.astype(f32)
    return jnp.concatenate(terms + [jnp.ones_like(terms[0])], axis=0)


def rotary_pattern():
    e = np.zeros((64, 9 * 128), np.float32)
    for tile in range(3):
        for lane in range(128):
            col = tile * 128 + lane
            part, d = (col % 192) // HD, col % HD
            base = tile * 384 + lane
            if part == 2 or d >= ROT:
                e[48, base] = 1.0
                continue
            for term in range(3):
                e[term * 16 + d % 8, base] = 1.0
                if d < 8:
                    e[term * 16 + 8 + d, base + 128] = -1.0
                else:
                    e[term * 16 + d, base + 256] = 1.0
    return e


def turn(tile, table, t, sign):
    c = table[:, t * 384 : t * 384 + 128]
    up = table[:, t * 384 + 128 : t * 384 + 256]
    dn = table[:, t * 384 + 256 : t * 384 + 384]
    return tile * c + sign * (pltpu.roll(tile, 120, 1) * up + pltpu.roll(tile, 8, 1) * dn)


def key_docs(seg, j, blk):
    return jnp.broadcast_to(seg[j, 4:5, :], (blk, blk)).T


def attention_setup(qkv, gc, seg, kt, vt, gt, c_buf):
    blocks, _, blk, _ = qkv.shape
    for j in range(blocks):
        rows = pl.ds(j * blk, blk)
        kt[:, rows] = qkv[j, 1].astype(f32).T.astype(bf16)
        vt[:, rows] = qkv[j, 2].astype(f32).T.astype(bf16)
        gt[:, rows] = gc[j].astype(f32).T
    c_buf[...] = key_docs(seg, 0, blk)


def attention_block(h, i, qkv, seg, kt, vt, gt, p_buf, s_buf, acc, t_buf, c_buf):
    blocks, _, blk, lanes = qkv.shape
    half = lanes // 2
    lane = lax.broadcasted_iota(jnp.int32, (blk, lanes), 1) // half
    sub = lax.broadcasted_iota(jnp.int32, (lanes, blk), 0) // half
    causal = lax.broadcasted_iota(jnp.int32, (blk, blk), 0) <= lax.broadcasted_iota(jnp.int32, (blk, blk), 1)
    drow = seg[i, 4:5, :]
    own = pl.ds(pl.multiple_of(h * half, half), half)
    rest = pl.ds(pl.multiple_of((1 - h) * half, half), half)
    q_h = jnp.where(lane == h, qkv[i, 0].astype(f32) * 0.125, 0.0).astype(bf16)
    top = jnp.full((8, blk), masked_fill, f32)
    for j in range(i + 1):
        rows = pl.ds(j * blk, blk)
        s = nt(qkv[j, 1], q_h)
        seen = None
        if j == 0:
            seen = c_buf[...] == drow
        elif i == blocks - 1:
            seen = key_docs(seg, j, blk) == drow
        if j == i:
            seen = causal if seen is None else jnp.logical_and(causal, seen)
        if seen is not None:
            s = jnp.where(seen, s, masked_fill)
        s_buf[rows, :] = s
        top = jnp.maximum(top, jnp.max(s.reshape(blk // 8, 8, blk), axis=0))
    top = jnp.max(top, axis=0, keepdims=True)
    total = jnp.zeros((8, blk), f32)
    out = jnp.zeros((half, blk), f32)
    for j in range(i + 1):
        rows = pl.ds(j * blk, blk)
        p = jnp.exp(s_buf[rows, :] - top)
        s_buf[rows, :] = p
        total = total + jnp.sum(p.reshape(blk // 8, 8, blk), axis=0)
        rounded = p.astype(bf16)
        p_buf[j // 4, :, (j % 4) * blk : (j % 4 + 1) * blk] = rounded
        out = out + nn(vt[own, rows], rounded)
    inv = 1.0 / jnp.sum(total, axis=0, keepdims=True)
    out = out * inv
    t_buf[own, :] = out
    g_h = gt[own, i * blk : (i + 1) * blk]
    corr = jnp.sum(g_h * out, axis=0, keepdims=True) * inv
    gw = g_h * inv
    gw = jnp.concatenate([gw, gw], axis=0)
    gw_t = jnp.where(sub == h, gw, 0.0).astype(bf16)
    right = jnp.concatenate([q_h, jnp.where(sub == h, 0.0, gw).T.astype(bf16)], axis=0)
    dq = jnp.zeros((half, blk), f32)
    for j in range(i + 1):
        rows = pl.ds(j * blk, blk)
        ds = (s_buf[rows, :] * (nn(qkv[j, 2], gw_t) - corr)).astype(bf16)
        acc[rows, :] += nn(jnp.concatenate([ds, p_buf[j // 4, :, (j % 4) * blk : (j % 4 + 1) * blk]], axis=1), right)
        dq = dq + nn(kt[own, rows], ds)
    t_buf[rest, :] = dq * 0.125


SUM_AT = (5, 8, 11)


def kernel_m(
    n_f, n_c, n_y,
    x_hbm, dy_hbm, wq_hbm, wu_hbm, wd_hbm, wn_hbm, pk_hbm, pat_ref, vec_ref,
    out_ref, gx_ref, od_hbm, ou_hbm, on_hbm, oq_hbm, sum_ref,
    X, DY, WQ, WU, WD, WN, PK, N1, N2, XH, SQ, SG, ACT, GUP, PT, H2, GAIN, SMALL,
    CT, DQ, OR, HR, ROWS, GD, GU, GN, GQ, YD, YU, YN, YQ, ZD, ZU, ZN, ZQ, FD, FU, FN, FQ, UU, UQ, S1, R1, S2, R2, ES,
    AQ, AG, AS, KT, VT, GT, SB, DK, TB, CB, CX,
    loca, fsa, fra, vs, vr, asa, ara, fs, fr, as_, ar, ys, yr, zs, zr, gs, gr, hs, hr, own,
):
    me_f, me_c = lax.axis_index("fsdp"), lax.axis_index("ctx")
    rows, width = x_hbm.shape
    n_z, last = n_c // n_y, n_c // n_y - 1
    group = n_c // n_f
    qc, uc = WQ.shape[2], WU.shape[2]
    total, cut = n_f * rows, width // n_f

    bar = pltpu.get_barrier_semaphore()
    for d in range(1, n_f):
        pl.semaphore_signal(bar, inc=1, device_id=(flipped(me_f, d, n_f), me_c), device_id_type=MESH)
    for d in range(1, n_c):
        pl.semaphore_signal(bar, inc=1, device_id=(me_f, (me_c + d) % n_c), device_id_type=MESH)

    def cols(ref, i, n):
        return ref.at[:, pl.ds(pl.multiple_of(i * n, 128), n)]

    local = [
        pltpu.make_async_copy(x_hbm, X.at[me_f], loca.at[0]),
        pltpu.make_async_copy(pk_hbm, PK.at[me_f], loca.at[1]),
        pltpu.make_async_copy(cols(wq_hbm, me_f, qc), WQ.at[me_f], loca.at[2]),
        pltpu.make_async_copy(dy_hbm, DY.at[me_f], loca.at[3]),
        pltpu.make_async_copy(wn_hbm, WN, loca.at[4]),
        pltpu.make_async_copy(cols(wu_hbm, me_f, uc), WU.at[me_f], loca.at[5]),
        pltpu.make_async_copy(wd_hbm, WD, loca.at[6]),
    ]
    for cp in local:
        cp.start()
    pl.semaphore_wait(bar, n_f + n_c - 2)

    my_z, my_y = me_c // n_y, me_c % n_y
    other_y = 1 - my_y
    over_y = me_c + 1 - 2 * my_y
    over_z = me_c + n_y * (1 - 2 * (my_z % 2))
    quarter = WQ.shape[1] // 4

    def to_f(kind, d, src, dst, dest=None):
        return pltpu.make_async_remote_copy(
            src_ref=src, dst_ref=dst, send_sem=fsa.at[kind, d], recv_sem=fra.at[kind, d],
            device_id=(flipped(me_f, d, n_f) if dest is None else dest, me_c), device_id_type=MESH,
        )

    def part(ref, c):
        at = 2 * ((c // n_y) % 2) + c % n_y
        return ref.at[pl.ds(pl.multiple_of(at * quarter, 16), quarter)]

    def copy_of(kind, d):
        dest = flipped(me_f, d, n_f)
        if kind in (0, 1, 4):
            src, buf = ((x_hbm, X), (dy_hbm, DY), None, None, (pk_hbm, PK))[kind]
            return to_f(kind, d, src, buf.at[me_f])
        src, buf, n = ((wq_hbm, WQ, qc), (wu_hbm, WU, uc))[kind - 2]
        if d == 1:
            return to_f(kind, d, cols(src, dest, n), buf.at[me_f])
        return to_f(kind, d, cols(part(src, me_c), dest, n), part(buf.at[me_f], me_c))

    def arrival(kind, d):
        buf = (X, DY, WQ, WU, PK)[kind].at[flipped(me_f, d, n_f)]
        if kind in (2, 3) and d > 1:
            buf = part(buf, me_c)
        to_f(kind, d, buf, buf).wait_recv()

    def share(kind, d, way, mine=True):
        to, far = (over_y, over_z, over_z)[way], over_z + 1 - 2 * my_y
        which = (me_c, me_c, over_y)[way] if mine else (over_y, over_z, far)[way]
        buf = part((WQ, WU)[kind - 2].at[flipped(me_f, d, n_f)], which)
        return pltpu.make_async_remote_copy(
            src_ref=buf, dst_ref=buf, send_sem=vs.at[kind - 2, way, d], recv_sem=vr.at[kind - 2, way, d],
            device_id=(me_f, to), device_id_type=MESH,
        )

    def first_shares(kind):
        for d in range(2, n_f):
            arrival(kind, d)
            share(kind, d, 0).start()
            share(kind, d, 1).start()

    def next_shares(kind):
        for d in range(2, n_f):
            share(kind, d, 0, False).wait_recv()
            share(kind, d, 2).start()

    def weights(kind):
        arrival(kind, 1)
        for d in range(2, n_f):
            share(kind, d, 1, False).wait_recv()
            share(kind, d, 2, False).wait_recv()

    def forward(kind, d):
        buf = (X, DY)[kind].at[flipped(me_f, d, n_f)]
        return to_f(kind, d + 1, buf, buf, flipped(me_f, 1, n_f))

    direct = [1] + list(range(2, n_f, 2))
    for kind, to in ((4, range(1, n_f)), (2, (2, 3, 1)), (3, (2, 3, 1)), (0, direct), (1, direct)):
        for d in to:
            copy_of(kind, d).start()

    local[0].wait()
    local[1].wait()
    for d in range(1, n_f):
        arrival(4, d)
    for j in range(n_f):
        GAIN[0:4, j * (width // n_f) : (j + 1) * (width // n_f)] = PK[j, ROT : ROT + 4, :]
    g1, b1, g2, b2 = GAIN[0:1, :], GAIN[1:2, :], GAIN[2:3, :], GAIN[3:4, :]

    def norm_chunk(src):
        v = X[src].astype(f32)
        center = v - jnp.mean(v, axis=-1, keepdims=True)
        xhat = center * lax.rsqrt(jnp.mean(center * center, axis=-1, keepdims=True) + norm_eps)
        N1[src] = (xhat * g1 + b1).astype(bf16)
        N2[src] = (xhat * g2 + b2).astype(bf16)
        XH[src] = xhat.astype(bf16)

    lane_low = lax.broadcasted_iota(jnp.int32, (rows, 128), 1) < HD

    def to_heads(kind, k, src, dst):
        return pltpu.make_async_remote_copy(
            src_ref=src, dst_ref=dst, send_sem=asa.at[kind, k], recv_sem=ara.at[kind, k],
            device_id=(me_f, (me_c + k) % n_c), device_id_type=MESH,
        )

    def heads_arrival(kind):
        src, buf = ((SQ.at[0, 0], AQ), (SG.at[0, 0], AG), (PK.at[0, pl.ds(ROT, 8)], AS))[kind]
        pltpu.make_async_copy(src, buf.at[me_c], asa.at[kind, 0]).wait()
        for k in range(1, n_c):
            to_heads(kind, k, src, buf.at[(me_c - k + n_c) % n_c]).wait_recv()

    def to_c(kind, s, g, src, dst):
        dest = s * group + g
        k = (dest - me_c + n_c) % n_c

        @pl.when(k != 0)
        def _():
            to_heads(kind, k, src, dst).start()

        @pl.when(k == 0)
        def _():
            pltpu.make_async_copy(src, dst, asa.at[kind, 0]).start()

    def qkv_chunk(d, carry):
        s = flipped(me_f, d, n_f)
        table = tn(rotary_terms(PK[s]), pat_ref[...])
        mixed = nn(N1[s], WQ[...].reshape(width, qc)) + vec_ref[0:1, 0:qc]
        for g in range(group):
            t = [turn(mixed[:, g * 384 + i * 128 : g * 384 + (i + 1) * 128], table, i, 1.0) for i in range(3)]
            SQ[s, g, 0] = jnp.where(lane_low, t[0], t[1]).astype(bf16)
            SQ[s, g, 1] = jnp.where(lane_low, pltpu.roll(t[0], 64, 1), pltpu.roll(t[2], 64, 1)).astype(bf16)
            SQ[s, g, 2] = jnp.where(lane_low, t[1], t[2]).astype(bf16)
            to_c(0, s, g, SQ.at[s, g], AQ.at[me_c])
            to_c(2, s, g, PK.at[s, pl.ds(ROT, 8)], AS.at[me_c])
        return carry

    norm_chunk(me_f)
    first_shares(2)
    arrival(0, 1)
    norm_chunk(flipped(me_f, 1, n_f))
    first_shares(3)
    next_shares(2)
    next_shares(3)
    local[2].wait()
    weights(2)
    lax.fori_loop(0, 2, qkv_chunk, 0)
    for d in range(2, n_f):
        arrival(0, d)
        if d % 2 == 0:
            forward(0, d).start()
        norm_chunk(flipped(me_f, d, n_f))
        lax.fori_loop(d, d + 1, qkv_chunk, 0)
    local[3].wait()
    local[4].wait()
    for d in range(1, n_f):
        arrival(1, d)
        if d % 2 == 0:
            forward(1, d).start()

    def gc_chunk(d, carry):
        s = flipped(me_f, d, n_f)
        gc = nt(DY[s], WN[...])
        for g in range(group):
            SG[s, g] = gc[:, g * 128 : (g + 1) * 128].astype(bf16)
            to_c(1, s, g, SG.at[s, g], AG.at[me_c])
        return carry

    lax.fori_loop(0, n_f, gc_chunk, 0)
    local[5].wait()
    local[6].wait()
    weights(3)
    SMALL[...] = jnp.zeros_like(SMALL)

    def mlp_chunk(s, carry):
        up = nn(N2[s], WU[...].reshape(width, uc)) + vec_ref[1:2, 0:uc]
        cdf = 0.5 * (1.0 + lax.erf(up * (2.0 ** -0.5)))
        ACT[s] = (up * cdf).astype(bf16)
        slope = cdf + up * jnp.exp(-0.5 * up * up) * ((2.0 * np.pi) ** -0.5)
        gu = (nt(DY[s], WD[...]) * slope).astype(bf16)
        GUP[s] = gu
        SMALL[0:1, 0:uc] += jnp.sum(gu.astype(f32), axis=0, keepdims=True)
        SMALL[1:2, 0:width] += jnp.sum(DY[s].astype(f32), axis=0, keepdims=True)
        PT[s] = nn(ACT[s], WD[...]).astype(bf16)
        e = nt(GUP[s], WU[...].reshape(width, uc))
        SMALL[2:3, 0:width] += jnp.sum(e * XH[s].astype(f32), axis=0, keepdims=True)
        SMALL[3:4, 0:width] += jnp.sum(e, axis=0, keepdims=True)
        H2[s] = (e * g2).astype(bf16)
        return carry

    lax.fori_loop(0, n_f, mlp_chunk, 0)

    def down_grad(r, carry):
        at = pl.ds(pl.multiple_of(r * 256, 256), 256)
        per = 256 // (uc // n_c)
        res = tn(ACT[:, :, at].reshape(total, 256), DY[...].reshape(total, width)).astype(bf16)
        GD[pl.ds(r * per, per)] = res.reshape(per, uc // n_c, width)
        return carry

    def up_grad(r, carry):
        at = pl.ds(pl.multiple_of(r * 256, 256), 256)
        res = tn(N2[:, :, at].reshape(total, 256), GUP[...].reshape(total, uc)).astype(bf16)
        GU[:, r] = res.reshape(n_c, 256 // n_c, uc)
        return carry

    def remote(src, dst, ssem, rsem, dev):
        return pltpu.make_async_remote_copy(
            src_ref=src, dst_ref=dst, send_sem=ssem, recv_sem=rsem, device_id=dev, device_id_type=MESH)

    def result(pair, h, i):
        return GUP.at[2 * pair + h, :, pl.ds(pl.multiple_of(i * 128, 128), 128)]

    def back(pair, h, k, i):
        return remote(result(pair, h, i), (CT, DQ)[pair].at[me_c // group, me_c % group, h], as_.at[2 * pair + h, k],
                      ar.at[2 * pair + h, k], (me_f, (me_c + k) % n_c))

    def back_own(pair, h, i):
        return pltpu.make_async_copy(
            result(pair, h, i), (CT, DQ)[pair].at[me_c // group, me_c % group, h], as_.at[2 * pair + h, 0])

    def back_arrival(pair, h):
        back_own(pair, h, me_c).wait()
        for k in range(1, n_c):
            src = (me_c - k + n_c) % n_c
            buf = (CT, DQ)[pair].at[src // group, src % group, h]
            remote(buf, buf, as_.at[2 * pair + h, k], ar.at[2 * pair + h, k], (me_f, src)).wait_recv()

    def give(pair, h, t):
        i = (me_c + 1 + t) % n_c

        @pl.when(t < n_c - 1)
        def _():
            back(pair, h, t + 1, i).start()

        @pl.when(t == n_c - 1)
        def _():
            back_own(pair, h, i).start()

    G, YR, ZI, FP = (GD, GU, GN, GQ), (YD, YU, YN, YQ), (ZD, ZU, ZN, ZQ), (FD, FU, FN, FQ)
    UA, OUT = (None, UU, None, UQ), (od_hbm, ou_hbm, on_hbm, oq_hbm)
    low_half = 1 - my_z // (n_z // 2)

    def order(k):
        if k == last:
            return my_z
        down = last - k - (my_z - (last - k) + n_z) // n_z
        up = k + (k - my_z + n_z) // n_z
        return low_half * down + (1 - low_half) * up

    def toward(z):
        return (z - my_z + n_z) // n_z

    @pl.when(my_z == 0)
    def _():
        for buf in ZI:
            buf[1] = jnp.zeros(buf.shape[1:], bf16)

    @pl.when(my_z == last)
    def _():
        for buf in ZI:
            buf[0] = jnp.zeros(buf.shape[1:], bf16)

    def line_wait(item, way, z):
        @pl.when(jnp.logical_or(jnp.logical_and(way == 1, my_z > 0), jnp.logical_and(way == 0, my_z < last)))
        def _():
            line_copy(item, way, z, ZI[item].at[way, z]).wait_recv()

    def line_copy(item, way, z, src):
        return remote(src, ZI[item].at[way, z], zs.at[item, z], zr.at[item, way, z],
                      (me_f, (my_z + 2 * way - 1) * n_y + my_y))

    def y_send(item, z):
        src = G[item]
        return remote(src.at[z * n_y + other_y], YR[item].at[z], ys.at[item, z], yr.at[item, z],
                      (me_f, my_z * n_y + other_y))

    def y_start(item, k):
        y_send(item, order(k)).start()

    def y_sum(item, k):
        z = order(k)
        way = toward(z)
        y_send(item, z).wait_recv()
        line_wait(item, way, z)
        acc = YR[item][z].astype(f32) + G[item][z * n_y + my_y].astype(f32) + ZI[item][way, z].astype(f32)
        YR[item][z] = acc.astype(bf16)
        line_copy(item, way, z, YR[item].at[z]).start()

    def piece_total(item):
        y_send(item, my_z).wait_recv()
        for way in (0, 1):
            line_wait(item, way, my_z)
        acc = YR[item][my_z].astype(f32) + G[item][me_c].astype(f32)
        FP[item][...] = (acc + ZI[item][0, my_z].astype(f32) + ZI[item][1, my_z].astype(f32)).astype(bf16)

    def columns(item):
        n = FP[item].shape[2]
        return UA[item].at[:, pl.ds(pl.multiple_of(me_f * n, 128), n)]

    def f_send(item, d):
        dest = flipped(me_f, d, n_f)
        return remote(FP[item].at[dest], columns(item), fs.at[1 + item, d], fr.at[1 + item, d], (dest, me_c))

    def f_start(item):
        for d in range(1, n_f):
            f_send(item, d).start()
        columns(item)[...] = FP[item][me_f]

    def f_wait(item):
        for d in range(1, n_f):
            f_send(item, d).wait_recv()

    def ready(item):
        return FP[item] if UA[item] is None else UA[item]

    def g_send(item, z, step):
        src = ready(item) if z is None else OUT[item].at[z * n_y + my_y]
        at = my_z if z is None else z
        dst = OUT[item].at[at * n_y + my_y]
        return remote(src, dst, gs.at[item, (step + 1) // 2, at], gr.at[item, at],
                      (me_f, (my_z + step) * n_y + my_y))

    def h_send(item, z):
        src = ready(item) if z is None else OUT[item].at[z * n_y + my_y]
        at = my_z if z is None else z
        return remote(src, OUT[item].at[at * n_y + my_y], hs.at[item, at], hr.at[item, at],
                      (me_f, my_z * n_y + other_y))

    def spread(item):
        @pl.when(my_z < n_z - 1)
        def _():
            g_send(item, None, 1).start()

        @pl.when(my_z > 0)
        def _():
            g_send(item, None, -1).start()

        h_send(item, None).start()
        pltpu.make_async_copy(ready(item), OUT[item].at[me_c], own.at[item]).start()

    def pass_on(item, far):
        for step in (1, -1):
            z = my_z - step * far

            @pl.when(jnp.logical_and(z >= 0, z < n_z))
            def _(step=step, z=z):
                g_send(item, z, step).wait_recv()
                h_send(item, z).start()

                @pl.when(jnp.logical_and(my_z + step >= 0, my_z + step < n_z))
                def _():
                    g_send(item, z, step).start()

    def spread_wait(item):
        for step in (1, -1):

            @pl.when(jnp.logical_and(my_z + step >= 0, my_z + step < n_z))
            def _(step=step):
                g_send(item, None, step).wait_send()

            for far in range(1, n_z):
                z = my_z - step * far

                @pl.when(jnp.logical_and(jnp.logical_and(z >= 0, z < n_z),
                                         jnp.logical_and(my_z + step >= 0, my_z + step < n_z)))
                def _(step=step, z=z):
                    g_send(item, z, step).wait_send()

        for z in range(n_z):
            src = OUT[item].at[z * n_y + other_y]
            cp = remote(src, src, hs.at[item, z], hr.at[item, z], (me_f, my_z * n_y + other_y))
            cp.wait_send()
            cp.wait_recv()
        pltpu.make_async_copy(ready(item), OUT[item].at[me_c], own.at[item]).wait()

    lax.fori_loop(0, width // 256, down_grad, 0)
    for k in range(n_z):
        y_start(0, k)
    lax.fori_loop(0, width // 256, up_grad, 0)
    for k in range(n_z):
        y_start(1, k)

    at_end = jnp.logical_or(my_z == 0, my_z == last)
    between = jnp.logical_and(my_z > 0, my_z < last)

    @pl.when(at_end)
    def _():
        for k in range(last):
            y_sum(0, k)

    heads_arrival(0)
    heads_arrival(2)
    heads_arrival(1)
    attention_setup(AQ, AG, AS, KT, VT, GT, CB)

    def queries_of(i, h):
        def run():
            attention_block(h, i, AQ, AS, KT, VT, GT, ACT, SB, DK, TB, CB)
            GUP[h, :, i * 128 : (i + 1) * 128] = TB[...].T.astype(bf16)

        return run

    def one_head(h, carry):
        DK[...] = jnp.zeros_like(DK)

        def queries_step(t, inner):
            lax.switch((me_c + 1 + t) % n_c, [queries_of(i, h) for i in range(n_c)])
            give(0, h, t)
            for n, at in enumerate(SUM_AT):

                @pl.when(jnp.logical_and(h * n_c + t == at, between))
                def _(n=n):
                    y_sum(0, n)

            return inner

        lax.fori_loop(0, n_c, queries_step, 0)
        for i in range(n_c):
            GUP[2 + h, :, i * 128 : (i + 1) * 128] = DK[i * rows : (i + 1) * rows, :].astype(bf16)
        for t in range(n_c):
            give(1, h, t)
        return carry

    lax.fori_loop(0, 2, one_head, 0)
    piece_total(0)
    spread(0)

    @pl.when(at_end)
    def _():
        for k in range(last):
            y_sum(1, k)

    ROWS[...] = jnp.zeros_like(ROWS)
    for j in range(n_f):
        ROWS[0:1, j * cut : (j + 1) * cut] = PK[j, ROT : ROT + 1, :]
    ROWS[1:2, pl.ds(pl.multiple_of(me_f * cut, 128), cut)] = PK[me_f, ROT + 5 : ROT + 6, :]
    back_arrival(0, 0)
    back_arrival(0, 1)
    lane_low = lax.broadcasted_iota(jnp.int32, (rows, 128), 1) < HD

    def f_rows(kind, d, buf, land):
        dest = flipped(me_f, d, n_f)
        return remote(buf.at[dest], land.at[d - 1], fs.at[kind, d], fr.at[kind, d], (dest, me_c))

    def out_chunk(d, carry):
        s = flipped(me_f, d, n_f)
        for g in range(group):
            CX[s, :, g * 128 : (g + 1) * 128] = jnp.where(
                lane_low, CT[s, g, 0].astype(f32), CT[s, g, 1].astype(f32)).astype(bf16)
        PT[s] = (nn(CX[s], WN[...]) + PT[s].astype(f32) + ROWS[1:2, :]).astype(bf16)

        @pl.when(d != 0)
        def _():
            f_rows(0, d, PT, OR).start()

        return carry

    lax.fori_loop(0, n_f, out_chunk, 0)
    GN[...] = tn(CX[...].reshape(total, cut), DY[...].reshape(total, width)).astype(bf16).reshape(n_c, cut // n_c, width)
    for k in range(n_z):
        y_start(2, k)
    pass_on(0, 1)

    @pl.when(between)
    def _():
        y_sum(1, 0)

    back_arrival(1, 0)
    back_arrival(1, 1)
    ES[...] = jnp.zeros_like(ES)

    def mixed_chunk(d, carry):
        s = flipped(me_f, d, n_f)
        table = tn(rotary_terms(PK[s]), pat_ref[...])
        for g in range(group):
            c0, c1 = CT[s, g, 0].astype(f32), CT[s, g, 1].astype(f32)
            d0, d1 = DQ[s, g, 0].astype(f32), DQ[s, g, 1].astype(f32)
            t = [pltpu.roll(v, HD, 1) for v in (jnp.where(lane_low, d0, c0), jnp.where(lane_low, c1, d0), d1)]
            for i in range(3):
                lo = g * 384 + i * 128
                m = turn(t[i], table, i, -1.0).astype(bf16)
                N2[s, :, lo : lo + 128] = m
                ES[4:5, lo : lo + 128] += jnp.sum(m.astype(f32), axis=0, keepdims=True)
        e = nt(N2[s, :, 0:qc], WQ[...].reshape(width, qc))
        ES[0:1, :] += jnp.sum(e * XH[s].astype(f32), axis=0, keepdims=True)
        ES[1:2, :] += jnp.sum(e, axis=0, keepdims=True)
        H2[s] = (e * ROWS[0:1, :] + H2[s].astype(f32)).astype(bf16)

        @pl.when(d != 0)
        def _():
            f_rows(1, d, H2, HR).start()

        return carry

    lax.fori_loop(0, n_f, mixed_chunk, 0)
    tile = width // n_f

    def qkv_grad(r, carry):
        at = pl.ds(pl.multiple_of(r * tile, tile), tile)
        res = tn(N1[:, :, at].reshape(total, tile), N2[:, :, 0:qc].reshape(total, qc)).astype(bf16)
        GQ[:, r] = res.reshape(n_c, tile // n_c, qc)
        return carry

    lax.fori_loop(0, n_f, qkv_grad, 0)
    for k in range(n_z):
        y_start(3, k)

    for j in range(n_f):
        S1[j, 0:2, :] = ES[0:2, j * tile : (j + 1) * tile]
        S1[j, 2:4, :] = SMALL[2:4, j * tile : (j + 1) * tile]
        S1[j, 4:8, :] = jnp.zeros((4, tile), f32)
    for d in range(1, n_f):
        f_rows(3, d, S1, R1).start()

    @pl.when(between)
    def _():
        y_sum(1, 1)
        y_sum(1, 2)

    for k in range(last):
        y_sum(2, k)
    pass_on(0, 2)
    piece_total(1)
    f_start(1)
    pass_on(0, 3)
    for k in range(last):
        y_sum(3, k)
    piece_total(2)
    spread(2)
    f_wait(1)
    spread(1)

    for d in range(1, n_f):
        f_rows(3, d, S1, R1).wait_recv()
    S2[...] = jnp.zeros_like(S2)
    S2[0:1, 0:qc] = ES[4:5, 0:qc]
    S2[1:2, :] = SMALL[0:1, :]
    S2[2:3, 0:tile] = SMALL[1:2, pl.ds(pl.multiple_of(me_f * tile, tile), tile)]
    vec = S1[me_f, 0:4, :]
    for d in range(1, n_f):
        vec = vec + R1[d - 1, 0:4, :]
    S2[3:7, 0:tile] = vec

    def s2_send(k):
        dest = (me_c + k) % n_c
        return remote(S2, R2.at[k], as_.at[4, k], ar.at[4, k], (me_f, dest))

    for k in range(1, n_c):
        s2_send(k).start()

    piece_total(3)
    f_start(3)
    pass_on(1, 1)
    pass_on(2, 1)
    f_wait(3)
    spread(3)
    pass_on(1, 2)
    pass_on(2, 2)
    for d in range(1, n_f):
        f_rows(0, d, PT, OR).wait_recv()
    v = X[me_f].astype(f32)
    acc = v + PT[me_f].astype(f32)
    for d in range(1, n_f):
        acc = acc + OR[d - 1].astype(f32)
    out_ref[...] = acc.astype(bf16)

    pass_on(3, 1)
    pass_on(1, 3)
    pass_on(2, 3)
    for d in range(1, n_f):
        f_rows(1, d, H2, HR).wait_recv()
    h = H2[me_f].astype(f32)
    for d in range(1, n_f):
        h = h + HR[d - 1].astype(f32)
    center = v - jnp.mean(v, axis=-1, keepdims=True)
    rstd = lax.rsqrt(jnp.mean(center * center, axis=-1, keepdims=True) + norm_eps)
    xhat = center * rstd
    grad = rstd * (h - jnp.mean(h, axis=-1, keepdims=True) - xhat * jnp.mean(h * xhat, axis=-1, keepdims=True))
    gx_ref[...] = (DY[me_f].astype(f32) + grad).astype(bf16)
    pass_on(3, 2)
    pass_on(3, 3)
    tot = S2[...]
    for k in range(1, n_c):
        s2_send(k).wait_recv()
        tot = tot + R2[k]
    sum_ref[...] = tot

    for kind in range(5):
        for d in range(1, n_f):
            if kind < 2 and d % 2 == 1 and d > 1:
                forward(kind, d - 1).wait_send()
            else:
                copy_of(kind, d).wait_send()
            if kind in (2, 3) and d > 1:
                for way in range(3):
                    share(kind, d, way).wait_send()
    for kind, src in ((0, SQ.at[0, 0]), (1, SG.at[0, 0]), (2, PK.at[0, pl.ds(ROT, 8)])):
        for k in range(1, n_c):
            to_heads(kind, k, src, src).wait_send()
    for k in range(1, n_c):
        for kind in range(4):
            back(kind // 2, kind % 2, k, (me_c + k) % n_c).wait_send()
        s2_send(k).wait_send()
    for d in range(1, n_f):
        f_rows(0, d, PT, OR).wait_send()
        f_rows(1, d, H2, HR).wait_send()
        f_rows(3, d, S1, R1).wait_send()
        f_send(1, d).wait_send()
        f_send(3, d).wait_send()
    for item in range(4):
        for z in range(n_z):
            y_send(item, z).wait_send()

            @pl.when(my_z != z)
            def _(item=item, z=z):
                line_copy(item, toward(z), z, YR[item].at[z]).wait_send()

        spread_wait(item)


def call_m(n_f, n_c, n_y, x, dy, wq, wu, wd, wn, pk, vectors):
    rows, width = x.shape
    qc, uc = wq.shape[1] // n_f, wu.shape[1] // n_f
    n_z, group, cut, n = n_c // n_y, n_c // n_f, width // n_f, n_c * rows
    S, V, D = jax.ShapeDtypeStruct, pltpu.VMEM, pltpu.SemaphoreType.DMA
    pat = jnp.asarray(rotary_pattern(), bf16)
    shapes = [(uc // n_c, width), (n_f, cut // n_c, uc), (cut // n_c, width), (n_f, cut // n_c, qc)]
    wides = [shapes[0], (cut // n_c, n_f * uc), shapes[2], (cut // n_c, n_f * qc)]
    act = V((n_f, rows, width), bf16)
    scratch = [
        act, act, V((n_f, cut, qc), bf16), V((n_f, cut, uc), bf16), V((uc, width), bf16), V((cut, width), bf16),
        V((n_f,) + pk.shape, f32), act, act, act, V((n_f, group, 3, rows, 128), bf16), V((n_f, group, rows, 128), bf16),
        V((n_f, rows, uc), bf16), V((n_f, rows, uc), bf16), act, act, V((8, width), f32), V((8, max(uc, width)), f32),
    ]
    scratch += [
        V((n_f, group, 2, rows, 128), bf16), V((n_f, group, 2, rows, 128), bf16),
        V((n_f - 1, rows, width), bf16), V((n_f - 1, rows, width), bf16), V((8, width), f32),
    ]
    scratch += [V((n_c,) + s, bf16) for s in shapes]
    scratch += [V((n_z,) + s, bf16) for s in shapes]
    scratch += [V((2, n_z) + s, bf16) for s in shapes]
    scratch += [V(s, bf16) for s in shapes] + [V(wides[1], bf16), V(wides[3], bf16)]
    scratch += [V((n_f, 8, cut), f32), V((n_f - 1, 8, cut), f32), V((8, uc), f32), V((n_c, 8, uc), f32), V((8, width), f32)]
    scratch += [
        V((n_c, 3, rows, 128), bf16), V((n_c, rows, 128), bf16), V((n_c, 8, rows), f32), V((128, n), bf16), V((128, n), bf16),
        V((128, n), f32), V((n, rows), f32), V((n, 128), f32), V((128, rows), f32), V((rows, rows), f32),
        V((n_f, rows, cut), bf16),
    ]
    scratch += [
        D((7,)), D((5, n_f)), D((5, n_f)), D((2, 3, n_f)), D((2, 3, n_f)), D((3, n_c)), D((3, n_c)),
        D((5, n_f)), D((5, n_f)), D((5, n_c)), D((5, n_c)),
        D((4, n_z)), D((4, n_z)), D((4, n_z)), D((4, 2, n_z)), D((4, 2, n_z)), D((4, n_z)), D((4, n_z)), D((4, n_z)), D((4,)),
    ]
    return pl.pallas_call(
        functools.partial(kernel_m, n_f, n_c, n_y),
        out_shape=(S((rows, width), bf16), S((rows, width), bf16))
        + tuple(S((n_c,) + s, bf16) for s in wides) + (S((8, uc), f32),),
        in_specs=[hbm] * 7 + [vmem] * 2,
        out_specs=(vmem, vmem) + (hbm,) * 4 + (vmem,),
        scratch_shapes=scratch,
        compiler_params=pltpu.CompilerParams(collective_id=0, has_side_effects=True, vmem_limit_bytes=63 * 2**20),
        name="layer",
    )(x, dy, wq, wu, wd, wn, pk, pat, vectors)


def kernel_d(od, ou, on, oq, out, gx, vec, fd, fu, fn, fq, o1, o2, bq, b1, bu, n1g, n1b, n2g, n2b):
    for src, dst in ((od, fd), (ou, fu), (on, fn), (oq, fq)):
        dst[...] = src[0].astype(f32)
    o1[...] = out[...]
    o2[...] = gx[...]

    @pl.when(pl.program_id(0) == 0)
    def _():
        for ref, row in ((bq, 0), (bu, 1), (b1, 2), (n1g, 3), (n1b, 4), (n2g, 5), (n2b, 6)):
            ref[...] = vec[row, 0 : ref.shape[0]]


def call_d(od, ou, on, oq, out, gx, vec, qc):
    n_c, rows, cut = od.shape[0], out.shape[0], on.shape[0] * on.shape[1]
    S = jax.ShapeDtypeStruct

    def whole(n):
        return pl.BlockSpec((n,), lambda i: (0,))

    def block(a):
        return pl.BlockSpec((1,) + a.shape[1:], lambda i: (i, 0, 0))

    def flat(a):
        return pl.BlockSpec(a.shape[1:], lambda i: (i, 0))

    strip = pl.BlockSpec((rows // n_c, out.shape[1]), lambda i: (i, 0))
    grads = (od, ou, on, oq)
    sizes = (qc, cut, vec.shape[1], cut, cut, cut, cut)
    return pl.pallas_call(
        kernel_d,
        grid=(n_c,),
        out_shape=tuple(S((n_c * a.shape[1], a.shape[2]), f32) for a in grads)
        + (S(out.shape, bf16), S(out.shape, bf16)) + tuple(S((n,), f32) for n in sizes),
        in_specs=[block(a) for a in grads] + [strip, strip, pl.BlockSpec(vec.shape, lambda i: (0, 0))],
        out_specs=tuple(flat(a) for a in grads) + (strip, strip) + tuple(whole(n) for n in sizes),
        compiler_params=pltpu.CompilerParams(vmem_limit_bytes=62 * 2**20),
        name="widen",
    )(od, ou, on, oq, out, gx, vec)


def low(v):
    return v.astype(bf16)


def rotate_back(grad_part, cosine_table, sine_table):
    half_rot = ROT // 2
    g = grad_part[..., :ROT]
    b = g * sine_table[:, None, :]
    turned = jnp.concatenate([b[..., half_rot:], -b[..., :half_rot]], axis=-1)
    return jnp.concatenate([g * cosine_table[:, None, :] + turned, grad_part[..., ROT:]], axis=-1)


def body(
    tokens, segments, positions, cotangent, qkv_weight, qkv_bias, dense_weight, dense_bias,
    up_weight, up_bias, down_weight, down_bias, norm1_gain, norm1_bias, norm2_gain, norm2_bias,
):
    n_f, n_c = lax.axis_size("fsdp"), lax.axis_size("ctx")
    n_y = 2
    pk, vectors = call_p(positions, segments, norm1_gain, norm1_bias, norm2_gain, norm2_bias,
                         dense_bias, down_bias, qkv_bias, up_bias)
    out, gx, od, ou, on, oq, vec = call_m(
        n_f, n_c, n_y, tokens, cotangent, qkv_weight, up_weight, down_weight, dense_weight, pk, vectors)
    gd, gu, gn, gq, out, gx, bq, b1, bu, n1g, n1b, n2g, n2b = call_d(
        od, ou, on, oq, out, gx, vec, qkv_bias.shape[0])
    return out, gx, gq, bq, gn, b1, gu, bu, gd, b1, n1g, n1b, n2g, n2b


def rotary_tables(places):
    half_rot = ROT // 2
    inverse = 10000.0 ** (-2.0 * jnp.arange(half_rot, dtype=jnp.float32) / ROT)
    angles = places.astype(jnp.float32)[:, None] * inverse[None, :]
    angles = jnp.concatenate([angles, angles], axis=1)
    return (jnp.cos(angles), jnp.sin(angles))


def rotate(head_part, cosine_table, sine_table):
    half_rot = ROT // 2
    rotated_part = head_part[..., :ROT]
    turned = jnp.concatenate([-rotated_part[..., half_rot:], rotated_part[..., :half_rot]], axis=-1)
    rotated_part = rotated_part * cosine_table[:, None, :] + turned * sine_table[:, None, :]
    return jnp.concatenate([rotated_part, head_part[..., ROT:]], axis=-1)


def attention_pair(q, k, v, gc, doc):
    length = q.shape[0]
    place = jnp.arange(length, dtype=jnp.int32)
    visible = (place[None, :] <= place[:, None]) & (doc[None, :] == doc[:, None])
    scores = nt(q, k) * (1.0 / math.sqrt(HD))
    row_max = jnp.max(jnp.where(visible, scores, masked_fill), axis=-1, keepdims=True)
    terms = jnp.where(visible, jnp.exp(jnp.where(visible, scores - row_max, 0.0)), 0.0)
    total = jnp.sum(terms, axis=-1, keepdims=True)
    context = nn(low(terms), v) / total
    correction = jnp.sum(gc * context, axis=-1, keepdims=True) / total
    gw = low(gc / total)
    gv = tn(low(terms), gw)
    gs = low(terms * (nt(gw, v) - correction))
    gq = nn(gs, k) * (1.0 / math.sqrt(HD))
    gk = tn(gs, q) * (1.0 / math.sqrt(HD))
    return context, gq, gk, gv


def plain_body(
    tokens, segments, positions, cotangent, qkv_weight, qkv_bias, dense_weight, dense_bias,
    up_weight, up_bias, down_weight, down_bias, norm1_gain, norm1_bias, norm2_gain, norm2_bias,
):
    f32 = jnp.float32
    n_f, n_c = lax.axis_size("fsdp"), lax.axis_size("ctx")
    rows, width = tokens.shape
    heads = width // HD
    pairs = heads // n_c
    group = n_c // n_f
    me_c = lax.axis_index("ctx")
    me_f = lax.axis_index("fsdp")

    x = lax.all_gather(tokens, "fsdp", axis=0, tiled=True).astype(f32)
    dy = lax.all_gather(cotangent, "fsdp", axis=0, tiled=True)
    pos = lax.all_gather(positions, "fsdp", axis=0, tiled=True)
    docs = lax.all_gather(segments, ("fsdp", "ctx"), axis=0, tiled=True)
    w_qkv = lax.all_to_all(qkv_weight, "fsdp", 1, 0, tiled=True)
    w_up = lax.all_to_all(up_weight, "fsdp", 1, 0, tiled=True)
    norms = lax.all_gather(
        jnp.stack([norm1_gain, norm1_bias, norm2_gain, norm2_bias]), "fsdp", axis=1, tiled=True
    ).astype(f32)

    center = x - jnp.mean(x, axis=-1, keepdims=True)
    rstd = lax.rsqrt(jnp.mean(center * center, axis=-1, keepdims=True) + norm_eps)
    xhat = center * rstd
    normed_one = low(xhat * norms[0] + norms[1])
    normed_two = low(xhat * norms[2] + norms[3])

    mixed = nn(normed_one, w_qkv) + qkv_bias.astype(f32)
    total_rows = x.shape[0]
    cos, sin = rotary_tables(pos)
    mixed = mixed.reshape(total_rows, heads // n_f, 3, HD)
    mixed = jnp.stack(
        [rotate(mixed[:, :, 0], cos, sin), rotate(mixed[:, :, 1], cos, sin), mixed[:, :, 2]], axis=2
    )

    def to_heads(a, cols):
        a = a.reshape(n_f, rows, group, cols).transpose(0, 2, 1, 3).reshape(n_c, rows, cols)
        return lax.all_to_all(a, "ctx", 0, 0, tiled=True).reshape(n_c * rows, cols)

    def to_tokens(a, cols):
        a = lax.all_to_all(a.reshape(n_c, rows, cols), "ctx", 0, 0, tiled=True)
        return a.reshape(n_f, group, rows, cols).transpose(0, 2, 1, 3).reshape(total_rows, group * cols)

    qkv = to_heads(low(mixed).reshape(total_rows, -1), pairs * 3 * HD).reshape(-1, pairs, 3, HD)
    grad_context = nt(dy, dense_weight)
    gc = to_heads(low(grad_context), pairs * HD).reshape(-1, pairs, HD).astype(f32)
    seq_doc = lax.dynamic_slice_in_dim(docs, (me_c // group) * (n_c * rows), n_c * rows, 0)

    results = [
        attention_pair(qkv[:, i, 0], qkv[:, i, 1], qkv[:, i, 2], gc[:, i], seq_doc) for i in range(pairs)
    ]
    context = to_tokens(low(jnp.concatenate([r[0] for r in results], axis=1)), pairs * HD)
    grads = jnp.stack([jnp.stack(r[1:], axis=1) for r in results], axis=1)
    grads = to_tokens(low(grads).reshape(n_c * rows, -1), pairs * 3 * HD).astype(f32)
    grads = grads.reshape(total_rows, heads // n_f, 3, HD)
    grad_mixed = low(
        jnp.stack(
            [rotate_back(grads[:, :, 0], cos, sin), rotate_back(grads[:, :, 1], cos, sin), grads[:, :, 2]],
            axis=2,
        )
    ).reshape(total_rows, -1)

    up = nn(normed_two, w_up) + up_bias.astype(f32)
    active, pull = jax.vjp(lambda v: jax.nn.gelu(v, approximate=False), up)
    active = low(active)
    grad_up = low(pull(nt(dy, down_weight))[0])
    g_up_w = tn(normed_two, grad_up)
    g_up_b = jnp.sum(grad_up.astype(f32), axis=0)
    g_down_w = tn(active, dy)
    e_two = nt(grad_up, w_up)

    part = nn(context, dense_weight) + nn(active, down_weight)
    bias = lax.dynamic_update_slice_in_dim(
        jnp.zeros((width,), f32), dense_bias.astype(f32) + down_bias.astype(f32), me_f * (width // n_f), 0
    )
    part = low(part + bias)
    out = lax.psum_scatter(part, "fsdp", scatter_dimension=0, tiled=True).astype(f32)
    layer_out = low(tokens.astype(f32) + out)

    g_dense_w = tn(context, dy)
    g_qkv_w = tn(normed_one, grad_mixed)
    g_qkv_b = jnp.sum(grad_mixed.astype(f32), axis=0)
    e_one = nt(grad_mixed, w_qkv)
    h = low(e_one * norms[0] + e_two * norms[2])
    h = lax.psum_scatter(h, "fsdp", scatter_dimension=0, tiled=True).astype(f32)
    own_xhat = lax.dynamic_slice_in_dim(xhat, me_f * rows, rows, 0)
    own_rstd = lax.dynamic_slice_in_dim(rstd, me_f * rows, rows, 0)
    grad_in = own_rstd * (
        h - jnp.mean(h, axis=-1, keepdims=True) - own_xhat * jnp.mean(h * own_xhat, axis=-1, keepdims=True)
    )
    grad_tokens = low(cotangent.astype(f32) + grad_in)
    vecs = jnp.stack(
        [jnp.sum(e_one * xhat, 0), jnp.sum(e_one, 0), jnp.sum(e_two * xhat, 0), jnp.sum(e_two, 0)]
    )
    vecs = lax.psum(lax.psum_scatter(vecs, "fsdp", scatter_dimension=1, tiled=True), "ctx")
    dy_sum = jnp.sum(cotangent.astype(f32), axis=0)
    dy_sum = lax.psum(lax.psum_scatter(dy_sum, "fsdp", scatter_dimension=0, tiled=True), "ctx")
    g_qkv_b = lax.psum(g_qkv_b, "ctx")
    g_up_b = lax.psum(g_up_b, "ctx")

    def reduced(g, columns):
        if columns:
            g = lax.psum_scatter(low(g).reshape(n_f, -1, g.shape[1]), "ctx", scatter_dimension=1, tiled=True)
            g = lax.all_to_all(g, "fsdp", 0, 0, tiled=True)
            g = g.transpose(1, 0, 2).reshape(g.shape[1], -1)
            return lax.all_gather(g, "ctx", axis=0, tiled=True).astype(f32)
        g = lax.psum_scatter(low(g), "ctx", scatter_dimension=0, tiled=True)
        return lax.all_gather(g, "ctx", axis=0, tiled=True).astype(f32)

    return (
        layer_out, grad_tokens,
        reduced(g_qkv_w, True), g_qkv_b, reduced(g_dense_w, False), dy_sum,
        reduced(g_up_w, True), g_up_b, reduced(g_down_w, False), dy_sum,
        vecs[0], vecs[1], vecs[2], vecs[3],
    )


def solution(mesh):
    n_f, n_c = mesh.shape["fsdp"], mesh.shape["ctx"]
    fits = n_c % n_f == 0 and n_c == 8 and n_f == 4
    row, flat, w, b = P(("fsdp", "ctx"), None), P(("fsdp", "ctx")), P("fsdp", None), P("fsdp")
    return jax.shard_map(
        body if fits else plain_body,
        mesh=mesh,
        in_specs=(row, flat, flat, row, w, b, w, b, w, b, w, b, b, b, b, b),
        out_specs=(row, row, w, b, w, b, w, b, w, b, b, b, b, b),
        check_vma=False,
    )
```

```python
import functools
import math

import numpy as np
import jax, jax.numpy as jnp
from jax import lax
from jax.experimental import pallas as pl
from jax.experimental.pallas import tpu as pltpu
from jax.sharding import PartitionSpec as P

HD, ROT = 64, 16
f32, bf16 = jnp.float32, jnp.bfloat16
MESH = pl.DeviceIdType.MESH
vmem = pl.BlockSpec(memory_space=pltpu.VMEM)
hbm = pl.BlockSpec(memory_space=pl.ANY)
norm_eps = 1e-5
masked_fill = -1e30


def nn(a, b):
    return jnp.dot(a, b, preferred_element_type=f32)


def nt(a, b):
    return lax.dot_general(a, b, (((1,), (1,)), ((), ())), preferred_element_type=f32)


def tn(a, b):
    return lax.dot_general(a, b, (((0,), (0,)), ((), ())), preferred_element_type=f32)


def flipped(a, d, n):
    out, bit = 0, 1
    while bit < n:
        out = out + bit * ((a // bit + d // bit) % 2)
        bit *= 2
    return out


def kernel_p(pos, seg, g1, b1, g2, b2, dense, down, qkv, up, pk, vec):
    half, rows = ROT // 2, pos.shape[0]
    row = lax.broadcasted_iota(jnp.int32, (ROT, rows), 0)
    rate = jnp.zeros((ROT, rows), f32)
    for j in range(half):
        rate = jnp.where(row % half == j, float(np.float32(10000.0) ** np.float32(-2.0 * j / ROT)), rate)
    angle = rate * jnp.broadcast_to(pos[...].astype(f32).reshape(1, rows), (ROT, rows))
    pk[0:ROT, :] = jnp.where(row < half, jnp.cos(angle), jnp.sin(angle))
    pk[ROT:, :] = jnp.zeros((8, rows), f32)
    vec[...] = jnp.zeros_like(vec)

    def line(ref):
        return ref[...].astype(f32).reshape(1, ref.shape[0])

    for i, ref in enumerate((g1, b1, g2, b2, seg)):
        pk[ROT + i : ROT + i + 1, :] = line(ref)
    pk[ROT + 5 : ROT + 6, :] = line(dense) + line(down)
    vec[0:1, 0 : qkv.shape[0]] = line(qkv)
    vec[1:2, 0 : up.shape[0]] = line(up)


def call_p(pos, seg, g1, b1, g2, b2, dense, down, qkv, up):
    n = max(qkv.shape[0], up.shape[0])
    return pl.pallas_call(
        kernel_p,
        out_shape=(jax.ShapeDtypeStruct((24, pos.shape[0]), f32), jax.ShapeDtypeStruct((8, n), f32)),
        name="pack",
    )(pos, seg, g1, b1, g2, b2, dense, down, qkv, up)


def rotary_terms(pk):
    rest = pk[0:ROT, :]
    terms = []
    for _ in range(3):
        part = rest.astype(bf16)
        terms.append(part)
        rest = rest - part.astype(f32)
    return jnp.concatenate(terms + [jnp.ones_like(terms[0])], axis=0)


def rotary_pattern():
    e = np.zeros((64, 9 * 128), np.float32)
    for tile in range(3):
        for lane in range(128):
            col = tile * 128 + lane
            part, d = (col % 192) // HD, col % HD
            base = tile * 384 + lane
            if part == 2 or d >= ROT:
                e[48, base] = 1.0
                continue
            for term in range(3):
                e[term * 16 + d % 8, base] = 1.0
                if d < 8:
                    e[term * 16 + 8 + d, base + 128] = -1.0
                else:
                    e[term * 16 + d, base + 256] = 1.0
    return e


def turn(tile, table, t, sign):
    c = table[:, t * 384 : t * 384 + 128]
    up = table[:, t * 384 + 128 : t * 384 + 256]
    dn = table[:, t * 384 + 256 : t * 384 + 384]
    return tile * c + sign * (pltpu.roll(tile, 120, 1) * up + pltpu.roll(tile, 8, 1) * dn)


def key_docs(seg, j, blk):
    return jnp.broadcast_to(seg[j, 4:5, :], (blk, blk)).T


def attention_setup(qkv, gc, seg, kt, vt, gt, c_buf):
    blocks, _, blk, _ = qkv.shape
    for j in range(blocks):
        rows = pl.ds(j * blk, blk)
        kt[:, rows] = qkv[j, 1].astype(f32).T.astype(bf16)
        vt[:, rows] = qkv[j, 2].astype(f32).T.astype(bf16)
        gt[:, rows] = gc[j].astype(f32).T
    c_buf[...] = key_docs(seg, 0, blk)


def attention_block(h, i, qkv, seg, kt, vt, gt, p_buf, s_buf, acc, t_buf, c_buf):
    blocks, _, blk, lanes = qkv.shape
    half = lanes // 2
    lane = lax.broadcasted_iota(jnp.int32, (blk, lanes), 1) // half
    sub = lax.broadcasted_iota(jnp.int32, (lanes, blk), 0) // half
    causal = lax.broadcasted_iota(jnp.int32, (blk, blk), 0) <= lax.broadcasted_iota(jnp.int32, (blk, blk), 1)
    drow = seg[i, 4:5, :]
    own = pl.ds(pl.multiple_of(h * half, half), half)
    rest = pl.ds(pl.multiple_of((1 - h) * half, half), half)
    q_h = jnp.where(lane == h, qkv[i, 0].astype(f32) * 0.125, 0.0).astype(bf16)
    top = jnp.full((8, blk), masked_fill, f32)
    for j in range(i + 1):
        rows = pl.ds(j * blk, blk)
        s = nt(qkv[j, 1], q_h)
        seen = None
        if j == 0:
            seen = c_buf[...] == drow
        elif i == blocks - 1:
            seen = key_docs(seg, j, blk) == drow
        if j == i:
            seen = causal if seen is None else jnp.logical_and(causal, seen)
        if seen is not None:
            s = jnp.where(seen, s, masked_fill)
        s_buf[rows, :] = s
        top = jnp.maximum(top, jnp.max(s.reshape(blk // 8, 8, blk), axis=0))
    top = jnp.max(top, axis=0, keepdims=True)
    total = jnp.zeros((8, blk), f32)
    out = jnp.zeros((half, blk), f32)
    for j in range(i + 1):
        rows = pl.ds(j * blk, blk)
        p = jnp.exp(s_buf[rows, :] - top)
        s_buf[rows, :] = p
        total = total + jnp.sum(p.reshape(blk // 8, 8, blk), axis=0)
        rounded = p.astype(bf16)
        p_buf[j // 4, :, (j % 4) * blk : (j % 4 + 1) * blk] = rounded
        out = out + nn(vt[own, rows], rounded)
    inv = 1.0 / jnp.sum(total, axis=0, keepdims=True)
    out = out * inv
    t_buf[own, :] = out
    g_h = gt[own, i * blk : (i + 1) * blk]
    corr = jnp.sum(g_h * out, axis=0, keepdims=True) * inv
    gw = g_h * inv
    gw = jnp.concatenate([gw, gw], axis=0)
    gw_t = jnp.where(sub == h, gw, 0.0).astype(bf16)
    right = jnp.concatenate([q_h, jnp.where(sub == h, 0.0, gw).T.astype(bf16)], axis=0)
    dq = jnp.zeros((half, blk), f32)
    for j in range(i + 1):
        rows = pl.ds(j * blk, blk)
        ds = (s_buf[rows, :] * (nn(qkv[j, 2], gw_t) - corr)).astype(bf16)
        acc[rows, :] += nn(jnp.concatenate([ds, p_buf[j // 4, :, (j % 4) * blk : (j % 4 + 1) * blk]], axis=1), right)
        dq = dq + nn(kt[own, rows], ds)
    t_buf[rest, :] = dq * 0.125


SUMS_IN = ((1, 0, 1, (0, 1, 2)), (4, 1, 0, (0,)), (6, 1, 1, (0,)), (9, 1, 0, (1, 2)), (12, 1, 1, (1, 2)))


def kernel_m(
    n_f, n_c, n_y,
    x_hbm, dy_hbm, wq_hbm, wu_hbm, wd_hbm, wn_hbm, pk_hbm, pat_ref, vec_ref,
    out_ref, gx_ref, od_hbm, ou_hbm, on_hbm, oq_hbm, sum_ref,
    X, DY, WQ, WU, WD, WN, PK, N1, N2, XH, SQ, SG, ACT, GUP, PT, H2, GAIN, SMALL,
    CT, DQ, OR, HR, ROWS, GD, GU, GN, GQ, YD, YU, YN, YQ, ZD, ZU, ZN, ZQ, FD, FU, FN, FQ, UU, UQ, S1, R1, S2, R2, ES,
    AQ, AG, AS, KT, VT, GT, SB, DK, TB, CB, CX,
    loca, fsa, fra, vs, vr, asa, ara, fs, fr, as_, ar, ys, yr, zs, zr, gs, gr, hs, hr, own,
):
    me_f, me_c = lax.axis_index("fsdp"), lax.axis_index("ctx")
    rows, width = x_hbm.shape
    n_z, last = n_c // n_y, n_c // n_y - 1
    group = n_c // n_f
    qc, uc = WQ.shape[2], WU.shape[2]
    total, cut = n_f * rows, width // n_f

    bar = pltpu.get_barrier_semaphore()
    for d in range(1, n_f):
        pl.semaphore_signal(bar, inc=1, device_id=(flipped(me_f, d, n_f), me_c), device_id_type=MESH)
    for d in range(1, n_c):
        pl.semaphore_signal(bar, inc=1, device_id=(me_f, (me_c + d) % n_c), device_id_type=MESH)

    def cols(ref, i, n):
        return ref.at[:, pl.ds(pl.multiple_of(i * n, 128), n)]

    local = [
        pltpu.make_async_copy(x_hbm, X.at[me_f], loca.at[0]),
        pltpu.make_async_copy(pk_hbm, PK.at[me_f], loca.at[1]),
        pltpu.make_async_copy(cols(wq_hbm, me_f, qc), WQ.at[me_f], loca.at[2]),
        pltpu.make_async_copy(dy_hbm, DY.at[me_f], loca.at[3]),
        pltpu.make_async_copy(wn_hbm, WN, loca.at[4]),
        pltpu.make_async_copy(cols(wu_hbm, me_f, uc), WU.at[me_f], loca.at[5]),
        pltpu.make_async_copy(wd_hbm, WD, loca.at[6]),
    ]
    for cp in local:
        cp.start()
    pl.semaphore_wait(bar, n_f + n_c - 2)

    my_z, my_y = me_c // n_y, me_c % n_y
    other_y = 1 - my_y
    over_y = me_c + 1 - 2 * my_y
    over_z = me_c + n_y * (1 - 2 * (my_z % 2))
    quarter = WQ.shape[1] // 4

    def to_f(kind, d, src, dst, dest=None):
        return pltpu.make_async_remote_copy(
            src_ref=src, dst_ref=dst, send_sem=fsa.at[kind, d], recv_sem=fra.at[kind, d],
            device_id=(flipped(me_f, d, n_f) if dest is None else dest, me_c), device_id_type=MESH,
        )

    def part(ref, c):
        at = 2 * ((c // n_y) % 2) + c % n_y
        return ref.at[pl.ds(pl.multiple_of(at * quarter, 16), quarter)]

    def copy_of(kind, d):
        dest = flipped(me_f, d, n_f)
        if kind in (0, 1, 4):
            src, buf = ((x_hbm, X), (dy_hbm, DY), None, None, (pk_hbm, PK))[kind]
            return to_f(kind, d, src, buf.at[me_f])
        src, buf, n = ((wq_hbm, WQ, qc), (wu_hbm, WU, uc))[kind - 2]
        if d == 1:
            return to_f(kind, d, cols(src, dest, n), buf.at[me_f])
        return to_f(kind, d, cols(part(src, me_c), dest, n), part(buf.at[me_f], me_c))

    def arrival(kind, d):
        buf = (X, DY, WQ, WU, PK)[kind].at[flipped(me_f, d, n_f)]
        if kind in (2, 3) and d > 1:
            buf = part(buf, me_c)
        to_f(kind, d, buf, buf).wait_recv()

    def share(kind, d, way, mine=True):
        to, far = (over_y, over_z, over_z)[way], over_z + 1 - 2 * my_y
        which = (me_c, me_c, over_y)[way] if mine else (over_y, over_z, far)[way]
        buf = part((WQ, WU)[kind - 2].at[flipped(me_f, d, n_f)], which)
        return pltpu.make_async_remote_copy(
            src_ref=buf, dst_ref=buf, send_sem=vs.at[kind - 2, way, d], recv_sem=vr.at[kind - 2, way, d],
            device_id=(me_f, to), device_id_type=MESH,
        )

    def first_shares(kind):
        for d in range(2, n_f):
            arrival(kind, d)
            share(kind, d, 0).start()
            share(kind, d, 1).start()

    def next_shares(kind):
        for d in range(2, n_f):
            share(kind, d, 0, False).wait_recv()
            share(kind, d, 2).start()

    def weights(kind):
        arrival(kind, 1)
        for d in range(2, n_f):
            share(kind, d, 1, False).wait_recv()
            share(kind, d, 2, False).wait_recv()

    def forward(kind, d):
        buf = (X, DY)[kind].at[flipped(me_f, d, n_f)]
        return to_f(kind, d + 1, buf, buf, flipped(me_f, 1, n_f))

    direct = [1] + list(range(2, n_f, 2))
    for kind, to in ((4, range(1, n_f)), (2, (2, 3, 1)), (3, (2, 3, 1)), (0, direct), (1, direct)):
        for d in to:
            copy_of(kind, d).start()

    local[0].wait()
    local[1].wait()
    for d in range(1, n_f):
        arrival(4, d)
    for j in range(n_f):
        GAIN[0:4, j * (width // n_f) : (j + 1) * (width // n_f)] = PK[j, ROT : ROT + 4, :]
    g1, b1, g2, b2 = GAIN[0:1, :], GAIN[1:2, :], GAIN[2:3, :], GAIN[3:4, :]

    def norm_chunk(src):
        v = X[src].astype(f32)
        center = v - jnp.mean(v, axis=-1, keepdims=True)
        xhat = center * lax.rsqrt(jnp.mean(center * center, axis=-1, keepdims=True) + norm_eps)
        N1[src] = (xhat * g1 + b1).astype(bf16)
        N2[src] = (xhat * g2 + b2).astype(bf16)
        XH[src] = xhat.astype(bf16)

    lane_low = lax.broadcasted_iota(jnp.int32, (rows, 128), 1) < HD

    def to_heads(kind, k, src, dst):
        return pltpu.make_async_remote_copy(
            src_ref=src, dst_ref=dst, send_sem=asa.at[kind, k], recv_sem=ara.at[kind, k],
            device_id=(me_f, (me_c + k) % n_c), device_id_type=MESH,
        )

    def heads_arrival(kind):
        src, buf = ((SQ.at[0, 0], AQ), (SG.at[0, 0], AG), (PK.at[0, pl.ds(ROT, 8)], AS))[kind]
        pltpu.make_async_copy(src, buf.at[me_c], asa.at[kind, 0]).wait()
        for k in range(1, n_c):
            to_heads(kind, k, src, buf.at[(me_c - k + n_c) % n_c]).wait_recv()

    def to_c(kind, s, g, src, dst):
        dest = s * group + g
        k = (dest - me_c + n_c) % n_c

        @pl.when(k != 0)
        def _():
            to_heads(kind, k, src, dst).start()

        @pl.when(k == 0)
        def _():
            pltpu.make_async_copy(src, dst, asa.at[kind, 0]).start()

    def qkv_chunk(d, carry):
        s = flipped(me_f, d, n_f)
        table = tn(rotary_terms(PK[s]), pat_ref[...])
        mixed = nn(N1[s], WQ[...].reshape(width, qc)) + vec_ref[0:1, 0:qc]
        for g in range(group):
            t = [turn(mixed[:, g * 384 + i * 128 : g * 384 + (i + 1) * 128], table, i, 1.0) for i in range(3)]
            SQ[s, g, 0] = jnp.where(lane_low, t[0], t[1]).astype(bf16)
            SQ[s, g, 1] = jnp.where(lane_low, pltpu.roll(t[0], 64, 1), pltpu.roll(t[2], 64, 1)).astype(bf16)
            SQ[s, g, 2] = jnp.where(lane_low, t[1], t[2]).astype(bf16)
            to_c(0, s, g, SQ.at[s, g], AQ.at[me_c])
            to_c(2, s, g, PK.at[s, pl.ds(ROT, 8)], AS.at[me_c])
        return carry

    norm_chunk(me_f)
    first_shares(2)
    arrival(0, 1)
    norm_chunk(flipped(me_f, 1, n_f))
    first_shares(3)
    next_shares(2)
    next_shares(3)
    local[2].wait()
    weights(2)
    lax.fori_loop(0, 2, qkv_chunk, 0)
    for d in range(2, n_f):
        arrival(0, d)
        if d % 2 == 0:
            forward(0, d).start()
        norm_chunk(flipped(me_f, d, n_f))
        lax.fori_loop(d, d + 1, qkv_chunk, 0)
    local[5].wait()
    local[6].wait()
    weights(3)
    SMALL[...] = jnp.zeros_like(SMALL)

    def mlp_forward(s, carry):
        up = nn(N2[s], WU[...].reshape(width, uc)) + vec_ref[1:2, 0:uc]
        cdf = 0.5 * (1.0 + lax.erf(up * (2.0 ** -0.5)))
        ACT[s] = (up * cdf).astype(bf16)
        GUP[s] = (cdf + up * jnp.exp(-0.5 * up * up) * ((2.0 * np.pi) ** -0.5)).astype(bf16)
        PT[s] = nn(ACT[s], WD[...]).astype(bf16)
        return carry

    def mlp_backward(s, carry):
        gu = (nt(DY[s], WD[...]) * GUP[s].astype(f32)).astype(bf16)
        GUP[s] = gu
        SMALL[0:1, 0:uc] += jnp.sum(gu.astype(f32), axis=0, keepdims=True)
        SMALL[1:2, 0:width] += jnp.sum(DY[s].astype(f32), axis=0, keepdims=True)
        e = nt(GUP[s], WU[...].reshape(width, uc))
        SMALL[2:3, 0:width] += jnp.sum(e * XH[s].astype(f32), axis=0, keepdims=True)
        SMALL[3:4, 0:width] += jnp.sum(e, axis=0, keepdims=True)
        H2[s] = (e * g2).astype(bf16)
        return carry

    lax.fori_loop(0, n_f // 2, mlp_forward, 0)
    for d in range(2, n_f, 2):
        arrival(1, d)
        forward(1, d).start()
    lax.fori_loop(n_f // 2, n_f, mlp_forward, 0)
    local[3].wait()
    local[4].wait()
    for d in range(1, n_f, 2):
        arrival(1, d)

    def gc_chunk(d, carry):
        s = flipped(me_f, d, n_f)
        gc = nt(DY[s], WN[...])
        for g in range(group):
            SG[s, g] = gc[:, g * 128 : (g + 1) * 128].astype(bf16)
            to_c(1, s, g, SG.at[s, g], AG.at[me_c])
        return carry

    lax.fori_loop(0, n_f, gc_chunk, 0)


    def down_grad(r, carry):
        at = pl.ds(pl.multiple_of(r * 256, 256), 256)
        per = 256 // (uc // n_c)
        res = tn(ACT[:, :, at].reshape(total, 256), DY[...].reshape(total, width)).astype(bf16)
        res = res.reshape(per, 2, uc // n_c // 2, width)
        for i in range(2):
            GD[i, pl.ds(r * per, per)] = res[:, i]
        return carry

    def up_grad(r, carry):
        at = pl.ds(pl.multiple_of(r * 256, 256), 256)
        res = tn(N2[:, :, at].reshape(total, 256), GUP[...].reshape(total, uc)).astype(bf16)
        res = res.reshape(n_c, 2, 256 // n_c // 2, uc)
        for i in range(2):
            GU[i, :, r] = res[:, i]
        return carry

    def remote(src, dst, ssem, rsem, dev):
        return pltpu.make_async_remote_copy(
            src_ref=src, dst_ref=dst, send_sem=ssem, recv_sem=rsem, device_id=dev, device_id_type=MESH)

    def result(pair, h, i):
        return GUP.at[2 * pair + h, :, pl.ds(pl.multiple_of(i * 128, 128), 128)]

    def back(pair, h, k, i):
        return remote(result(pair, h, i), (CT, DQ)[pair].at[me_c // group, me_c % group, h], as_.at[2 * pair + h, k],
                      ar.at[2 * pair + h, k], (me_f, (me_c + k) % n_c))

    def back_own(pair, h, i):
        return pltpu.make_async_copy(
            result(pair, h, i), (CT, DQ)[pair].at[me_c // group, me_c % group, h], as_.at[2 * pair + h, 0])

    def back_arrival(pair, h):
        back_own(pair, h, me_c).wait()
        for k in range(1, n_c):
            src = (me_c - k + n_c) % n_c
            buf = (CT, DQ)[pair].at[src // group, src % group, h]
            remote(buf, buf, as_.at[2 * pair + h, k], ar.at[2 * pair + h, k], (me_f, src)).wait_recv()

    def give(pair, h, t):
        i = (me_c + 1 + t) % n_c

        @pl.when(t < n_c - 1)
        def _():
            back(pair, h, t + 1, i).start()

        @pl.when(t == n_c - 1)
        def _():
            back_own(pair, h, i).start()

    def items(d, u, n, q):
        return [d.at[0], d.at[1], u.at[0], u.at[1], n, q.at[0], q.at[1]]

    G, YR, ZI = items(GD, GU, GN, GQ), items(YD, YU, YN, YQ), items(ZD, ZU, ZN, ZQ)
    FP = items(FD, FU, FN, FQ)
    UA = [None, None, UU.at[0], UU.at[1], None, UQ.at[0], UQ.at[1]]
    DOWN, UP, DENSE, QKV = (0, 1), (2, 3), (4,), (5, 6)

    def out_at(item, c):
        if item in DENSE:
            return on_hbm.at[c]
        return (od_hbm if item in DOWN else ou_hbm if item in UP else oq_hbm).at[c, item - (0, 0, 2, 2, 4, 5, 5)[item]]

    low_half = 1 - my_z // (n_z // 2)

    def order(k):
        if k == last:
            return my_z
        down = last - k - (my_z - (last - k) + n_z) // n_z
        up = k + (k - my_z + n_z) // n_z
        return low_half * down + (1 - low_half) * up

    def toward(z):
        return (z - my_z + n_z) // n_z

    @pl.when(my_z == 0)
    def _():
        for buf in (ZD, ZU, ZQ):
            buf[:, 1] = jnp.zeros(buf.shape[:1] + buf.shape[2:], bf16)
        ZN[1] = jnp.zeros(ZN.shape[1:], bf16)

    @pl.when(my_z == last)
    def _():
        for buf in (ZD, ZU, ZQ):
            buf[:, 0] = jnp.zeros(buf.shape[:1] + buf.shape[2:], bf16)
        ZN[0] = jnp.zeros(ZN.shape[1:], bf16)

    def line_wait(item, way, z):
        @pl.when(jnp.logical_or(jnp.logical_and(way == 1, my_z > 0), jnp.logical_and(way == 0, my_z < last)))
        def _():
            line_copy(item, way, z, ZI[item].at[way, z]).wait_recv()

    def line_copy(item, way, z, src):
        return remote(src, ZI[item].at[way, z], zs.at[item, z], zr.at[item, way, z],
                      (me_f, (my_z + 2 * way - 1) * n_y + my_y))

    def y_send(item, z):
        src = G[item]
        return remote(src.at[z * n_y + other_y], YR[item].at[z], ys.at[item, z], yr.at[item, z],
                      (me_f, my_z * n_y + other_y))

    def y_start(item, k):
        y_send(item, order(k)).start()

    def y_sum(item, k):
        z = order(k)
        way = toward(z)
        y_send(item, z).wait_recv()
        line_wait(item, way, z)
        acc = YR[item][z].astype(f32) + G[item][z * n_y + my_y].astype(f32) + ZI[item][way, z].astype(f32)
        YR[item][z] = acc.astype(bf16)
        line_copy(item, way, z, YR[item].at[z]).start()

    def piece_total(item):
        y_send(item, my_z).wait_recv()
        for way in (0, 1):
            line_wait(item, way, my_z)
        acc = YR[item][my_z].astype(f32) + G[item][me_c].astype(f32)
        FP[item][...] = (acc + ZI[item][0, my_z].astype(f32) + ZI[item][1, my_z].astype(f32)).astype(bf16)

    def columns(item):
        n = FP[item].shape[2]
        return UA[item].at[:, pl.ds(pl.multiple_of(me_f * n, 128), n)]

    def f_send(item, d):
        dest = flipped(me_f, d, n_f)
        return remote(FP[item].at[dest], columns(item), fs.at[1 + item, d], fr.at[1 + item, d], (dest, me_c))

    def f_start(item):
        for d in range(1, n_f):
            f_send(item, d).start()
        columns(item)[...] = FP[item][me_f]

    def f_wait(item):
        for d in range(1, n_f):
            f_send(item, d).wait_recv()

    def ready(item):
        return FP[item] if UA[item] is None else UA[item]

    def g_send(item, z, step):
        src = ready(item) if z is None else out_at(item, z * n_y + my_y)
        at = my_z if z is None else z
        dst = out_at(item, at * n_y + my_y)
        return remote(src, dst, gs.at[item, (step + 1) // 2, at], gr.at[item, at],
                      (me_f, (my_z + step) * n_y + my_y))

    def h_send(item, z):
        src = ready(item) if z is None else out_at(item, z * n_y + my_y)
        at = my_z if z is None else z
        return remote(src, out_at(item, at * n_y + my_y), hs.at[item, at], hr.at[item, at],
                      (me_f, my_z * n_y + other_y))

    def spread(item):
        @pl.when(my_z < n_z - 1)
        def _():
            g_send(item, None, 1).start()

        @pl.when(my_z > 0)
        def _():
            g_send(item, None, -1).start()

        h_send(item, None).start()
        pltpu.make_async_copy(ready(item), out_at(item, me_c), own.at[item]).start()

    def pass_on(item, far):
        for step in (1, -1):
            z = my_z - step * far

            @pl.when(jnp.logical_and(z >= 0, z < n_z))
            def _(step=step, z=z):
                g_send(item, z, step).wait_recv()
                h_send(item, z).start()

                @pl.when(jnp.logical_and(my_z + step >= 0, my_z + step < n_z))
                def _():
                    g_send(item, z, step).start()

    def spread_wait(item):
        for step in (1, -1):

            @pl.when(jnp.logical_and(my_z + step >= 0, my_z + step < n_z))
            def _(step=step):
                g_send(item, None, step).wait_send()

            for far in range(1, n_z):
                z = my_z - step * far

                @pl.when(jnp.logical_and(jnp.logical_and(z >= 0, z < n_z),
                                         jnp.logical_and(my_z + step >= 0, my_z + step < n_z)))
                def _(step=step, z=z):
                    g_send(item, z, step).wait_send()

        for z in range(n_z):
            src = out_at(item, z * n_y + other_y)
            cp = remote(src, src, hs.at[item, z], hr.at[item, z], (me_f, my_z * n_y + other_y))
            cp.wait_send()
            cp.wait_recv()
        pltpu.make_async_copy(ready(item), out_at(item, me_c), own.at[item]).wait()

    lax.fori_loop(0, width // 256, down_grad, 0)
    for item in DOWN:
        for k in range(n_z):
            y_start(item, k)
    lax.fori_loop(0, n_f, mlp_backward, 0)
    lax.fori_loop(0, width // 256, up_grad, 0)
    for item in UP:
        for k in range(n_z):
            y_start(item, k)

    def sums(item, steps=range(n_c // n_y - 1)):
        for k in steps:
            y_sum(item, k)

    far_first, nearer = range(1), range(1, n_c // n_y - 1)

    at_end = jnp.logical_or(my_z == 0, my_z == last)
    between = jnp.logical_and(my_z > 0, my_z < last)

    heads_arrival(0)
    heads_arrival(2)

    @pl.when(at_end)
    def _():
        sums(0)

    heads_arrival(1)
    attention_setup(AQ, AG, AS, KT, VT, GT, CB)

    def queries_of(i, h):
        def run():
            attention_block(h, i, AQ, AS, KT, VT, GT, ACT, SB, DK, TB, CB)
            GUP[h, :, i * 128 : (i + 1) * 128] = TB[...].T.astype(bf16)

        return run

    def one_head(h, carry):
        DK[...] = jnp.zeros_like(DK)

        def queries_step(t, inner):
            lax.switch((me_c + 1 + t) % n_c, [queries_of(i, h) for i in range(n_c)])
            give(0, h, t)
            for at, where, item, steps in SUMS_IN:

                @pl.when(jnp.logical_and(h * n_c + t == at, at_end if where == 0 else between))
                def _(item=item, steps=steps):
                    sums(item, steps)

            return inner

        lax.fori_loop(0, n_c, queries_step, 0)
        for i in range(n_c):
            GUP[2 + h, :, i * 128 : (i + 1) * 128] = DK[i * rows : (i + 1) * rows, :].astype(bf16)
        for t in range(n_c):
            give(1, h, t)
        return carry

    lax.fori_loop(0, 2, one_head, 0)
    for item in DOWN:
        piece_total(item)
        spread(item)

    @pl.when(at_end)
    def _():
        for item in UP:
            sums(item)

    ROWS[...] = jnp.zeros_like(ROWS)
    for j in range(n_f):
        ROWS[0:1, j * cut : (j + 1) * cut] = PK[j, ROT : ROT + 1, :]
    ROWS[1:2, pl.ds(pl.multiple_of(me_f * cut, 128), cut)] = PK[me_f, ROT + 5 : ROT + 6, :]
    back_arrival(0, 0)
    back_arrival(0, 1)
    lane_low = lax.broadcasted_iota(jnp.int32, (rows, 128), 1) < HD

    def f_rows(kind, d, buf, land):
        dest = flipped(me_f, d, n_f)
        return remote(buf.at[dest], land.at[d - 1], fs.at[kind, d], fr.at[kind, d], (dest, me_c))

    def out_chunk(d, carry):
        s = flipped(me_f, d, n_f)
        for g in range(group):
            CX[s, :, g * 128 : (g + 1) * 128] = jnp.where(
                lane_low, CT[s, g, 0].astype(f32), CT[s, g, 1].astype(f32)).astype(bf16)
        PT[s] = (nn(CX[s], WN[...]) + PT[s].astype(f32) + ROWS[1:2, :]).astype(bf16)

        @pl.when(d != 0)
        def _():
            f_rows(0, d, PT, OR).start()

        return carry

    lax.fori_loop(0, n_f, out_chunk, 0)
    GN[...] = tn(CX[...].reshape(total, cut), DY[...].reshape(total, width)).astype(bf16).reshape(n_c, cut // n_c, width)
    for k in range(n_z):
        y_start(4, k)

    @pl.when(between)
    def _():
        for item in UP:
            sums(item, far_first)

    pass_on(0, 1)
    pass_on(1, 1)

    back_arrival(1, 0)
    back_arrival(1, 1)
    ES[...] = jnp.zeros_like(ES)

    def mixed_chunk(d, carry):
        s = flipped(me_f, d, n_f)
        table = tn(rotary_terms(PK[s]), pat_ref[...])
        for g in range(group):
            c0, c1 = CT[s, g, 0].astype(f32), CT[s, g, 1].astype(f32)
            d0, d1 = DQ[s, g, 0].astype(f32), DQ[s, g, 1].astype(f32)
            t = [pltpu.roll(v, HD, 1) for v in (jnp.where(lane_low, d0, c0), jnp.where(lane_low, c1, d0), d1)]
            for i in range(3):
                lo = g * 384 + i * 128
                m = turn(t[i], table, i, -1.0).astype(bf16)
                N2[s, :, lo : lo + 128] = m
                ES[4:5, lo : lo + 128] += jnp.sum(m.astype(f32), axis=0, keepdims=True)
        e = nt(N2[s, :, 0:qc], WQ[...].reshape(width, qc))
        ES[0:1, :] += jnp.sum(e * XH[s].astype(f32), axis=0, keepdims=True)
        ES[1:2, :] += jnp.sum(e, axis=0, keepdims=True)
        H2[s] = (e * ROWS[0:1, :] + H2[s].astype(f32)).astype(bf16)
        return carry

    lax.fori_loop(0, n_f, mixed_chunk, 0)
    tile = width // n_f

    def qkv_grad(r, carry):
        at = pl.ds(pl.multiple_of(r * tile, tile), tile)
        res = tn(N1[:, :, at].reshape(total, tile), N2[:, :, 0:qc].reshape(total, qc)).astype(bf16)
        res = res.reshape(n_c, 2, tile // n_c // 2, qc)
        for i in range(2):
            GQ[i, :, r] = res[:, i]
        return carry

    lax.fori_loop(0, n_f, qkv_grad, 0)
    for item in QKV:
        for k in range(n_z):
            y_start(item, k)

    for j in range(n_f):
        S1[j, 0:2, :] = ES[0:2, j * tile : (j + 1) * tile]
        S1[j, 2:4, :] = SMALL[2:4, j * tile : (j + 1) * tile]
        S1[j, 4:8, :] = jnp.zeros((4, tile), f32)
    for d in range(1, n_f):
        f_rows(2, d, S1, R1).start()

    @pl.when(between)
    def _():
        for item in UP:
            sums(item, nearer)
        sums(4, far_first)

    @pl.when(at_end)
    def _():
        sums(4)

    pass_on(0, 2)
    pass_on(1, 2)
    for item in UP:
        piece_total(item)
        f_start(item)

    @pl.when(between)
    def _():
        sums(4, nearer)
        sums(5, far_first)

    @pl.when(at_end)
    def _():
        sums(5)

    pass_on(0, 3)
    pass_on(1, 3)
    for d in range(1, n_f):
        f_rows(1, d, H2, HR).start()
    for item in UP:
        f_wait(item)
        spread(item)
    piece_total(4)
    spread(4)

    @pl.when(between)
    def _():
        sums(6, far_first)
        sums(5, nearer)
        sums(6, nearer)

    @pl.when(at_end)
    def _():
        sums(6)

    for d in range(1, n_f):
        f_rows(2, d, S1, R1).wait_recv()
    S2[...] = jnp.zeros_like(S2)
    S2[0:1, 0:qc] = ES[4:5, 0:qc]
    S2[1:2, :] = SMALL[0:1, :]
    S2[2:3, 0:tile] = SMALL[1:2, pl.ds(pl.multiple_of(me_f * tile, tile), tile)]
    vec = S1[me_f, 0:4, :]
    for d in range(1, n_f):
        vec = vec + R1[d - 1, 0:4, :]
    S2[3:7, 0:tile] = vec

    def s2_send(k):
        dest = (me_c + k) % n_c
        return remote(S2, R2.at[k], as_.at[4, k], ar.at[4, k], (me_f, dest))

    for k in range(1, n_c):
        s2_send(k).start()

    pass_on(2, 1)
    piece_total(5)
    f_start(5)
    pass_on(3, 1)
    pass_on(4, 1)
    piece_total(6)
    f_start(6)
    pass_on(2, 2)
    f_wait(5)
    spread(5)
    pass_on(3, 2)
    pass_on(4, 2)
    for d in range(1, n_f):
        f_rows(0, d, PT, OR).wait_recv()
    v = X[me_f].astype(f32)
    acc = v + PT[me_f].astype(f32)
    for d in range(1, n_f):
        acc = acc + OR[d - 1].astype(f32)
    out_ref[...] = acc.astype(bf16)

    f_wait(6)
    spread(6)
    pass_on(5, 1)
    pass_on(2, 3)
    pass_on(3, 3)
    pass_on(4, 3)
    for d in range(1, n_f):
        f_rows(1, d, H2, HR).wait_recv()
    h = H2[me_f].astype(f32)
    for d in range(1, n_f):
        h = h + HR[d - 1].astype(f32)
    center = v - jnp.mean(v, axis=-1, keepdims=True)
    rstd = lax.rsqrt(jnp.mean(center * center, axis=-1, keepdims=True) + norm_eps)
    xhat = center * rstd
    grad = rstd * (h - jnp.mean(h, axis=-1, keepdims=True) - xhat * jnp.mean(h * xhat, axis=-1, keepdims=True))
    gx_ref[...] = (DY[me_f].astype(f32) + grad).astype(bf16)
    pass_on(6, 1)
    pass_on(5, 2)
    pass_on(6, 2)
    pass_on(5, 3)
    pass_on(6, 3)
    tot = S2[...]
    for k in range(1, n_c):
        s2_send(k).wait_recv()
        tot = tot + R2[k]
    sum_ref[...] = tot

    for kind in range(5):
        for d in range(1, n_f):
            if kind < 2 and d % 2 == 1 and d > 1:
                forward(kind, d - 1).wait_send()
            else:
                copy_of(kind, d).wait_send()
            if kind in (2, 3) and d > 1:
                for way in range(3):
                    share(kind, d, way).wait_send()
    for kind, src in ((0, SQ.at[0, 0]), (1, SG.at[0, 0]), (2, PK.at[0, pl.ds(ROT, 8)])):
        for k in range(1, n_c):
            to_heads(kind, k, src, src).wait_send()
    for k in range(1, n_c):
        for kind in range(4):
            back(kind // 2, kind % 2, k, (me_c + k) % n_c).wait_send()
        s2_send(k).wait_send()
    for d in range(1, n_f):
        f_rows(0, d, PT, OR).wait_send()
        f_rows(1, d, H2, HR).wait_send()
        f_rows(2, d, S1, R1).wait_send()
        for item in UP + QKV:
            f_send(item, d).wait_send()
    for item in range(len(G)):
        for z in range(n_z):
            y_send(item, z).wait_send()

            @pl.when(my_z != z)
            def _(item=item, z=z):
                line_copy(item, toward(z), z, YR[item].at[z]).wait_send()

        spread_wait(item)


def call_m(n_f, n_c, n_y, x, dy, wq, wu, wd, wn, pk, vectors):
    rows, width = x.shape
    qc, uc = wq.shape[1] // n_f, wu.shape[1] // n_f
    n_z, group, cut, n = n_c // n_y, n_c // n_f, width // n_f, n_c * rows
    S, V, D = jax.ShapeDtypeStruct, pltpu.VMEM, pltpu.SemaphoreType.DMA
    pat = jnp.asarray(rotary_pattern(), bf16)
    shapes = [(uc // n_c // 2, width), (n_f, cut // n_c // 2, uc), (cut // n_c, width), (n_f, cut // n_c // 2, qc)]
    wides = [shapes[0], (cut // n_c // 2, n_f * uc), shapes[2], (cut // n_c // 2, n_f * qc)]
    act = V((n_f, rows, width), bf16)
    scratch = [
        act, act, V((n_f, cut, qc), bf16), V((n_f, cut, uc), bf16), V((uc, width), bf16), V((cut, width), bf16),
        V((n_f,) + pk.shape, f32), act, act, act, V((n_f, group, 3, rows, 128), bf16), V((n_f, group, rows, 128), bf16),
        V((n_f, rows, uc), bf16), V((n_f, rows, uc), bf16), act, act, V((8, width), f32), V((8, max(uc, width)), f32),
    ]
    scratch += [
        V((n_f, group, 2, rows, 128), bf16), V((n_f, group, 2, rows, 128), bf16),
        V((n_f - 1, rows, width), bf16), V((n_f - 1, rows, width), bf16), V((8, width), f32),
    ]
    parts = [(2,), (2,), (), (2,)]
    scratch += [V(p + (n_c,) + s, bf16) for p, s in zip(parts, shapes)]
    scratch += [V(p + (n_z,) + s, bf16) for p, s in zip(parts, shapes)]
    scratch += [V(p + (2, n_z) + s, bf16) for p, s in zip(parts, shapes)]
    scratch += [V(p + s, bf16) for p, s in zip(parts, shapes)]
    scratch += [V((2,) + wides[1], bf16), V((2,) + wides[3], bf16)]
    scratch += [V((n_f, 8, cut), f32), V((n_f - 1, 8, cut), f32), V((8, uc), f32), V((n_c, 8, uc), f32), V((8, width), f32)]
    scratch += [
        V((n_c, 3, rows, 128), bf16), V((n_c, rows, 128), bf16), V((n_c, 8, rows), f32), V((128, n), bf16), V((128, n), bf16),
        V((128, n), f32), V((n, rows), f32), V((n, 128), f32), V((128, rows), f32), V((rows, rows), f32),
        V((n_f, rows, cut), bf16),
    ]
    scratch += [
        D((7,)), D((5, n_f)), D((5, n_f)), D((2, 3, n_f)), D((2, 3, n_f)), D((3, n_c)), D((3, n_c)),
        D((8, n_f)), D((8, n_f)), D((5, n_c)), D((5, n_c)),
        D((7, n_z)), D((7, n_z)), D((7, n_z)), D((7, 2, n_z)), D((7, 2, n_z)), D((7, n_z)), D((7, n_z)), D((7, n_z)), D((7,)),
    ]
    return pl.pallas_call(
        functools.partial(kernel_m, n_f, n_c, n_y),
        out_shape=(S((rows, width), bf16), S((rows, width), bf16))
        + tuple(S((n_c,) + p + s, bf16) for p, s in zip(parts, wides)) + (S((8, uc), f32),),
        in_specs=[hbm] * 7 + [vmem] * 2,
        out_specs=(vmem, vmem) + (hbm,) * 4 + (vmem,),
        scratch_shapes=scratch,
        compiler_params=pltpu.CompilerParams(collective_id=0, has_side_effects=True, vmem_limit_bytes=63 * 2**20),
        name="layer",
    )(x, dy, wq, wu, wd, wn, pk, pat, vectors)


def kernel_d(od, ou, on, oq, out, gx, vec, fd, fu, fn, fq, o1, o2, bq, b1, b2, bu, n1g, n1b, n2g, n2b):
    for src, dst in ((od, fd), (ou, fu), (on, fn), (oq, fq)):
        dst[...] = src[0].astype(f32)
    o1[...] = out[...]
    o2[...] = gx[...]

    @pl.when(pl.program_id(0) == 0)
    def _():
        for ref, row in ((bq, 0), (bu, 1), (b1, 2), (b2, 2), (n1g, 3), (n1b, 4), (n2g, 5), (n2b, 6)):
            ref[...] = vec[row, 0 : ref.shape[0]]


def call_d(od, ou, on, oq, out, gx, vec, qc):
    n_c, rows, cut = od.shape[0], out.shape[0], on.shape[0] * on.shape[1]
    S = jax.ShapeDtypeStruct

    def whole(n):
        return pl.BlockSpec((n,), lambda i: (0,))

    def block(a):
        return pl.BlockSpec((1,) + a.shape[1:], lambda i: (i, 0, 0))

    def flat(a):
        return pl.BlockSpec(a.shape[1:], lambda i: (i, 0))

    strip = pl.BlockSpec((rows // n_c, out.shape[1]), lambda i: (i, 0))
    grads = (od, ou, on, oq)
    sizes = (qc, cut, cut, vec.shape[1], cut, cut, cut, cut)
    return pl.pallas_call(
        kernel_d,
        grid=(n_c,),
        out_shape=tuple(S((n_c * a.shape[1], a.shape[2]), f32) for a in grads)
        + (S(out.shape, bf16), S(out.shape, bf16)) + tuple(S((n,), f32) for n in sizes),
        in_specs=[block(a) for a in grads] + [strip, strip, pl.BlockSpec(vec.shape, lambda i: (0, 0))],
        out_specs=tuple(flat(a) for a in grads) + (strip, strip) + tuple(whole(n) for n in sizes),
        compiler_params=pltpu.CompilerParams(vmem_limit_bytes=62 * 2**20),
        name="widen",
    )(od, ou, on, oq, out, gx, vec)


def low(v):
    return v.astype(bf16)


def rotate_back(grad_part, cosine_table, sine_table):
    half_rot = ROT // 2
    g = grad_part[..., :ROT]
    b = g * sine_table[:, None, :]
    turned = jnp.concatenate([b[..., half_rot:], -b[..., :half_rot]], axis=-1)
    return jnp.concatenate([g * cosine_table[:, None, :] + turned, grad_part[..., ROT:]], axis=-1)


def body(
    tokens, segments, positions, cotangent, qkv_weight, qkv_bias, dense_weight, dense_bias,
    up_weight, up_bias, down_weight, down_bias, norm1_gain, norm1_bias, norm2_gain, norm2_bias,
):
    n_f, n_c = lax.axis_size("fsdp"), lax.axis_size("ctx")
    n_y = 2
    pk, vectors = call_p(positions, segments, norm1_gain, norm1_bias, norm2_gain, norm2_bias,
                         dense_bias, down_bias, qkv_bias, up_bias)
    out, gx, od, ou, on, oq, vec = call_m(
        n_f, n_c, n_y, tokens, cotangent, qkv_weight, up_weight, down_weight, dense_weight, pk, vectors)
    od, ou, oq = (a.reshape(a.shape[0], -1, a.shape[3]) for a in (od, ou, oq))
    gd, gu, gn, gq, out, gx, bq, b1, b2, bu, n1g, n1b, n2g, n2b = call_d(
        od, ou, on, oq, out, gx, vec, qkv_bias.shape[0])
    return out, gx, gq, bq, gn, b1, gu, bu, gd, b2, n1g, n1b, n2g, n2b


def rotary_tables(places):
    half_rot = ROT // 2
    inverse = 10000.0 ** (-2.0 * jnp.arange(half_rot, dtype=jnp.float32) / ROT)
    angles = places.astype(jnp.float32)[:, None] * inverse[None, :]
    angles = jnp.concatenate([angles, angles], axis=1)
    return (jnp.cos(angles), jnp.sin(angles))


def rotate(head_part, cosine_table, sine_table):
    half_rot = ROT // 2
    rotated_part = head_part[..., :ROT]
    turned = jnp.concatenate([-rotated_part[..., half_rot:], rotated_part[..., :half_rot]], axis=-1)
    rotated_part = rotated_part * cosine_table[:, None, :] + turned * sine_table[:, None, :]
    return jnp.concatenate([rotated_part, head_part[..., ROT:]], axis=-1)


def attention_pair(q, k, v, gc, doc):
    length = q.shape[0]
    place = jnp.arange(length, dtype=jnp.int32)
    visible = (place[None, :] <= place[:, None]) & (doc[None, :] == doc[:, None])
    scores = nt(q, k) * (1.0 / math.sqrt(HD))
    row_max = jnp.max(jnp.where(visible, scores, masked_fill), axis=-1, keepdims=True)
    terms = jnp.where(visible, jnp.exp(jnp.where(visible, scores - row_max, 0.0)), 0.0)
    total = jnp.sum(terms, axis=-1, keepdims=True)
    context = nn(low(terms), v) / total
    correction = jnp.sum(gc * context, axis=-1, keepdims=True) / total
    gw = low(gc / total)
    gv = tn(low(terms), gw)
    gs = low(terms * (nt(gw, v) - correction))
    gq = nn(gs, k) * (1.0 / math.sqrt(HD))
    gk = tn(gs, q) * (1.0 / math.sqrt(HD))
    return context, gq, gk, gv


def plain_body(
    tokens, segments, positions, cotangent, qkv_weight, qkv_bias, dense_weight, dense_bias,
    up_weight, up_bias, down_weight, down_bias, norm1_gain, norm1_bias, norm2_gain, norm2_bias,
):
    f32 = jnp.float32
    n_f, n_c = lax.axis_size("fsdp"), lax.axis_size("ctx")
    rows, width = tokens.shape
    heads = width // HD
    pairs = heads // n_c
    group = n_c // n_f
    me_c = lax.axis_index("ctx")
    me_f = lax.axis_index("fsdp")

    x = lax.all_gather(tokens, "fsdp", axis=0, tiled=True).astype(f32)
    dy = lax.all_gather(cotangent, "fsdp", axis=0, tiled=True)
    pos = lax.all_gather(positions, "fsdp", axis=0, tiled=True)
    docs = lax.all_gather(segments, ("fsdp", "ctx"), axis=0, tiled=True)
    w_qkv = lax.all_to_all(qkv_weight, "fsdp", 1, 0, tiled=True)
    w_up = lax.all_to_all(up_weight, "fsdp", 1, 0, tiled=True)
    norms = lax.all_gather(
        jnp.stack([norm1_gain, norm1_bias, norm2_gain, norm2_bias]), "fsdp", axis=1, tiled=True
    ).astype(f32)

    center = x - jnp.mean(x, axis=-1, keepdims=True)
    rstd = lax.rsqrt(jnp.mean(center * center, axis=-1, keepdims=True) + norm_eps)
    xhat = center * rstd
    normed_one = low(xhat * norms[0] + norms[1])
    normed_two = low(xhat * norms[2] + norms[3])

    mixed = nn(normed_one, w_qkv) + qkv_bias.astype(f32)
    total_rows = x.shape[0]
    cos, sin = rotary_tables(pos)
    mixed = mixed.reshape(total_rows, heads // n_f, 3, HD)
    mixed = jnp.stack(
        [rotate(mixed[:, :, 0], cos, sin), rotate(mixed[:, :, 1], cos, sin), mixed[:, :, 2]], axis=2
    )

    def to_heads(a, cols):
        a = a.reshape(n_f, rows, group, cols).transpose(0, 2, 1, 3).reshape(n_c, rows, cols)
        return lax.all_to_all(a, "ctx", 0, 0, tiled=True).reshape(n_c * rows, cols)

    def to_tokens(a, cols):
        a = lax.all_to_all(a.reshape(n_c, rows, cols), "ctx", 0, 0, tiled=True)
        return a.reshape(n_f, group, rows, cols).transpose(0, 2, 1, 3).reshape(total_rows, group * cols)

    qkv = to_heads(low(mixed).reshape(total_rows, -1), pairs * 3 * HD).reshape(-1, pairs, 3, HD)
    grad_context = nt(dy, dense_weight)
    gc = to_heads(low(grad_context), pairs * HD).reshape(-1, pairs, HD).astype(f32)
    seq_doc = lax.dynamic_slice_in_dim(docs, (me_c // group) * (n_c * rows), n_c * rows, 0)

    results = [
        attention_pair(qkv[:, i, 0], qkv[:, i, 1], qkv[:, i, 2], gc[:, i], seq_doc) for i in range(pairs)
    ]
    context = to_tokens(low(jnp.concatenate([r[0] for r in results], axis=1)), pairs * HD)
    grads = jnp.stack([jnp.stack(r[1:], axis=1) for r in results], axis=1)
    grads = to_tokens(low(grads).reshape(n_c * rows, -1), pairs * 3 * HD).astype(f32)
    grads = grads.reshape(total_rows, heads // n_f, 3, HD)
    grad_mixed = low(
        jnp.stack(
            [rotate_back(grads[:, :, 0], cos, sin), rotate_back(grads[:, :, 1], cos, sin), grads[:, :, 2]],
            axis=2,
        )
    ).reshape(total_rows, -1)

    up = nn(normed_two, w_up) + up_bias.astype(f32)
    active, pull = jax.vjp(lambda v: jax.nn.gelu(v, approximate=False), up)
    active = low(active)
    grad_up = low(pull(nt(dy, down_weight))[0])
    g_up_w = tn(normed_two, grad_up)
    g_up_b = jnp.sum(grad_up.astype(f32), axis=0)
    g_down_w = tn(active, dy)
    e_two = nt(grad_up, w_up)

    part = nn(context, dense_weight) + nn(active, down_weight)
    bias = lax.dynamic_update_slice_in_dim(
        jnp.zeros((width,), f32), dense_bias.astype(f32) + down_bias.astype(f32), me_f * (width // n_f), 0
    )
    part = low(part + bias)
    out = lax.psum_scatter(part, "fsdp", scatter_dimension=0, tiled=True).astype(f32)
    layer_out = low(tokens.astype(f32) + out)

    g_dense_w = tn(context, dy)
    g_qkv_w = tn(normed_one, grad_mixed)
    g_qkv_b = jnp.sum(grad_mixed.astype(f32), axis=0)
    e_one = nt(grad_mixed, w_qkv)
    h = low(e_one * norms[0] + e_two * norms[2])
    h = lax.psum_scatter(h, "fsdp", scatter_dimension=0, tiled=True).astype(f32)
    own_xhat = lax.dynamic_slice_in_dim(xhat, me_f * rows, rows, 0)
    own_rstd = lax.dynamic_slice_in_dim(rstd, me_f * rows, rows, 0)
    grad_in = own_rstd * (
        h - jnp.mean(h, axis=-1, keepdims=True) - own_xhat * jnp.mean(h * own_xhat, axis=-1, keepdims=True)
    )
    grad_tokens = low(cotangent.astype(f32) + grad_in)
    vecs = jnp.stack(
        [jnp.sum(e_one * xhat, 0), jnp.sum(e_one, 0), jnp.sum(e_two * xhat, 0), jnp.sum(e_two, 0)]
    )
    vecs = lax.psum(lax.psum_scatter(vecs, "fsdp", scatter_dimension=1, tiled=True), "ctx")
    dy_sum = jnp.sum(cotangent.astype(f32), axis=0)
    dy_sum = lax.psum(lax.psum_scatter(dy_sum, "fsdp", scatter_dimension=0, tiled=True), "ctx")
    g_qkv_b = lax.psum(g_qkv_b, "ctx")
    g_up_b = lax.psum(g_up_b, "ctx")

    def reduced(g, columns):
        if columns:
            g = lax.psum_scatter(low(g).reshape(n_f, -1, g.shape[1]), "ctx", scatter_dimension=1, tiled=True)
            g = lax.all_to_all(g, "fsdp", 0, 0, tiled=True)
            g = g.transpose(1, 0, 2).reshape(g.shape[1], -1)
            return lax.all_gather(g, "ctx", axis=0, tiled=True).astype(f32)
        g = lax.psum_scatter(low(g), "ctx", scatter_dimension=0, tiled=True)
        return lax.all_gather(g, "ctx", axis=0, tiled=True).astype(f32)

    return (
        layer_out, grad_tokens,
        reduced(g_qkv_w, True), g_qkv_b, reduced(g_dense_w, False), dy_sum,
        reduced(g_up_w, True), g_up_b, reduced(g_down_w, False), dy_sum,
        vecs[0], vecs[1], vecs[2], vecs[3],
    )


def solution(mesh):
    n_f, n_c = mesh.shape["fsdp"], mesh.shape["ctx"]
    fits = n_c % n_f == 0 and n_c == 8 and n_f == 4
    row, flat, w, b = P(("fsdp", "ctx"), None), P(("fsdp", "ctx")), P("fsdp", None), P("fsdp")
    return jax.shard_map(
        body if fits else plain_body,
        mesh=mesh,
        in_specs=(row, flat, flat, row, w, b, w, b, w, b, w, b, b, b, b, b),
        out_specs=(row, row, w, b, w, b, w, b, w, b, b, b, b, b),
        check_vma=False,
    )
```

```python
import functools
import math

import numpy as np
import jax, jax.numpy as jnp
from jax import lax
from jax.experimental import pallas as pl
from jax.experimental.pallas import tpu as pltpu
from jax.sharding import PartitionSpec as P

HD, ROT = 64, 16
f32, bf16 = jnp.float32, jnp.bfloat16
MESH = pl.DeviceIdType.MESH
vmem = pl.BlockSpec(memory_space=pltpu.VMEM)
hbm = pl.BlockSpec(memory_space=pl.ANY)
norm_eps = 1e-5
masked_fill = -1e30


def nn(a, b):
    return jnp.dot(a, b, preferred_element_type=f32)


def nt(a, b):
    return lax.dot_general(a, b, (((1,), (1,)), ((), ())), preferred_element_type=f32)


def tn(a, b):
    return lax.dot_general(a, b, (((0,), (0,)), ((), ())), preferred_element_type=f32)


def flipped(a, d, n):
    out, bit = 0, 1
    while bit < n:
        out = out + bit * ((a // bit + d // bit) % 2)
        bit *= 2
    return out


def kernel_p(pos, seg, g1, b1, g2, b2, dense, down, qkv, up, pk, vec):
    half, rows = ROT // 2, pos.shape[0]
    row = lax.broadcasted_iota(jnp.int32, (ROT, rows), 0)
    rate = jnp.zeros((ROT, rows), f32)
    for j in range(half):
        rate = jnp.where(row % half == j, float(np.float32(10000.0) ** np.float32(-2.0 * j / ROT)), rate)
    angle = rate * jnp.broadcast_to(pos[...].astype(f32).reshape(1, rows), (ROT, rows))
    pk[0:ROT, :] = jnp.where(row < half, jnp.cos(angle), jnp.sin(angle))
    pk[ROT:, :] = jnp.zeros((8, rows), f32)
    vec[...] = jnp.zeros_like(vec)

    def line(ref):
        return ref[...].astype(f32).reshape(1, ref.shape[0])

    for i, ref in enumerate((g1, b1, g2, b2, seg)):
        pk[ROT + i : ROT + i + 1, :] = line(ref)
    pk[ROT + 5 : ROT + 6, :] = line(dense) + line(down)
    vec[0:1, 0 : qkv.shape[0]] = line(qkv)
    vec[1:2, 0 : up.shape[0]] = line(up)


def call_p(pos, seg, g1, b1, g2, b2, dense, down, qkv, up):
    n = max(qkv.shape[0], up.shape[0])
    return pl.pallas_call(
        kernel_p,
        out_shape=(jax.ShapeDtypeStruct((24, pos.shape[0]), f32), jax.ShapeDtypeStruct((8, n), f32)),
        name="pack",
    )(pos, seg, g1, b1, g2, b2, dense, down, qkv, up)


def rotary_terms(pk):
    rest = pk[0:ROT, :]
    terms = []
    for _ in range(3):
        part = rest.astype(bf16)
        terms.append(part)
        rest = rest - part.astype(f32)
    return jnp.concatenate(terms + [jnp.ones_like(terms[0])], axis=0)


def rotary_pattern():
    e = np.zeros((64, 9 * 128), np.float32)
    for tile in range(3):
        for lane in range(128):
            col = tile * 128 + lane
            part, d = (col % 192) // HD, col % HD
            base = tile * 384 + lane
            if part == 2 or d >= ROT:
                e[48, base] = 1.0
                continue
            for term in range(3):
                e[term * 16 + d % 8, base] = 1.0
                if d < 8:
                    e[term * 16 + 8 + d, base + 128] = -1.0
                else:
                    e[term * 16 + d, base + 256] = 1.0
    return e


def turn(tile, table, t, sign):
    c = table[:, t * 384 : t * 384 + 128]
    up = table[:, t * 384 + 128 : t * 384 + 256]
    dn = table[:, t * 384 + 256 : t * 384 + 384]
    return tile * c + sign * (pltpu.roll(tile, 120, 1) * up + pltpu.roll(tile, 8, 1) * dn)


def key_docs(seg, j, blk):
    return jnp.broadcast_to(seg[j, 4:5, :], (blk, blk)).T


def attention_setup(qkv, gc, seg, kt, vt, gt, c_buf):
    blocks, _, blk, _ = qkv.shape
    for j in range(blocks):
        rows = pl.ds(j * blk, blk)
        kt[:, rows] = qkv[j, 1].astype(f32).T.astype(bf16)
        vt[:, rows] = qkv[j, 2].astype(f32).T.astype(bf16)
        gt[:, rows] = gc[j].astype(f32).T
    c_buf[...] = key_docs(seg, 0, blk)


def attention_block(h, i, qkv, seg, kt, vt, gt, p_buf, s_buf, acc, t_buf, c_buf):
    blocks, _, blk, lanes = qkv.shape
    half = lanes // 2
    lane = lax.broadcasted_iota(jnp.int32, (blk, lanes), 1) // half
    sub = lax.broadcasted_iota(jnp.int32, (lanes, blk), 0) // half
    causal = lax.broadcasted_iota(jnp.int32, (blk, blk), 0) <= lax.broadcasted_iota(jnp.int32, (blk, blk), 1)
    drow = seg[i, 4:5, :]
    own = pl.ds(pl.multiple_of(h * half, half), half)
    rest = pl.ds(pl.multiple_of((1 - h) * half, half), half)
    q_h = jnp.where(lane == h, qkv[i, 0].astype(f32) * 0.125, 0.0).astype(bf16)
    top = jnp.full((8, blk), masked_fill, f32)
    for j in range(i + 1):
        rows = pl.ds(j * blk, blk)
        s = nt(qkv[j, 1], q_h)
        seen = None
        if j == 0:
            seen = c_buf[...] == drow
        elif i == blocks - 1:
            seen = key_docs(seg, j, blk) == drow
        if j == i:
            seen = causal if seen is None else jnp.logical_and(causal, seen)
        if seen is not None:
            s = jnp.where(seen, s, masked_fill)
        s_buf[rows, :] = s
        top = jnp.maximum(top, jnp.max(s.reshape(blk // 8, 8, blk), axis=0))
    top = jnp.max(top, axis=0, keepdims=True)
    total = jnp.zeros((8, blk), f32)
    out = jnp.zeros((half, blk), f32)
    for j in range(i + 1):
        rows = pl.ds(j * blk, blk)
        p = jnp.exp(s_buf[rows, :] - top)
        s_buf[rows, :] = p
        total = total + jnp.sum(p.reshape(blk // 8, 8, blk), axis=0)
        rounded = p.astype(bf16)
        p_buf[j // 4, :, (j % 4) * blk : (j % 4 + 1) * blk] = rounded
        out = out + nn(vt[own, rows], rounded)
    inv = 1.0 / jnp.sum(total, axis=0, keepdims=True)
    out = out * inv
    t_buf[own, :] = out
    g_h = gt[own, i * blk : (i + 1) * blk]
    corr = jnp.sum(g_h * out, axis=0, keepdims=True) * inv
    gw = g_h * inv
    gw = jnp.concatenate([gw, gw], axis=0)
    gw_t = jnp.where(sub == h, gw, 0.0).astype(bf16)
    right = jnp.concatenate([q_h, jnp.where(sub == h, 0.0, gw).T.astype(bf16)], axis=0)
    dq = jnp.zeros((half, blk), f32)
    for j in range(i + 1):
        rows = pl.ds(j * blk, blk)
        ds = (s_buf[rows, :] * (nn(qkv[j, 2], gw_t) - corr)).astype(bf16)
        acc[rows, :] += nn(jnp.concatenate([ds, p_buf[j // 4, :, (j % 4) * blk : (j % 4 + 1) * blk]], axis=1), right)
        dq = dq + nn(kt[own, rows], ds)
    t_buf[rest, :] = dq * 0.125


SUMS_IN = ((1, 0, 1, (0, 1, 2)), (4, 1, 0, (0,)), (5, 1, 1, (0,)), (8, 1, 0, (1, 2)), (10, 1, 1, (1, 2)))


def kernel_m(
    n_f, n_c, n_y,
    x_hbm, dy_hbm, wq_hbm, wu_hbm, wd_hbm, wn_hbm, pk_hbm, pat_ref, vec_ref,
    out_ref, gx_ref, od_hbm, ou_hbm, on_hbm, oq_hbm, sum_ref,
    X, DY, WQ, WU, WD, WN, PK, N1, N2, XH, SQ, SG, ACT, GUP, PT, H2, GAIN, SMALL,
    CT, DQ, OR, HR, ROWS, GD, GU, GN, GQ, YD, YU, YN, YQ, ZD, ZU, ZN, ZQ, FD, FU, FN, FQ, UU, UQ, S1, R1, S2, R2, ES,
    AQ, AG, AS, KT, VT, GT, SB, DK, TB, CB, CX,
    loca, fsa, fra, vs, vr, asa, ara, fs, fr, as_, ar, ys, yr, zs, zr, gs, gr, hs, hr, own,
):
    me_f, me_c = lax.axis_index("fsdp"), lax.axis_index("ctx")
    rows, width = x_hbm.shape
    n_z, last = n_c // n_y, n_c // n_y - 1
    group = n_c // n_f
    qc, uc = WQ.shape[2], WU.shape[2]
    total, cut = n_f * rows, width // n_f

    bar = pltpu.get_barrier_semaphore()
    for d in range(1, n_f):
        pl.semaphore_signal(bar, inc=1, device_id=(flipped(me_f, d, n_f), me_c), device_id_type=MESH)
    for d in range(1, n_c):
        pl.semaphore_signal(bar, inc=1, device_id=(me_f, (me_c + d) % n_c), device_id_type=MESH)

    def cols(ref, i, n):
        return ref.at[:, pl.ds(pl.multiple_of(i * n, 128), n)]

    local = [
        pltpu.make_async_copy(x_hbm, X.at[me_f], loca.at[0]),
        pltpu.make_async_copy(pk_hbm, PK.at[me_f], loca.at[1]),
        pltpu.make_async_copy(cols(wq_hbm, me_f, qc), WQ.at[me_f], loca.at[2]),
        pltpu.make_async_copy(dy_hbm, DY.at[me_f], loca.at[3]),
        pltpu.make_async_copy(wn_hbm, WN, loca.at[4]),
        pltpu.make_async_copy(cols(wu_hbm, me_f, uc), WU.at[me_f], loca.at[5]),
        pltpu.make_async_copy(wd_hbm, WD, loca.at[6]),
    ]
    for cp in local:
        cp.start()
    pl.semaphore_wait(bar, n_f + n_c - 2)

    my_z, my_y = me_c // n_y, me_c % n_y
    other_y = 1 - my_y
    over_y = me_c + 1 - 2 * my_y
    over_z = me_c + n_y * (1 - 2 * (my_z % 2))
    quarter = WQ.shape[1] // 4

    def to_f(kind, d, src, dst, dest=None):
        return pltpu.make_async_remote_copy(
            src_ref=src, dst_ref=dst, send_sem=fsa.at[kind, d], recv_sem=fra.at[kind, d],
            device_id=(flipped(me_f, d, n_f) if dest is None else dest, me_c), device_id_type=MESH,
        )

    def part(ref, c):
        at = 2 * ((c // n_y) % 2) + c % n_y
        return ref.at[pl.ds(pl.multiple_of(at * quarter, 16), quarter)]

    def copy_of(kind, d):
        dest = flipped(me_f, d, n_f)
        if kind in (0, 1, 4):
            src, buf = ((x_hbm, X), (dy_hbm, DY), None, None, (pk_hbm, PK))[kind]
            return to_f(kind, d, src, buf.at[me_f])
        src, buf, n = ((wq_hbm, WQ, qc), (wu_hbm, WU, uc))[kind - 2]
        if d == 1:
            return to_f(kind, d, cols(src, dest, n), buf.at[me_f])
        return to_f(kind, d, cols(part(src, me_c), dest, n), part(buf.at[me_f], me_c))

    def arrival(kind, d):
        buf = (X, DY, WQ, WU, PK)[kind].at[flipped(me_f, d, n_f)]
        if kind in (2, 3) and d > 1:
            buf = part(buf, me_c)
        to_f(kind, d, buf, buf).wait_recv()

    def share(kind, d, way, mine=True):
        to, far = (over_y, over_z, over_z)[way], over_z + 1 - 2 * my_y
        which = (me_c, me_c, over_y)[way] if mine else (over_y, over_z, far)[way]
        buf = part((WQ, WU)[kind - 2].at[flipped(me_f, d, n_f)], which)
        return pltpu.make_async_remote_copy(
            src_ref=buf, dst_ref=buf, send_sem=vs.at[kind - 2, way, d], recv_sem=vr.at[kind - 2, way, d],
            device_id=(me_f, to), device_id_type=MESH,
        )

    def first_shares(kind):
        for d in range(2, n_f):
            arrival(kind, d)
            share(kind, d, 0).start()
            share(kind, d, 1).start()

    def next_shares(kind):
        for d in range(2, n_f):
            share(kind, d, 0, False).wait_recv()
            share(kind, d, 2).start()

    def weights(kind):
        arrival(kind, 1)
        for d in range(2, n_f):
            share(kind, d, 1, False).wait_recv()
            share(kind, d, 2, False).wait_recv()

    def forward(kind, d):
        buf = (X, DY)[kind].at[flipped(me_f, d, n_f)]
        return to_f(kind, d + 1, buf, buf, flipped(me_f, 1, n_f))

    direct = [1] + list(range(2, n_f, 2))
    for kind, to in ((4, range(1, n_f)), (2, (2, 3, 1)), (3, (2, 3, 1)), (0, direct), (1, direct)):
        for d in to:
            copy_of(kind, d).start()

    local[0].wait()
    local[1].wait()
    for d in range(1, n_f):
        arrival(4, d)
    for j in range(n_f):
        GAIN[0:4, j * (width // n_f) : (j + 1) * (width // n_f)] = PK[j, ROT : ROT + 4, :]
    g1, b1, g2, b2 = GAIN[0:1, :], GAIN[1:2, :], GAIN[2:3, :], GAIN[3:4, :]

    def norm_chunk(src):
        v = X[src].astype(f32)
        center = v - jnp.mean(v, axis=-1, keepdims=True)
        xhat = center * lax.rsqrt(jnp.mean(center * center, axis=-1, keepdims=True) + norm_eps)
        N1[src] = (xhat * g1 + b1).astype(bf16)
        N2[src] = (xhat * g2 + b2).astype(bf16)
        XH[src] = xhat.astype(bf16)

    lane_low = lax.broadcasted_iota(jnp.int32, (rows, 128), 1) < HD

    def to_heads(kind, k, src, dst):
        return pltpu.make_async_remote_copy(
            src_ref=src, dst_ref=dst, send_sem=asa.at[kind, k], recv_sem=ara.at[kind, k],
            device_id=(me_f, (me_c + k) % n_c), device_id_type=MESH,
        )

    def heads_arrival(kind):
        src, buf = ((SQ.at[0, 0], AQ), (SG.at[0, 0], AG), (PK.at[0, pl.ds(ROT, 8)], AS))[kind]
        pltpu.make_async_copy(src, buf.at[me_c], asa.at[kind, 0]).wait()
        for k in range(1, n_c):
            to_heads(kind, k, src, buf.at[(me_c - k + n_c) % n_c]).wait_recv()

    def to_c(kind, s, g, src, dst):
        dest = s * group + g
        k = (dest - me_c + n_c) % n_c

        @pl.when(k != 0)
        def _():
            to_heads(kind, k, src, dst).start()

        @pl.when(k == 0)
        def _():
            pltpu.make_async_copy(src, dst, asa.at[kind, 0]).start()

    def qkv_chunk(d, carry):
        s = flipped(me_f, d, n_f)
        table = tn(rotary_terms(PK[s]), pat_ref[...])
        mixed = nn(N1[s], WQ[...].reshape(width, qc)) + vec_ref[0:1, 0:qc]
        for g in range(group):
            t = [turn(mixed[:, g * 384 + i * 128 : g * 384 + (i + 1) * 128], table, i, 1.0) for i in range(3)]
            SQ[s, g, 0] = jnp.where(lane_low, t[0], t[1]).astype(bf16)
            SQ[s, g, 1] = jnp.where(lane_low, pltpu.roll(t[0], 64, 1), pltpu.roll(t[2], 64, 1)).astype(bf16)
            SQ[s, g, 2] = jnp.where(lane_low, t[1], t[2]).astype(bf16)
            to_c(0, s, g, SQ.at[s, g], AQ.at[me_c])
            to_c(2, s, g, PK.at[s, pl.ds(ROT, 8)], AS.at[me_c])
        return carry

    norm_chunk(me_f)
    first_shares(2)
    arrival(0, 1)
    norm_chunk(flipped(me_f, 1, n_f))
    next_shares(2)
    first_shares(3)
    next_shares(3)
    local[2].wait()
    weights(2)
    lax.fori_loop(0, 2, qkv_chunk, 0)
    for d in range(2, n_f):
        arrival(0, d)
        if d % 2 == 0:
            forward(0, d).start()
        norm_chunk(flipped(me_f, d, n_f))
        lax.fori_loop(d, d + 1, qkv_chunk, 0)
    local[5].wait()
    local[6].wait()
    weights(3)
    SMALL[...] = jnp.zeros_like(SMALL)

    def mlp_forward(s, carry):
        up = nn(N2[s], WU[...].reshape(width, uc)) + vec_ref[1:2, 0:uc]
        cdf = 0.5 * (1.0 + lax.erf(up * (2.0 ** -0.5)))
        ACT[s] = (up * cdf).astype(bf16)
        GUP[s] = (cdf + up * jnp.exp(-0.5 * up * up) * ((2.0 * np.pi) ** -0.5)).astype(bf16)
        PT[s] = nn(ACT[s], WD[...]).astype(bf16)
        return carry

    def mlp_backward(s, carry):
        gu = (nt(DY[s], WD[...]) * GUP[s].astype(f32)).astype(bf16)
        GUP[s] = gu
        SMALL[0:1, 0:uc] += jnp.sum(gu.astype(f32), axis=0, keepdims=True)
        SMALL[1:2, 0:width] += jnp.sum(DY[s].astype(f32), axis=0, keepdims=True)
        e = nt(GUP[s], WU[...].reshape(width, uc))
        SMALL[2:3, 0:width] += jnp.sum(e * XH[s].astype(f32), axis=0, keepdims=True)
        SMALL[3:4, 0:width] += jnp.sum(e, axis=0, keepdims=True)
        H2[s] = (e * g2).astype(bf16)
        return carry

    lax.fori_loop(0, n_f // 2, mlp_forward, 0)
    for d in range(2, n_f, 2):
        arrival(1, d)
        forward(1, d).start()
    local[3].wait()
    local[4].wait()
    for d in range(1, n_f, 2):
        arrival(1, d)

    def gc_chunk(d, carry):
        s = flipped(me_f, d, n_f)
        gc = nt(DY[s], WN[...])
        for g in range(group):
            SG[s, g] = gc[:, g * 128 : (g + 1) * 128].astype(bf16)
            to_c(1, s, g, SG.at[s, g], AG.at[me_c])
        return carry

    lax.fori_loop(0, n_f, gc_chunk, 0)
    lax.fori_loop(n_f // 2, n_f, mlp_forward, 0)


    def down_grad(r, carry):
        at = pl.ds(pl.multiple_of(r * 256, 256), 256)
        per = 256 // (uc // n_c)
        res = tn(ACT[:, :, at].reshape(total, 256), DY[...].reshape(total, width)).astype(bf16)
        res = res.reshape(per, 2, uc // n_c // 2, width)
        for i in range(2):
            GD[i, pl.ds(r * per, per)] = res[:, i]
        return carry

    def up_grad(r, carry):
        at = pl.ds(pl.multiple_of(r * 256, 256), 256)
        res = tn(N2[:, :, at].reshape(total, 256), GUP[...].reshape(total, uc)).astype(bf16)
        res = res.reshape(n_c, 2, 256 // n_c // 2, uc)
        for i in range(2):
            GU[i, :, r] = res[:, i]
        return carry

    def remote(src, dst, ssem, rsem, dev):
        return pltpu.make_async_remote_copy(
            src_ref=src, dst_ref=dst, send_sem=ssem, recv_sem=rsem, device_id=dev, device_id_type=MESH)

    def result(pair, h, i):
        return GUP.at[2 * pair + h, :, pl.ds(pl.multiple_of(i * 128, 128), 128)]

    def back(pair, h, k, i):
        return remote(result(pair, h, i), (CT, DQ)[pair].at[me_c // group, me_c % group, h], as_.at[2 * pair + h, k],
                      ar.at[2 * pair + h, k], (me_f, (me_c + k) % n_c))

    def back_own(pair, h, i):
        return pltpu.make_async_copy(
            result(pair, h, i), (CT, DQ)[pair].at[me_c // group, me_c % group, h], as_.at[2 * pair + h, 0])

    def back_arrival(pair, h):
        back_own(pair, h, me_c).wait()
        for k in range(1, n_c):
            src = (me_c - k + n_c) % n_c
            buf = (CT, DQ)[pair].at[src // group, src % group, h]
            remote(buf, buf, as_.at[2 * pair + h, k], ar.at[2 * pair + h, k], (me_f, src)).wait_recv()

    def give(pair, h, t):
        i = (me_c + 1 + t) % n_c

        @pl.when(t < n_c - 1)
        def _():
            back(pair, h, t + 1, i).start()

        @pl.when(t == n_c - 1)
        def _():
            back_own(pair, h, i).start()

    def items(d, u, n, q):
        return [d.at[0], d.at[1], u.at[0], u.at[1], n, q.at[0], q.at[1]]

    G, YR, ZI = items(GD, GU, GN, GQ), items(YD, YU, YN, YQ), items(ZD, ZU, ZN, ZQ)
    FP = items(FD, FU, FN, FQ)
    UA = [None, None, UU.at[0], UU.at[1], None, UQ.at[0], UQ.at[1]]
    DOWN, UP, DENSE, QKV = (0, 1), (2, 3), (4,), (5, 6)

    def out_at(item, c):
        if item in DENSE:
            return on_hbm.at[c]
        return (od_hbm if item in DOWN else ou_hbm if item in UP else oq_hbm).at[c, item - (0, 0, 2, 2, 4, 5, 5)[item]]

    low_half = 1 - my_z // (n_z // 2)

    def order(k):
        if k == last:
            return my_z
        down = last - k - (my_z - (last - k) + n_z) // n_z
        up = k + (k - my_z + n_z) // n_z
        return low_half * down + (1 - low_half) * up

    def toward(z):
        return (z - my_z + n_z) // n_z

    @pl.when(my_z == 0)
    def _():
        for buf in (ZD, ZU, ZQ):
            buf[:, 1] = jnp.zeros(buf.shape[:1] + buf.shape[2:], bf16)
        ZN[1] = jnp.zeros(ZN.shape[1:], bf16)

    @pl.when(my_z == last)
    def _():
        for buf in (ZD, ZU, ZQ):
            buf[:, 0] = jnp.zeros(buf.shape[:1] + buf.shape[2:], bf16)
        ZN[0] = jnp.zeros(ZN.shape[1:], bf16)

    def line_wait(item, way, z):
        @pl.when(jnp.logical_or(jnp.logical_and(way == 1, my_z > 0), jnp.logical_and(way == 0, my_z < last)))
        def _():
            line_copy(item, way, z, ZI[item].at[way, z]).wait_recv()

    def line_copy(item, way, z, src):
        return remote(src, ZI[item].at[way, z], zs.at[item, z], zr.at[item, way, z],
                      (me_f, (my_z + 2 * way - 1) * n_y + my_y))

    def y_send(item, z):
        src = G[item]
        return remote(src.at[z * n_y + other_y], YR[item].at[z], ys.at[item, z], yr.at[item, z],
                      (me_f, my_z * n_y + other_y))

    def y_start(item, k):
        y_send(item, order(k)).start()

    def y_sum(item, k):
        z = order(k)
        way = toward(z)
        y_send(item, z).wait_recv()
        line_wait(item, way, z)
        acc = YR[item][z].astype(f32) + G[item][z * n_y + my_y].astype(f32) + ZI[item][way, z].astype(f32)
        YR[item][z] = acc.astype(bf16)
        line_copy(item, way, z, YR[item].at[z]).start()

    def piece_total(item):
        y_send(item, my_z).wait_recv()
        for way in (0, 1):
            line_wait(item, way, my_z)
        acc = YR[item][my_z].astype(f32) + G[item][me_c].astype(f32)
        FP[item][...] = (acc + ZI[item][0, my_z].astype(f32) + ZI[item][1, my_z].astype(f32)).astype(bf16)

    def columns(item):
        n = FP[item].shape[2]
        return UA[item].at[:, pl.ds(pl.multiple_of(me_f * n, 128), n)]

    def f_send(item, d):
        dest = flipped(me_f, d, n_f)
        return remote(FP[item].at[dest], columns(item), fs.at[1 + item, d], fr.at[1 + item, d], (dest, me_c))

    def f_start(item):
        for d in range(1, n_f):
            f_send(item, d).start()
        columns(item)[...] = FP[item][me_f]

    def f_wait(item):
        for d in range(1, n_f):
            f_send(item, d).wait_recv()

    def ready(item):
        return FP[item] if UA[item] is None else UA[item]

    def g_send(item, z, step):
        src = ready(item) if z is None else out_at(item, z * n_y + my_y)
        at = my_z if z is None else z
        dst = out_at(item, at * n_y + my_y)
        return remote(src, dst, gs.at[item, (step + 1) // 2, at], gr.at[item, at],
                      (me_f, (my_z + step) * n_y + my_y))

    def h_send(item, z):
        src = ready(item) if z is None else out_at(item, z * n_y + my_y)
        at = my_z if z is None else z
        return remote(src, out_at(item, at * n_y + my_y), hs.at[item, at], hr.at[item, at],
                      (me_f, my_z * n_y + other_y))

    def spread(item):
        @pl.when(my_z < n_z - 1)
        def _():
            g_send(item, None, 1).start()

        @pl.when(my_z > 0)
        def _():
            g_send(item, None, -1).start()

        h_send(item, None).start()
        pltpu.make_async_copy(ready(item), out_at(item, me_c), own.at[item]).start()

    def pass_on(item, far):
        for step in (1, -1):
            z = my_z - step * far

            @pl.when(jnp.logical_and(z >= 0, z < n_z))
            def _(step=step, z=z):
                g_send(item, z, step).wait_recv()
                h_send(item, z).start()

                @pl.when(jnp.logical_and(my_z + step >= 0, my_z + step < n_z))
                def _():
                    g_send(item, z, step).start()

    def spread_wait(item):
        for step in (1, -1):

            @pl.when(jnp.logical_and(my_z + step >= 0, my_z + step < n_z))
            def _(step=step):
                g_send(item, None, step).wait_send()

            for far in range(1, n_z):
                z = my_z - step * far

                @pl.when(jnp.logical_and(jnp.logical_and(z >= 0, z < n_z),
                                         jnp.logical_and(my_z + step >= 0, my_z + step < n_z)))
                def _(step=step, z=z):
                    g_send(item, z, step).wait_send()

        for z in range(n_z):
            src = out_at(item, z * n_y + other_y)
            cp = remote(src, src, hs.at[item, z], hr.at[item, z], (me_f, my_z * n_y + other_y))
            cp.wait_send()
            cp.wait_recv()
        pltpu.make_async_copy(ready(item), out_at(item, me_c), own.at[item]).wait()

    lax.fori_loop(0, width // 256, down_grad, 0)
    for item in DOWN:
        for k in range(n_z):
            y_start(item, k)
    lax.fori_loop(0, n_f, mlp_backward, 0)
    lax.fori_loop(0, width // 256, up_grad, 0)
    for item in UP:
        for k in range(n_z):
            y_start(item, k)

    def sums(item, steps=range(n_c // n_y - 1)):
        for k in steps:
            y_sum(item, k)

    far_first, nearer = range(1), range(1, n_c // n_y - 1)

    at_end = jnp.logical_or(my_z == 0, my_z == last)
    between = jnp.logical_and(my_z > 0, my_z < last)

    heads_arrival(0)
    heads_arrival(2)

    @pl.when(at_end)
    def _():
        sums(0)

    heads_arrival(1)
    attention_setup(AQ, AG, AS, KT, VT, GT, CB)

    def queries_of(i, h):
        def run():
            attention_block(h, i, AQ, AS, KT, VT, GT, ACT, SB, DK, TB, CB)
            GUP[h, :, i * 128 : (i + 1) * 128] = TB[...].T.astype(bf16)

        return run

    def one_head(h, carry):
        DK[...] = jnp.zeros_like(DK)

        def queries_step(t, inner):
            lax.switch((me_c + 1 + t) % n_c, [queries_of(i, h) for i in range(n_c)])
            give(0, h, t)
            for at, where, item, steps in SUMS_IN:

                @pl.when(jnp.logical_and(h * n_c + t == at, at_end if where == 0 else between))
                def _(item=item, steps=steps):
                    sums(item, steps)

            return inner

        lax.fori_loop(0, n_c, queries_step, 0)
        for i in range(n_c):
            GUP[2 + h, :, i * 128 : (i + 1) * 128] = DK[i * rows : (i + 1) * rows, :].astype(bf16)
        for t in range(n_c):
            give(1, h, t)
        return carry

    lax.fori_loop(0, 2, one_head, 0)
    for item in DOWN:
        piece_total(item)
        spread(item)

    @pl.when(at_end)
    def _():
        for item in UP:
            sums(item)

    ROWS[...] = jnp.zeros_like(ROWS)
    for j in range(n_f):
        ROWS[0:1, j * cut : (j + 1) * cut] = PK[j, ROT : ROT + 1, :]
    ROWS[1:2, pl.ds(pl.multiple_of(me_f * cut, 128), cut)] = PK[me_f, ROT + 5 : ROT + 6, :]
    back_arrival(0, 0)
    back_arrival(0, 1)
    lane_low = lax.broadcasted_iota(jnp.int32, (rows, 128), 1) < HD

    def f_rows(kind, d, buf, land):
        dest = flipped(me_f, d, n_f)
        return remote(buf.at[dest], land.at[d - 1], fs.at[kind, d], fr.at[kind, d], (dest, me_c))

    def out_chunk(d, carry):
        s = flipped(me_f, d, n_f)
        for g in range(group):
            CX[s, :, g * 128 : (g + 1) * 128] = jnp.where(
                lane_low, CT[s, g, 0].astype(f32), CT[s, g, 1].astype(f32)).astype(bf16)
        PT[s] = (nn(CX[s], WN[...]) + PT[s].astype(f32) + ROWS[1:2, :]).astype(bf16)

        @pl.when(d != 0)
        def _():
            f_rows(0, d, PT, OR).start()

        return carry

    lax.fori_loop(0, n_f, out_chunk, 0)
    GN[...] = tn(CX[...].reshape(total, cut), DY[...].reshape(total, width)).astype(bf16).reshape(n_c, cut // n_c, width)
    for k in range(n_z):
        y_start(4, k)

    @pl.when(between)
    def _():
        for item in UP:
            sums(item, far_first)

    pass_on(0, 1)
    pass_on(1, 1)

    back_arrival(1, 0)
    back_arrival(1, 1)
    ES[...] = jnp.zeros_like(ES)

    def mixed_chunk(d, carry):
        s = flipped(me_f, d, n_f)
        table = tn(rotary_terms(PK[s]), pat_ref[...])
        for g in range(group):
            c0, c1 = CT[s, g, 0].astype(f32), CT[s, g, 1].astype(f32)
            d0, d1 = DQ[s, g, 0].astype(f32), DQ[s, g, 1].astype(f32)
            t = [pltpu.roll(v, HD, 1) for v in (jnp.where(lane_low, d0, c0), jnp.where(lane_low, c1, d0), d1)]
            for i in range(3):
                lo = g * 384 + i * 128
                m = turn(t[i], table, i, -1.0).astype(bf16)
                N2[s, :, lo : lo + 128] = m
                ES[4:5, lo : lo + 128] += jnp.sum(m.astype(f32), axis=0, keepdims=True)
        e = nt(N2[s, :, 0:qc], WQ[...].reshape(width, qc))
        ES[0:1, :] += jnp.sum(e * XH[s].astype(f32), axis=0, keepdims=True)
        ES[1:2, :] += jnp.sum(e, axis=0, keepdims=True)
        H2[s] = (e * ROWS[0:1, :] + H2[s].astype(f32)).astype(bf16)
        return carry

    lax.fori_loop(0, n_f, mixed_chunk, 0)
    tile = width // n_f

    def qkv_grad(r, carry):
        at = pl.ds(pl.multiple_of(r * tile, tile), tile)
        res = tn(N1[:, :, at].reshape(total, tile), N2[:, :, 0:qc].reshape(total, qc)).astype(bf16)
        res = res.reshape(n_c, 2, tile // n_c // 2, qc)
        for i in range(2):
            GQ[i, :, r] = res[:, i]
        return carry

    lax.fori_loop(0, n_f, qkv_grad, 0)
    for item in QKV:
        for k in range(n_z):
            y_start(item, k)

    for j in range(n_f):
        S1[j, 0:2, :] = ES[0:2, j * tile : (j + 1) * tile]
        S1[j, 2:4, :] = SMALL[2:4, j * tile : (j + 1) * tile]
        S1[j, 4:8, :] = jnp.zeros((4, tile), f32)
    for d in range(1, n_f):
        f_rows(2, d, S1, R1).start()

    @pl.when(between)
    def _():
        for item in UP:
            sums(item, nearer)
        sums(4, far_first)

    @pl.when(at_end)
    def _():
        sums(4)

    pass_on(0, 2)
    pass_on(1, 2)
    for item in UP:
        piece_total(item)
        f_start(item)

    @pl.when(between)
    def _():
        sums(4, nearer)
        sums(5, far_first)

    @pl.when(at_end)
    def _():
        sums(5)

    pass_on(0, 3)
    pass_on(1, 3)
    for d in range(1, n_f):
        f_rows(1, d, H2, HR).start()
    for item in UP:
        f_wait(item)
        spread(item)
    piece_total(4)
    spread(4)

    @pl.when(between)
    def _():
        sums(5, nearer)

    pass_on(2, 1)
    pass_on(3, 1)

    @pl.when(at_end)
    def _():
        sums(6)

    @pl.when(between)
    def _():
        sums(6, far_first)

    piece_total(5)
    f_start(5)
    pass_on(4, 1)

    @pl.when(between)
    def _():
        sums(6, nearer)

    pass_on(2, 2)
    pass_on(3, 2)
    piece_total(6)
    f_start(6)
    f_wait(5)
    spread(5)
    pass_on(4, 2)

    for d in range(1, n_f):
        f_rows(2, d, S1, R1).wait_recv()
    S2[...] = jnp.zeros_like(S2)
    S2[0:1, 0:qc] = ES[4:5, 0:qc]
    S2[1:2, :] = SMALL[0:1, :]
    S2[2:3, 0:tile] = SMALL[1:2, pl.ds(pl.multiple_of(me_f * tile, tile), tile)]
    vec = S1[me_f, 0:4, :]
    for d in range(1, n_f):
        vec = vec + R1[d - 1, 0:4, :]
    S2[3:7, 0:tile] = vec

    def s2_send(k):
        dest = (me_c + k) % n_c
        return remote(S2, R2.at[k], as_.at[4, k], ar.at[4, k], (me_f, dest))

    for k in range(1, n_c):
        s2_send(k).start()

    for d in range(1, n_f):
        f_rows(0, d, PT, OR).wait_recv()
    v = X[me_f].astype(f32)
    acc = v + PT[me_f].astype(f32)
    for d in range(1, n_f):
        acc = acc + OR[d - 1].astype(f32)
    out_ref[...] = acc.astype(bf16)
    f_wait(6)
    spread(6)
    pass_on(2, 3)
    pass_on(3, 3)
    pass_on(5, 1)
    pass_on(4, 3)
    pass_on(6, 1)

    for d in range(1, n_f):
        f_rows(1, d, H2, HR).wait_recv()
    h = H2[me_f].astype(f32)
    for d in range(1, n_f):
        h = h + HR[d - 1].astype(f32)
    center = v - jnp.mean(v, axis=-1, keepdims=True)
    rstd = lax.rsqrt(jnp.mean(center * center, axis=-1, keepdims=True) + norm_eps)
    xhat = center * rstd
    grad = rstd * (h - jnp.mean(h, axis=-1, keepdims=True) - xhat * jnp.mean(h * xhat, axis=-1, keepdims=True))
    gx_ref[...] = (DY[me_f].astype(f32) + grad).astype(bf16)
    pass_on(5, 2)
    pass_on(6, 2)
    pass_on(5, 3)
    pass_on(6, 3)
    tot = S2[...]
    for k in range(1, n_c):
        s2_send(k).wait_recv()
        tot = tot + R2[k]
    sum_ref[...] = tot

    for kind in range(5):
        for d in range(1, n_f):
            if kind < 2 and d % 2 == 1 and d > 1:
                forward(kind, d - 1).wait_send()
            else:
                copy_of(kind, d).wait_send()
            if kind in (2, 3) and d > 1:
                for way in range(3):
                    share(kind, d, way).wait_send()
    for kind, src in ((0, SQ.at[0, 0]), (1, SG.at[0, 0]), (2, PK.at[0, pl.ds(ROT, 8)])):
        for k in range(1, n_c):
            to_heads(kind, k, src, src).wait_send()
    for k in range(1, n_c):
        for kind in range(4):
            back(kind // 2, kind % 2, k, (me_c + k) % n_c).wait_send()
        s2_send(k).wait_send()
    for d in range(1, n_f):
        f_rows(0, d, PT, OR).wait_send()
        f_rows(1, d, H2, HR).wait_send()
        f_rows(2, d, S1, R1).wait_send()
        for item in UP + QKV:
            f_send(item, d).wait_send()
    for item in range(len(G)):
        for z in range(n_z):
            y_send(item, z).wait_send()

            @pl.when(my_z != z)
            def _(item=item, z=z):
                line_copy(item, toward(z), z, YR[item].at[z]).wait_send()

        spread_wait(item)


def call_m(n_f, n_c, n_y, x, dy, wq, wu, wd, wn, pk, vectors):
    rows, width = x.shape
    qc, uc = wq.shape[1] // n_f, wu.shape[1] // n_f
    n_z, group, cut, n = n_c // n_y, n_c // n_f, width // n_f, n_c * rows
    S, V, D = jax.ShapeDtypeStruct, pltpu.VMEM, pltpu.SemaphoreType.DMA
    pat = jnp.asarray(rotary_pattern(), bf16)
    shapes = [(uc // n_c // 2, width), (n_f, cut // n_c // 2, uc), (cut // n_c, width), (n_f, cut // n_c // 2, qc)]
    wides = [shapes[0], (cut // n_c // 2, n_f * uc), shapes[2], (cut // n_c // 2, n_f * qc)]
    act = V((n_f, rows, width), bf16)
    scratch = [
        act, act, V((n_f, cut, qc), bf16), V((n_f, cut, uc), bf16), V((uc, width), bf16), V((cut, width), bf16),
        V((n_f,) + pk.shape, f32), act, act, act, V((n_f, group, 3, rows, 128), bf16), V((n_f, group, rows, 128), bf16),
        V((n_f, rows, uc), bf16), V((n_f, rows, uc), bf16), act, act, V((8, width), f32), V((8, max(uc, width)), f32),
    ]
    scratch += [
        V((n_f, group, 2, rows, 128), bf16), V((n_f, group, 2, rows, 128), bf16),
        V((n_f - 1, rows, width), bf16), V((n_f - 1, rows, width), bf16), V((8, width), f32),
    ]
    parts = [(2,), (2,), (), (2,)]
    scratch += [V(p + (n_c,) + s, bf16) for p, s in zip(parts, shapes)]
    scratch += [V(p + (n_z,) + s, bf16) for p, s in zip(parts, shapes)]
    scratch += [V(p + (2, n_z) + s, bf16) for p, s in zip(parts, shapes)]
    scratch += [V(p + s, bf16) for p, s in zip(parts, shapes)]
    scratch += [V((2,) + wides[1], bf16), V((2,) + wides[3], bf16)]
    scratch += [V((n_f, 8, cut), f32), V((n_f - 1, 8, cut), f32), V((8, uc), f32), V((n_c, 8, uc), f32), V((8, width), f32)]
    scratch += [
        V((n_c, 3, rows, 128), bf16), V((n_c, rows, 128), bf16), V((n_c, 8, rows), f32), V((128, n), bf16), V((128, n), bf16),
        V((128, n), f32), V((n, rows), f32), V((n, 128), f32), V((128, rows), f32), V((rows, rows), f32),
        V((n_f, rows, cut), bf16),
    ]
    scratch += [
        D((7,)), D((5, n_f)), D((5, n_f)), D((2, 3, n_f)), D((2, 3, n_f)), D((3, n_c)), D((3, n_c)),
        D((8, n_f)), D((8, n_f)), D((5, n_c)), D((5, n_c)),
        D((7, n_z)), D((7, n_z)), D((7, n_z)), D((7, 2, n_z)), D((7, 2, n_z)), D((7, n_z)), D((7, n_z)), D((7, n_z)), D((7,)),
    ]
    return pl.pallas_call(
        functools.partial(kernel_m, n_f, n_c, n_y),
        out_shape=(S((rows, width), bf16), S((rows, width), bf16))
        + tuple(S((n_c,) + p + s, bf16) for p, s in zip(parts, wides)) + (S((8, uc), f32),),
        in_specs=[hbm] * 7 + [vmem] * 2,
        out_specs=(vmem, vmem) + (hbm,) * 4 + (vmem,),
        scratch_shapes=scratch,
        compiler_params=pltpu.CompilerParams(collective_id=0, has_side_effects=True, vmem_limit_bytes=63 * 2**20),
        name="layer",
    )(x, dy, wq, wu, wd, wn, pk, pat, vectors)


def kernel_d(od, ou, on, oq, out, gx, vec, fd, fu, fn, fq, o1, o2, bq, b1, b2, bu, n1g, n1b, n2g, n2b):
    for src, dst in ((od, fd), (ou, fu), (on, fn), (oq, fq)):
        dst[...] = src[...].astype(f32)
    o1[...] = out[...]
    o2[...] = gx[...]

    @pl.when(pl.program_id(0) == 0)
    def _():
        for ref, row in ((bq, 0), (bu, 1), (b1, 2), (b2, 2), (n1g, 3), (n1b, 4), (n2g, 5), (n2b, 6)):
            ref[...] = vec[row, 0 : ref.shape[0]]


def call_d(od, ou, on, oq, out, gx, vec, qc):
    steps, cut = 2, on.shape[0]
    S = jax.ShapeDtypeStruct

    def whole(n):
        return pl.BlockSpec((n,), lambda i: (0,))

    def block(a):
        return pl.BlockSpec((a.shape[0] // steps, a.shape[1]), lambda i: (i, 0))

    grads = (od, ou, on, oq)
    sizes = (qc, cut, cut, vec.shape[1], cut, cut, cut, cut)
    return pl.pallas_call(
        kernel_d,
        grid=(steps,),
        out_shape=tuple(S(a.shape, f32) for a in grads)
        + (S(out.shape, bf16), S(out.shape, bf16)) + tuple(S((n,), f32) for n in sizes),
        in_specs=[block(a) for a in grads + (out, gx)] + [pl.BlockSpec(vec.shape, lambda i: (0, 0))],
        out_specs=tuple(block(a) for a in grads + (out, gx)) + tuple(whole(n) for n in sizes),
        compiler_params=pltpu.CompilerParams(vmem_limit_bytes=62 * 2**20),
        name="widen",
    )(od, ou, on, oq, out, gx, vec)


def low(v):
    return v.astype(bf16)


def rotate_back(grad_part, cosine_table, sine_table):
    half_rot = ROT // 2
    g = grad_part[..., :ROT]
    b = g * sine_table[:, None, :]
    turned = jnp.concatenate([b[..., half_rot:], -b[..., :half_rot]], axis=-1)
    return jnp.concatenate([g * cosine_table[:, None, :] + turned, grad_part[..., ROT:]], axis=-1)


def body(
    tokens, segments, positions, cotangent, qkv_weight, qkv_bias, dense_weight, dense_bias,
    up_weight, up_bias, down_weight, down_bias, norm1_gain, norm1_bias, norm2_gain, norm2_bias,
):
    n_f, n_c = lax.axis_size("fsdp"), lax.axis_size("ctx")
    n_y = 2
    pk, vectors = call_p(positions, segments, norm1_gain, norm1_bias, norm2_gain, norm2_bias,
                         dense_bias, down_bias, qkv_bias, up_bias)
    out, gx, od, ou, on, oq, vec = call_m(
        n_f, n_c, n_y, tokens, cotangent, qkv_weight, up_weight, down_weight, dense_weight, pk, vectors)
    od, ou, on, oq = (a.reshape(-1, a.shape[-1]) for a in (od, ou, on, oq))
    gd, gu, gn, gq, out, gx, bq, b1, b2, bu, n1g, n1b, n2g, n2b = call_d(
        od, ou, on, oq, out, gx, vec, qkv_bias.shape[0])
    return out, gx, gq, bq, gn, b1, gu, bu, gd, b2, n1g, n1b, n2g, n2b


def rotary_tables(places):
    half_rot = ROT // 2
    inverse = 10000.0 ** (-2.0 * jnp.arange(half_rot, dtype=jnp.float32) / ROT)
    angles = places.astype(jnp.float32)[:, None] * inverse[None, :]
    angles = jnp.concatenate([angles, angles], axis=1)
    return (jnp.cos(angles), jnp.sin(angles))


def rotate(head_part, cosine_table, sine_table):
    half_rot = ROT // 2
    rotated_part = head_part[..., :ROT]
    turned = jnp.concatenate([-rotated_part[..., half_rot:], rotated_part[..., :half_rot]], axis=-1)
    rotated_part = rotated_part * cosine_table[:, None, :] + turned * sine_table[:, None, :]
    return jnp.concatenate([rotated_part, head_part[..., ROT:]], axis=-1)


def attention_pair(q, k, v, gc, doc):
    length = q.shape[0]
    place = jnp.arange(length, dtype=jnp.int32)
    visible = (place[None, :] <= place[:, None]) & (doc[None, :] == doc[:, None])
    scores = nt(q, k) * (1.0 / math.sqrt(HD))
    row_max = jnp.max(jnp.where(visible, scores, masked_fill), axis=-1, keepdims=True)
    terms = jnp.where(visible, jnp.exp(jnp.where(visible, scores - row_max, 0.0)), 0.0)
    total = jnp.sum(terms, axis=-1, keepdims=True)
    context = nn(low(terms), v) / total
    correction = jnp.sum(gc * context, axis=-1, keepdims=True) / total
    gw = low(gc / total)
    gv = tn(low(terms), gw)
    gs = low(terms * (nt(gw, v) - correction))
    gq = nn(gs, k) * (1.0 / math.sqrt(HD))
    gk = tn(gs, q) * (1.0 / math.sqrt(HD))
    return context, gq, gk, gv


def plain_body(
    tokens, segments, positions, cotangent, qkv_weight, qkv_bias, dense_weight, dense_bias,
    up_weight, up_bias, down_weight, down_bias, norm1_gain, norm1_bias, norm2_gain, norm2_bias,
):
    f32 = jnp.float32
    n_f, n_c = lax.axis_size("fsdp"), lax.axis_size("ctx")
    rows, width = tokens.shape
    heads = width // HD
    pairs = heads // n_c
    group = n_c // n_f
    me_c = lax.axis_index("ctx")
    me_f = lax.axis_index("fsdp")

    x = lax.all_gather(tokens, "fsdp", axis=0, tiled=True).astype(f32)
    dy = lax.all_gather(cotangent, "fsdp", axis=0, tiled=True)
    pos = lax.all_gather(positions, "fsdp", axis=0, tiled=True)
    docs = lax.all_gather(segments, ("fsdp", "ctx"), axis=0, tiled=True)
    w_qkv = lax.all_to_all(qkv_weight, "fsdp", 1, 0, tiled=True)
    w_up = lax.all_to_all(up_weight, "fsdp", 1, 0, tiled=True)
    norms = lax.all_gather(
        jnp.stack([norm1_gain, norm1_bias, norm2_gain, norm2_bias]), "fsdp", axis=1, tiled=True
    ).astype(f32)

    center = x - jnp.mean(x, axis=-1, keepdims=True)
    rstd = lax.rsqrt(jnp.mean(center * center, axis=-1, keepdims=True) + norm_eps)
    xhat = center * rstd
    normed_one = low(xhat * norms[0] + norms[1])
    normed_two = low(xhat * norms[2] + norms[3])

    mixed = nn(normed_one, w_qkv) + qkv_bias.astype(f32)
    total_rows = x.shape[0]
    cos, sin = rotary_tables(pos)
    mixed = mixed.reshape(total_rows, heads // n_f, 3, HD)
    mixed = jnp.stack(
        [rotate(mixed[:, :, 0], cos, sin), rotate(mixed[:, :, 1], cos, sin), mixed[:, :, 2]], axis=2
    )

    def to_heads(a, cols):
        a = a.reshape(n_f, rows, group, cols).transpose(0, 2, 1, 3).reshape(n_c, rows, cols)
        return lax.all_to_all(a, "ctx", 0, 0, tiled=True).reshape(n_c * rows, cols)

    def to_tokens(a, cols):
        a = lax.all_to_all(a.reshape(n_c, rows, cols), "ctx", 0, 0, tiled=True)
        return a.reshape(n_f, group, rows, cols).transpose(0, 2, 1, 3).reshape(total_rows, group * cols)

    qkv = to_heads(low(mixed).reshape(total_rows, -1), pairs * 3 * HD).reshape(-1, pairs, 3, HD)
    grad_context = nt(dy, dense_weight)
    gc = to_heads(low(grad_context), pairs * HD).reshape(-1, pairs, HD).astype(f32)
    seq_doc = lax.dynamic_slice_in_dim(docs, (me_c // group) * (n_c * rows), n_c * rows, 0)

    results = [
        attention_pair(qkv[:, i, 0], qkv[:, i, 1], qkv[:, i, 2], gc[:, i], seq_doc) for i in range(pairs)
    ]
    context = to_tokens(low(jnp.concatenate([r[0] for r in results], axis=1)), pairs * HD)
    grads = jnp.stack([jnp.stack(r[1:], axis=1) for r in results], axis=1)
    grads = to_tokens(low(grads).reshape(n_c * rows, -1), pairs * 3 * HD).astype(f32)
    grads = grads.reshape(total_rows, heads // n_f, 3, HD)
    grad_mixed = low(
        jnp.stack(
            [rotate_back(grads[:, :, 0], cos, sin), rotate_back(grads[:, :, 1], cos, sin), grads[:, :, 2]],
            axis=2,
        )
    ).reshape(total_rows, -1)

    up = nn(normed_two, w_up) + up_bias.astype(f32)
    active, pull = jax.vjp(lambda v: jax.nn.gelu(v, approximate=False), up)
    active = low(active)
    grad_up = low(pull(nt(dy, down_weight))[0])
    g_up_w = tn(normed_two, grad_up)
    g_up_b = jnp.sum(grad_up.astype(f32), axis=0)
    g_down_w = tn(active, dy)
    e_two = nt(grad_up, w_up)

    part = nn(context, dense_weight) + nn(active, down_weight)
    bias = lax.dynamic_update_slice_in_dim(
        jnp.zeros((width,), f32), dense_bias.astype(f32) + down_bias.astype(f32), me_f * (width // n_f), 0
    )
    part = low(part + bias)
    out = lax.psum_scatter(part, "fsdp", scatter_dimension=0, tiled=True).astype(f32)
    layer_out = low(tokens.astype(f32) + out)

    g_dense_w = tn(context, dy)
    g_qkv_w = tn(normed_one, grad_mixed)
    g_qkv_b = jnp.sum(grad_mixed.astype(f32), axis=0)
    e_one = nt(grad_mixed, w_qkv)
    h = low(e_one * norms[0] + e_two * norms[2])
    h = lax.psum_scatter(h, "fsdp", scatter_dimension=0, tiled=True).astype(f32)
    own_xhat = lax.dynamic_slice_in_dim(xhat, me_f * rows, rows, 0)
    own_rstd = lax.dynamic_slice_in_dim(rstd, me_f * rows, rows, 0)
    grad_in = own_rstd * (
        h - jnp.mean(h, axis=-1, keepdims=True) - own_xhat * jnp.mean(h * own_xhat, axis=-1, keepdims=True)
    )
    grad_tokens = low(cotangent.astype(f32) + grad_in)
    vecs = jnp.stack(
        [jnp.sum(e_one * xhat, 0), jnp.sum(e_one, 0), jnp.sum(e_two * xhat, 0), jnp.sum(e_two, 0)]
    )
    vecs = lax.psum(lax.psum_scatter(vecs, "fsdp", scatter_dimension=1, tiled=True), "ctx")
    dy_sum = jnp.sum(cotangent.astype(f32), axis=0)
    dy_sum = lax.psum(lax.psum_scatter(dy_sum, "fsdp", scatter_dimension=0, tiled=True), "ctx")
    g_qkv_b = lax.psum(g_qkv_b, "ctx")
    g_up_b = lax.psum(g_up_b, "ctx")

    def reduced(g, columns):
        if columns:
            g = lax.psum_scatter(low(g).reshape(n_f, -1, g.shape[1]), "ctx", scatter_dimension=1, tiled=True)
            g = lax.all_to_all(g, "fsdp", 0, 0, tiled=True)
            g = g.transpose(1, 0, 2).reshape(g.shape[1], -1)
            return lax.all_gather(g, "ctx", axis=0, tiled=True).astype(f32)
        g = lax.psum_scatter(low(g), "ctx", scatter_dimension=0, tiled=True)
        return lax.all_gather(g, "ctx", axis=0, tiled=True).astype(f32)

    return (
        layer_out, grad_tokens,
        reduced(g_qkv_w, True), g_qkv_b, reduced(g_dense_w, False), dy_sum,
        reduced(g_up_w, True), g_up_b, reduced(g_down_w, False), dy_sum,
        vecs[0], vecs[1], vecs[2], vecs[3],
    )


def solution(mesh):
    n_f, n_c = mesh.shape["fsdp"], mesh.shape["ctx"]
    fits = n_c % n_f == 0 and n_c == 8 and n_f == 4
    row, flat, w, b = P(("fsdp", "ctx"), None), P(("fsdp", "ctx")), P("fsdp", None), P("fsdp")
    return jax.shard_map(
        body if fits else plain_body,
        mesh=mesh,
        in_specs=(row, flat, flat, row, w, b, w, b, w, b, w, b, b, b, b, b),
        out_specs=(row, row, w, b, w, b, w, b, w, b, b, b, b, b),
        check_vma=False,
    )
```

```python
import functools
import math

import numpy as np
import jax, jax.numpy as jnp
from jax import lax
from jax.experimental import pallas as pl
from jax.experimental.pallas import tpu as pltpu
from jax.sharding import PartitionSpec as P

HD, ROT = 64, 16
f32, bf16 = jnp.float32, jnp.bfloat16
MESH = pl.DeviceIdType.MESH
vmem = pl.BlockSpec(memory_space=pltpu.VMEM)
hbm = pl.BlockSpec(memory_space=pl.ANY)
norm_eps = 1e-5
masked_fill = -1e30


def nn(a, b):
    return jnp.dot(a, b, preferred_element_type=f32)


def nt(a, b):
    return lax.dot_general(a, b, (((1,), (1,)), ((), ())), preferred_element_type=f32)


def tn(a, b):
    return lax.dot_general(a, b, (((0,), (0,)), ((), ())), preferred_element_type=f32)


def flipped(a, d, n):
    out, bit = 0, 1
    while bit < n:
        out = out + bit * ((a // bit + d // bit) % 2)
        bit *= 2
    return out


def kernel_p(pos, seg, g1, b1, g2, b2, dense, down, qkv, up, pk, vec):
    half, rows = ROT // 2, pos.shape[0]
    row = lax.broadcasted_iota(jnp.int32, (ROT, rows), 0)
    rate = jnp.zeros((ROT, rows), f32)
    for j in range(half):
        rate = jnp.where(row % half == j, float(np.float32(10000.0) ** np.float32(-2.0 * j / ROT)), rate)
    angle = rate * jnp.broadcast_to(pos[...].astype(f32).reshape(1, rows), (ROT, rows))
    pk[0:ROT, :] = jnp.where(row < half, jnp.cos(angle), jnp.sin(angle))
    pk[ROT:, :] = jnp.zeros((8, rows), f32)
    vec[...] = jnp.zeros_like(vec)

    def line(ref):
        return ref[...].astype(f32).reshape(1, ref.shape[0])

    for i, ref in enumerate((g1, b1, g2, b2, seg)):
        pk[ROT + i : ROT + i + 1, :] = line(ref)
    pk[ROT + 5 : ROT + 6, :] = line(dense) + line(down)
    vec[0:1, 0 : qkv.shape[0]] = line(qkv)
    vec[1:2, 0 : up.shape[0]] = line(up)


def call_p(pos, seg, g1, b1, g2, b2, dense, down, qkv, up):
    n = max(qkv.shape[0], up.shape[0])
    return pl.pallas_call(
        kernel_p,
        out_shape=(jax.ShapeDtypeStruct((24, pos.shape[0]), f32), jax.ShapeDtypeStruct((8, n), f32)),
        name="pack",
    )(pos, seg, g1, b1, g2, b2, dense, down, qkv, up)


def rotary_terms(pk):
    rest = pk[0:ROT, :]
    terms = []
    for _ in range(3):
        part = rest.astype(bf16)
        terms.append(part)
        rest = rest - part.astype(f32)
    return jnp.concatenate(terms + [jnp.ones_like(terms[0])], axis=0)


def rotary_pattern():
    e = np.zeros((64, 9 * 128), np.float32)
    for tile in range(3):
        for lane in range(128):
            col = tile * 128 + lane
            part, d = (col % 192) // HD, col % HD
            base = tile * 384 + lane
            if part == 2 or d >= ROT:
                e[48, base] = 1.0
                continue
            for term in range(3):
                e[term * 16 + d % 8, base] = 1.0
                if d < 8:
                    e[term * 16 + 8 + d, base + 128] = -1.0
                else:
                    e[term * 16 + d, base + 256] = 1.0
    return e


def turn(tile, table, t, sign):
    c = table[:, t * 384 : t * 384 + 128]
    up = table[:, t * 384 + 128 : t * 384 + 256]
    dn = table[:, t * 384 + 256 : t * 384 + 384]
    return tile * c + sign * (pltpu.roll(tile, 120, 1) * up + pltpu.roll(tile, 8, 1) * dn)


def key_docs(seg, j, blk):
    return jnp.broadcast_to(seg[j, 4:5, :], (blk, blk)).T


def attention_setup(qkv, gc, seg, kt, vt, gt, c_buf):
    blocks, _, blk, _ = qkv.shape
    for j in range(blocks):
        rows = pl.ds(j * blk, blk)
        kt[:, rows] = qkv[j, 1].astype(f32).T.astype(bf16)
        vt[:, rows] = qkv[j, 2].astype(f32).T.astype(bf16)
        gt[:, rows] = gc[j].astype(f32).T
    c_buf[...] = key_docs(seg, 0, blk)


def attention_block(h, i, qkv, seg, kt, vt, gt, p_buf, s_buf, acc, t_buf, c_buf):
    blocks, _, blk, lanes = qkv.shape
    half = lanes // 2
    lane = lax.broadcasted_iota(jnp.int32, (blk, lanes), 1) // half
    sub = lax.broadcasted_iota(jnp.int32, (lanes, blk), 0) // half
    causal = lax.broadcasted_iota(jnp.int32, (blk, blk), 0) <= lax.broadcasted_iota(jnp.int32, (blk, blk), 1)
    drow = seg[i, 4:5, :]
    own = pl.ds(pl.multiple_of(h * half, half), half)
    rest = pl.ds(pl.multiple_of((1 - h) * half, half), half)
    q_h = jnp.where(lane == h, qkv[i, 0].astype(f32) * 0.125, 0.0).astype(bf16)
    top = jnp.full((8, blk), masked_fill, f32)
    for j in range(i + 1):
        rows = pl.ds(j * blk, blk)
        s = nt(qkv[j, 1], q_h)
        seen = None
        if j == 0:
            seen = c_buf[...] == drow
        elif i == blocks - 1:
            seen = key_docs(seg, j, blk) == drow
        if j == i:
            seen = causal if seen is None else jnp.logical_and(causal, seen)
        if seen is not None:
            s = jnp.where(seen, s, masked_fill)
        s_buf[rows, :] = s
        top = jnp.maximum(top, jnp.max(s.reshape(blk // 8, 8, blk), axis=0))
    top = jnp.max(top, axis=0, keepdims=True)
    total = jnp.zeros((8, blk), f32)
    out = jnp.zeros((half, blk), f32)
    for j in range(i + 1):
        rows = pl.ds(j * blk, blk)
        p = jnp.exp(s_buf[rows, :] - top)
        s_buf[rows, :] = p
        total = total + jnp.sum(p.reshape(blk // 8, 8, blk), axis=0)
        rounded = p.astype(bf16)
        p_buf[j // 4, :, (j % 4) * blk : (j % 4 + 1) * blk] = rounded
        out = out + nn(vt[own, rows], rounded)
    inv = 1.0 / jnp.sum(total, axis=0, keepdims=True)
    out = out * inv
    t_buf[own, :] = out
    g_h = gt[own, i * blk : (i + 1) * blk]
    corr = jnp.sum(g_h * out, axis=0, keepdims=True) * inv
    gw = g_h * inv
    gw = jnp.concatenate([gw, gw], axis=0)
    gw_t = jnp.where(sub == h, gw, 0.0).astype(bf16)
    right = jnp.concatenate([q_h, jnp.where(sub == h, 0.0, gw).T.astype(bf16)], axis=0)
    dq = jnp.zeros((half, blk), f32)
    for j in range(i + 1):
        rows = pl.ds(j * blk, blk)
        ds = (s_buf[rows, :] * (nn(qkv[j, 2], gw_t) - corr)).astype(bf16)
        acc[rows, :] += nn(jnp.concatenate([ds, p_buf[j // 4, :, (j % 4) * blk : (j % 4 + 1) * blk]], axis=1), right)
        dq = dq + nn(kt[own, rows], ds)
    t_buf[rest, :] = dq * 0.125


SUMS_IN = ((1, 0, 1, (0, 1, 2)), (4, 1, 0, (0,)), (5, 1, 1, (0,)), (8, 1, 0, (1, 2)), (10, 1, 1, (1, 2)))


def kernel_m(
    n_f, n_c, n_y,
    x_hbm, dy_hbm, wq_hbm, wu_hbm, wd_hbm, wn_hbm, pk_hbm, pat_ref, vec_ref,
    out_ref, gx_ref, od_hbm, ou_hbm, on_hbm, oq_hbm, sum_ref,
    X, DY, WQ, WU, WD, WN, PK, N1, N2, XH, SQ, SG, ACT, GUP, PT, H2, GAIN, SMALL,
    CT, DQ, OR, HR, ROWS, GD, GU, GN, GQ, YD, YU, YN, YQ, ZD, ZU, ZN, ZQ, FD, FU, FN, FQ, UU, UQ, S1, R1, S2, R2, ES,
    AQ, AG, AS, KT, VT, GT, SB, DK, TB, CB, CX,
    loca, fsa, fra, vs, vr, asa, ara, fs, fr, as_, ar, ys, yr, zs, zr, gs, gr, hs, hr, own,
):
    me_f, me_c = lax.axis_index("fsdp"), lax.axis_index("ctx")
    rows, width = x_hbm.shape
    n_z, last = n_c // n_y, n_c // n_y - 1
    group = n_c // n_f
    qc, uc = WQ.shape[2], WU.shape[2]
    total, cut = n_f * rows, width // n_f

    bar = pltpu.get_barrier_semaphore()
    for d in range(1, n_f):
        pl.semaphore_signal(bar, inc=1, device_id=(flipped(me_f, d, n_f), me_c), device_id_type=MESH)
    for d in range(1, n_c):
        pl.semaphore_signal(bar, inc=1, device_id=(me_f, (me_c + d) % n_c), device_id_type=MESH)

    def cols(ref, i, n):
        return ref.at[:, pl.ds(pl.multiple_of(i * n, 128), n)]

    local = [
        pltpu.make_async_copy(x_hbm, X.at[me_f], loca.at[0]),
        pltpu.make_async_copy(pk_hbm, PK.at[me_f], loca.at[1]),
        pltpu.make_async_copy(cols(wq_hbm, me_f, qc), WQ.at[me_f], loca.at[2]),
        pltpu.make_async_copy(dy_hbm, DY.at[me_f], loca.at[3]),
        pltpu.make_async_copy(wn_hbm, WN, loca.at[4]),
        pltpu.make_async_copy(cols(wu_hbm, me_f, uc), WU.at[me_f], loca.at[5]),
        pltpu.make_async_copy(wd_hbm, WD, loca.at[6]),
    ]
    for cp in local:
        cp.start()
    pl.semaphore_wait(bar, n_f + n_c - 2)

    my_z, my_y = me_c // n_y, me_c % n_y
    other_y = 1 - my_y
    over_y = me_c + 1 - 2 * my_y
    over_z = me_c + n_y * (1 - 2 * (my_z % 2))
    quarter = WQ.shape[1] // 4

    def to_f(kind, d, src, dst, dest=None):
        return pltpu.make_async_remote_copy(
            src_ref=src, dst_ref=dst, send_sem=fsa.at[kind, d], recv_sem=fra.at[kind, d],
            device_id=(flipped(me_f, d, n_f) if dest is None else dest, me_c), device_id_type=MESH,
        )

    def part(ref, c):
        at = 2 * ((c // n_y) % 2) + c % n_y
        return ref.at[pl.ds(pl.multiple_of(at * quarter, 16), quarter)]

    def copy_of(kind, d):
        dest = flipped(me_f, d, n_f)
        if kind in (0, 1, 4):
            src, buf = ((x_hbm, X), (dy_hbm, DY), None, None, (pk_hbm, PK))[kind]
            return to_f(kind, d, src, buf.at[me_f])
        src, buf, n = ((wq_hbm, WQ, qc), (wu_hbm, WU, uc))[kind - 2]
        if d == 1:
            return to_f(kind, d, cols(src, dest, n), buf.at[me_f])
        return to_f(kind, d, cols(part(src, me_c), dest, n), part(buf.at[me_f], me_c))

    def arrival(kind, d):
        buf = (X, DY, WQ, WU, PK)[kind].at[flipped(me_f, d, n_f)]
        if kind in (2, 3) and d > 1:
            buf = part(buf, me_c)
        to_f(kind, d, buf, buf).wait_recv()

    def share(kind, d, way, mine=True):
        to, far = (over_y, over_z, over_z)[way], over_z + 1 - 2 * my_y
        which = (me_c, me_c, over_y)[way] if mine else (over_y, over_z, far)[way]
        buf = part((WQ, WU)[kind - 2].at[flipped(me_f, d, n_f)], which)
        return pltpu.make_async_remote_copy(
            src_ref=buf, dst_ref=buf, send_sem=vs.at[kind - 2, way, d], recv_sem=vr.at[kind - 2, way, d],
            device_id=(me_f, to), device_id_type=MESH,
        )

    def first_shares(kind):
        for d in range(2, n_f):
            arrival(kind, d)
            share(kind, d, 0).start()
            share(kind, d, 1).start()

    def next_shares(kind):
        for d in range(2, n_f):
            share(kind, d, 0, False).wait_recv()
            share(kind, d, 2).start()

    def weights(kind):
        arrival(kind, 1)
        for d in range(2, n_f):
            share(kind, d, 1, False).wait_recv()
            share(kind, d, 2, False).wait_recv()

    def forward(kind, d):
        buf = (X, DY)[kind].at[flipped(me_f, d, n_f)]
        return to_f(kind, d + 1, buf, buf, flipped(me_f, 1, n_f))

    direct = [1] + list(range(2, n_f, 2))
    for kind, to in ((4, range(1, n_f)), (2, (2, 3, 1)), (3, (2, 3, 1)), (0, direct), (1, direct)):
        for d in to:
            copy_of(kind, d).start()

    local[0].wait()
    local[1].wait()
    for d in range(1, n_f):
        arrival(4, d)
    for j in range(n_f):
        GAIN[0:4, j * (width // n_f) : (j + 1) * (width // n_f)] = PK[j, ROT : ROT + 4, :]
    g1, b1, g2, b2 = GAIN[0:1, :], GAIN[1:2, :], GAIN[2:3, :], GAIN[3:4, :]

    def norm_chunk(src):
        v = X[src].astype(f32)
        center = v - jnp.mean(v, axis=-1, keepdims=True)
        xhat = center * lax.rsqrt(jnp.mean(center * center, axis=-1, keepdims=True) + norm_eps)
        N1[src] = (xhat * g1 + b1).astype(bf16)
        N2[src] = (xhat * g2 + b2).astype(bf16)
        XH[src] = xhat.astype(bf16)

    lane_low = lax.broadcasted_iota(jnp.int32, (rows, 128), 1) < HD

    def to_heads(kind, k, src, dst):
        return pltpu.make_async_remote_copy(
            src_ref=src, dst_ref=dst, send_sem=asa.at[kind, k], recv_sem=ara.at[kind, k],
            device_id=(me_f, (me_c + k) % n_c), device_id_type=MESH,
        )

    def heads_arrival(kind):
        src, buf = ((SQ.at[0, 0], AQ), (SG.at[0, 0], AG), (PK.at[0, pl.ds(ROT, 8)], AS))[kind]
        pltpu.make_async_copy(src, buf.at[me_c], asa.at[kind, 0]).wait()
        for k in range(1, n_c):
            to_heads(kind, k, src, buf.at[(me_c - k + n_c) % n_c]).wait_recv()

    def to_c(kind, s, g, src, dst):
        dest = s * group + g
        k = (dest - me_c + n_c) % n_c

        @pl.when(k != 0)
        def _():
            to_heads(kind, k, src, dst).start()

        @pl.when(k == 0)
        def _():
            pltpu.make_async_copy(src, dst, asa.at[kind, 0]).start()

    def qkv_chunk(d, carry):
        s = flipped(me_f, d, n_f)
        table = tn(rotary_terms(PK[s]), pat_ref[...])
        mixed = nn(N1[s], WQ[...].reshape(width, qc)) + vec_ref[0:1, 0:qc]
        for g in range(group):
            t = [turn(mixed[:, g * 384 + i * 128 : g * 384 + (i + 1) * 128], table, i, 1.0) for i in range(3)]
            SQ[s, g, 0] = jnp.where(lane_low, t[0], t[1]).astype(bf16)
            SQ[s, g, 1] = jnp.where(lane_low, pltpu.roll(t[0], 64, 1), pltpu.roll(t[2], 64, 1)).astype(bf16)
            SQ[s, g, 2] = jnp.where(lane_low, t[1], t[2]).astype(bf16)
            to_c(0, s, g, SQ.at[s, g], AQ.at[me_c])
            to_c(2, s, g, PK.at[s, pl.ds(ROT, 8)], AS.at[me_c])
        return carry

    norm_chunk(me_f)
    first_shares(2)
    arrival(0, 1)
    norm_chunk(flipped(me_f, 1, n_f))
    next_shares(2)
    first_shares(3)
    next_shares(3)
    local[2].wait()
    weights(2)
    lax.fori_loop(0, 2, qkv_chunk, 0)
    for d in range(2, n_f):
        arrival(0, d)
        if d % 2 == 0:
            forward(0, d).start()
        norm_chunk(flipped(me_f, d, n_f))
        lax.fori_loop(d, d + 1, qkv_chunk, 0)
    local[5].wait()
    local[6].wait()
    weights(3)
    SMALL[...] = jnp.zeros_like(SMALL)

    def mlp_forward(s, carry):
        up = nn(N2[s], WU[...].reshape(width, uc)) + vec_ref[1:2, 0:uc]
        cdf = 0.5 * (1.0 + lax.erf(up * (2.0 ** -0.5)))
        ACT[s] = (up * cdf).astype(bf16)
        GUP[s] = (cdf + up * jnp.exp(-0.5 * up * up) * ((2.0 * np.pi) ** -0.5)).astype(bf16)
        PT[s] = nn(ACT[s], WD[...]).astype(bf16)
        return carry

    def mlp_backward(s, carry):
        gu = (nt(DY[s], WD[...]) * GUP[s].astype(f32)).astype(bf16)
        GUP[s] = gu
        SMALL[0:1, 0:uc] += jnp.sum(gu.astype(f32), axis=0, keepdims=True)
        SMALL[1:2, 0:width] += jnp.sum(DY[s].astype(f32), axis=0, keepdims=True)
        e = nt(GUP[s], WU[...].reshape(width, uc))
        SMALL[2:3, 0:width] += jnp.sum(e * XH[s].astype(f32), axis=0, keepdims=True)
        SMALL[3:4, 0:width] += jnp.sum(e, axis=0, keepdims=True)
        H2[s] = (e * g2).astype(bf16)
        return carry

    lax.fori_loop(0, n_f // 2, mlp_forward, 0)
    for d in range(2, n_f, 2):
        arrival(1, d)
        forward(1, d).start()
    local[3].wait()
    local[4].wait()
    for d in range(1, n_f, 2):
        arrival(1, d)

    def gc_chunk(d, carry):
        s = flipped(me_f, d, n_f)
        gc = nt(DY[s], WN[...])
        for g in range(group):
            SG[s, g] = gc[:, g * 128 : (g + 1) * 128].astype(bf16)
            to_c(1, s, g, SG.at[s, g], AG.at[me_c])
        return carry

    lax.fori_loop(0, n_f, gc_chunk, 0)
    lax.fori_loop(n_f // 2, n_f, mlp_forward, 0)


    def down_grad(r, carry):
        at = pl.ds(pl.multiple_of(r * 256, 256), 256)
        per = 256 // (uc // n_c)
        res = tn(ACT[:, :, at].reshape(total, 256), DY[...].reshape(total, width)).astype(bf16)
        res = res.reshape(per, 2, uc // n_c // 2, width)
        for i in range(2):
            GD[i, pl.ds(r * per, per)] = res[:, i]
        return carry

    def up_grad(r, carry):
        at = pl.ds(pl.multiple_of(r * 256, 256), 256)
        res = tn(N2[:, :, at].reshape(total, 256), GUP[...].reshape(total, uc)).astype(bf16)
        res = res.reshape(n_c, 2, 256 // n_c // 2, uc)
        for i in range(2):
            GU[i, :, r] = res[:, i]
        return carry

    def remote(src, dst, ssem, rsem, dev):
        return pltpu.make_async_remote_copy(
            src_ref=src, dst_ref=dst, send_sem=ssem, recv_sem=rsem, device_id=dev, device_id_type=MESH)

    def result(pair, h, i):
        return GUP.at[2 * pair + h, :, pl.ds(pl.multiple_of(i * 128, 128), 128)]

    def back(pair, h, k, i):
        return remote(result(pair, h, i), (CT, DQ)[pair].at[me_c // group, me_c % group, h], as_.at[2 * pair + h, k],
                      ar.at[2 * pair + h, k], (me_f, (me_c + k) % n_c))

    def back_own(pair, h, i):
        return pltpu.make_async_copy(
            result(pair, h, i), (CT, DQ)[pair].at[me_c // group, me_c % group, h], as_.at[2 * pair + h, 0])

    def back_arrival(pair, h):
        back_own(pair, h, me_c).wait()
        for k in range(1, n_c):
            src = (me_c - k + n_c) % n_c
            buf = (CT, DQ)[pair].at[src // group, src % group, h]
            remote(buf, buf, as_.at[2 * pair + h, k], ar.at[2 * pair + h, k], (me_f, src)).wait_recv()

    def turn_to(t):
        half = n_c // 2
        return (1 - t % 2) * (half + t // 2) + t % 2 * (half - 1 - t // 2)

    def give(pair, h, t):
        k = turn_to(t)
        i = (me_c + k) % n_c

        @pl.when(k != 0)
        def _():
            back(pair, h, k, i).start()

        @pl.when(k == 0)
        def _():
            back_own(pair, h, i).start()

    def items(d, u, n, q):
        return [d.at[0], d.at[1], u.at[0], u.at[1], n, q.at[0], q.at[1]]

    G, YR, ZI = items(GD, GU, GN, GQ), items(YD, YU, YN, YQ), items(ZD, ZU, ZN, ZQ)
    FP = items(FD, FU, FN, FQ)
    UA = [None, None, UU.at[0], UU.at[1], None, UQ.at[0], UQ.at[1]]
    DOWN, UP, DENSE, QKV = (0, 1), (2, 3), (4,), (5, 6)

    def out_at(item, c):
        if item in DENSE:
            return on_hbm.at[c]
        return (od_hbm if item in DOWN else ou_hbm if item in UP else oq_hbm).at[c, item - (0, 0, 2, 2, 4, 5, 5)[item]]

    low_half = 1 - my_z // (n_z // 2)

    def order(k):
        if k == last:
            return my_z
        down = last - k - (my_z - (last - k) + n_z) // n_z
        up = k + (k - my_z + n_z) // n_z
        return low_half * down + (1 - low_half) * up

    def toward(z):
        return (z - my_z + n_z) // n_z

    @pl.when(my_z == 0)
    def _():
        for buf in (ZD, ZU, ZQ):
            buf[:, 1] = jnp.zeros(buf.shape[:1] + buf.shape[2:], bf16)
        ZN[1] = jnp.zeros(ZN.shape[1:], bf16)

    @pl.when(my_z == last)
    def _():
        for buf in (ZD, ZU, ZQ):
            buf[:, 0] = jnp.zeros(buf.shape[:1] + buf.shape[2:], bf16)
        ZN[0] = jnp.zeros(ZN.shape[1:], bf16)

    def line_wait(item, way, z):
        @pl.when(jnp.logical_or(jnp.logical_and(way == 1, my_z > 0), jnp.logical_and(way == 0, my_z < last)))
        def _():
            line_copy(item, way, z, ZI[item].at[way, z]).wait_recv()

    def line_copy(item, way, z, src):
        return remote(src, ZI[item].at[way, z], zs.at[item, z], zr.at[item, way, z],
                      (me_f, (my_z + 2 * way - 1) * n_y + my_y))

    def y_send(item, z):
        src = G[item]
        return remote(src.at[z * n_y + other_y], YR[item].at[z], ys.at[item, z], yr.at[item, z],
                      (me_f, my_z * n_y + other_y))

    def y_start(item, k):
        y_send(item, order(k)).start()

    def y_sum(item, k):
        z = order(k)
        way = toward(z)
        y_send(item, z).wait_recv()
        line_wait(item, way, z)
        acc = YR[item][z].astype(f32) + G[item][z * n_y + my_y].astype(f32) + ZI[item][way, z].astype(f32)
        YR[item][z] = acc.astype(bf16)
        line_copy(item, way, z, YR[item].at[z]).start()

    def piece_total(item):
        y_send(item, my_z).wait_recv()
        for way in (0, 1):
            line_wait(item, way, my_z)
        acc = YR[item][my_z].astype(f32) + G[item][me_c].astype(f32)
        FP[item][...] = (acc + ZI[item][0, my_z].astype(f32) + ZI[item][1, my_z].astype(f32)).astype(bf16)

    def columns(item):
        n = FP[item].shape[2]
        return UA[item].at[:, pl.ds(pl.multiple_of(me_f * n, 128), n)]

    def f_send(item, d):
        dest = flipped(me_f, d, n_f)
        return remote(FP[item].at[dest], columns(item), fs.at[1 + item, d], fr.at[1 + item, d], (dest, me_c))

    def f_start(item):
        for d in range(1, n_f):
            f_send(item, d).start()
        columns(item)[...] = FP[item][me_f]

    def f_wait(item):
        for d in range(1, n_f):
            f_send(item, d).wait_recv()

    def ready(item):
        return FP[item] if UA[item] is None else UA[item]

    def g_send(item, z, step):
        src = ready(item) if z is None else out_at(item, z * n_y + my_y)
        at = my_z if z is None else z
        dst = out_at(item, at * n_y + my_y)
        return remote(src, dst, gs.at[item, (step + 1) // 2, at], gr.at[item, at],
                      (me_f, (my_z + step) * n_y + my_y))

    def h_send(item, z):
        src = ready(item) if z is None else out_at(item, z * n_y + my_y)
        at = my_z if z is None else z
        return remote(src, out_at(item, at * n_y + my_y), hs.at[item, at], hr.at[item, at],
                      (me_f, my_z * n_y + other_y))

    def spread(item):
        @pl.when(my_z < n_z - 1)
        def _():
            g_send(item, None, 1).start()

        @pl.when(my_z > 0)
        def _():
            g_send(item, None, -1).start()

        h_send(item, None).start()
        pltpu.make_async_copy(ready(item), out_at(item, me_c), own.at[item]).start()

    def pass_on(item, far):
        for step in (1, -1):
            z = my_z - step * far

            @pl.when(jnp.logical_and(z >= 0, z < n_z))
            def _(step=step, z=z):
                g_send(item, z, step).wait_recv()
                h_send(item, z).start()

                @pl.when(jnp.logical_and(my_z + step >= 0, my_z + step < n_z))
                def _():
                    g_send(item, z, step).start()

    def spread_wait(item):
        for step in (1, -1):

            @pl.when(jnp.logical_and(my_z + step >= 0, my_z + step < n_z))
            def _(step=step):
                g_send(item, None, step).wait_send()

            for far in range(1, n_z):
                z = my_z - step * far

                @pl.when(jnp.logical_and(jnp.logical_and(z >= 0, z < n_z),
                                         jnp.logical_and(my_z + step >= 0, my_z + step < n_z)))
                def _(step=step, z=z):
                    g_send(item, z, step).wait_send()

        for z in range(n_z):
            src = out_at(item, z * n_y + other_y)
            cp = remote(src, src, hs.at[item, z], hr.at[item, z], (me_f, my_z * n_y + other_y))
            cp.wait_send()
            cp.wait_recv()
        pltpu.make_async_copy(ready(item), out_at(item, me_c), own.at[item]).wait()

    lax.fori_loop(0, width // 256, down_grad, 0)
    for item in DOWN:
        for k in range(n_z):
            y_start(item, k)
    lax.fori_loop(0, n_f, mlp_backward, 0)
    lax.fori_loop(0, width // 256, up_grad, 0)
    for item in UP:
        for k in range(n_z):
            y_start(item, k)

    def sums(item, steps=range(n_c // n_y - 1)):
        for k in steps:
            y_sum(item, k)

    far_first, nearer = range(1), range(1, n_c // n_y - 1)

    at_end = jnp.logical_or(my_z == 0, my_z == last)
    between = jnp.logical_and(my_z > 0, my_z < last)

    heads_arrival(0)
    heads_arrival(2)

    @pl.when(at_end)
    def _():
        sums(0)

    heads_arrival(1)
    attention_setup(AQ, AG, AS, KT, VT, GT, CB)

    def queries_of(i, h):
        def run():
            attention_block(h, i, AQ, AS, KT, VT, GT, ACT, SB, DK, TB, CB)
            GUP[h, :, i * 128 : (i + 1) * 128] = TB[...].T.astype(bf16)

        return run

    def one_head(h, carry):
        DK[...] = jnp.zeros_like(DK)

        def queries_step(t, inner):
            lax.switch((me_c + turn_to(t)) % n_c, [queries_of(i, h) for i in range(n_c)])
            give(0, h, t)
            for at, where, item, steps in SUMS_IN:

                @pl.when(jnp.logical_and(h * n_c + t == at, at_end if where == 0 else between))
                def _(item=item, steps=steps):
                    sums(item, steps)

            return inner

        lax.fori_loop(0, n_c, queries_step, 0)
        for i in range(n_c):
            GUP[2 + h, :, i * 128 : (i + 1) * 128] = DK[i * rows : (i + 1) * rows, :].astype(bf16)
        for t in range(n_c):
            give(1, h, t)
        return carry

    lax.fori_loop(0, 2, one_head, 0)
    for item in DOWN:
        piece_total(item)
        spread(item)

    @pl.when(at_end)
    def _():
        for item in UP:
            sums(item)

    ROWS[...] = jnp.zeros_like(ROWS)
    for j in range(n_f):
        ROWS[0:1, j * cut : (j + 1) * cut] = PK[j, ROT : ROT + 1, :]
    ROWS[1:2, pl.ds(pl.multiple_of(me_f * cut, 128), cut)] = PK[me_f, ROT + 5 : ROT + 6, :]
    back_arrival(0, 0)
    back_arrival(0, 1)
    lane_low = lax.broadcasted_iota(jnp.int32, (rows, 128), 1) < HD

    def f_rows(kind, d, buf, land):
        dest = flipped(me_f, d, n_f)
        return remote(buf.at[dest], land.at[d - 1], fs.at[kind, d], fr.at[kind, d], (dest, me_c))

    def out_chunk(d, carry):
        s = flipped(me_f, d, n_f)
        for g in range(group):
            CX[s, :, g * 128 : (g + 1) * 128] = jnp.where(
                lane_low, CT[s, g, 0].astype(f32), CT[s, g, 1].astype(f32)).astype(bf16)
        PT[s] = (nn(CX[s], WN[...]) + PT[s].astype(f32) + ROWS[1:2, :]).astype(bf16)

        @pl.when(d != 0)
        def _():
            f_rows(0, d, PT, OR).start()

        return carry

    lax.fori_loop(0, n_f, out_chunk, 0)
    GN[...] = tn(CX[...].reshape(total, cut), DY[...].reshape(total, width)).astype(bf16).reshape(n_c, cut // n_c, width)
    for k in range(n_z):
        y_start(4, k)

    @pl.when(between)
    def _():
        for item in UP:
            sums(item, far_first)

    pass_on(0, 1)
    pass_on(1, 1)

    back_arrival(1, 0)
    back_arrival(1, 1)
    ES[...] = jnp.zeros_like(ES)

    def mixed_chunk(d, carry):
        s = flipped(me_f, d, n_f)
        table = tn(rotary_terms(PK[s]), pat_ref[...])
        for g in range(group):
            c0, c1 = CT[s, g, 0].astype(f32), CT[s, g, 1].astype(f32)
            d0, d1 = DQ[s, g, 0].astype(f32), DQ[s, g, 1].astype(f32)
            t = [pltpu.roll(v, HD, 1) for v in (jnp.where(lane_low, d0, c0), jnp.where(lane_low, c1, d0), d1)]
            for i in range(3):
                lo = g * 384 + i * 128
                m = turn(t[i], table, i, -1.0).astype(bf16)
                N2[s, :, lo : lo + 128] = m
                ES[4:5, lo : lo + 128] += jnp.sum(m.astype(f32), axis=0, keepdims=True)
        e = nt(N2[s, :, 0:qc], WQ[...].reshape(width, qc))
        ES[0:1, :] += jnp.sum(e * XH[s].astype(f32), axis=0, keepdims=True)
        ES[1:2, :] += jnp.sum(e, axis=0, keepdims=True)
        H2[s] = (e * ROWS[0:1, :] + H2[s].astype(f32)).astype(bf16)
        return carry

    lax.fori_loop(0, n_f, mixed_chunk, 0)
    tile = width // n_f

    def qkv_grad(r, carry):
        at = pl.ds(pl.multiple_of(r * tile, tile), tile)
        res = tn(N1[:, :, at].reshape(total, tile), N2[:, :, 0:qc].reshape(total, qc)).astype(bf16)
        res = res.reshape(n_c, 2, tile // n_c // 2, qc)
        for i in range(2):
            GQ[i, :, r] = res[:, i]
        return carry

    lax.fori_loop(0, n_f, qkv_grad, 0)
    for item in QKV:
        for k in range(n_z):
            y_start(item, k)

    for j in range(n_f):
        S1[j, 0:2, :] = ES[0:2, j * tile : (j + 1) * tile]
        S1[j, 2:4, :] = SMALL[2:4, j * tile : (j + 1) * tile]
        S1[j, 4:8, :] = jnp.zeros((4, tile), f32)
    for d in range(1, n_f):
        f_rows(2, d, S1, R1).start()

    @pl.when(between)
    def _():
        for item in UP:
            sums(item, nearer)
        sums(4, far_first)

    @pl.when(at_end)
    def _():
        sums(4)

    pass_on(0, 2)
    pass_on(1, 2)
    for item in UP:
        piece_total(item)
        f_start(item)

    @pl.when(between)
    def _():
        sums(4, nearer)
        sums(5, far_first)

    @pl.when(at_end)
    def _():
        sums(5)

    pass_on(0, 3)
    pass_on(1, 3)
    for d in range(1, n_f):
        f_rows(1, d, H2, HR).start()
    for item in UP:
        f_wait(item)
        spread(item)
    piece_total(4)
    spread(4)

    @pl.when(between)
    def _():
        sums(5, nearer)

    pass_on(2, 1)
    pass_on(3, 1)

    @pl.when(at_end)
    def _():
        sums(6)

    @pl.when(between)
    def _():
        sums(6, far_first)

    piece_total(5)
    f_start(5)
    pass_on(4, 1)

    @pl.when(between)
    def _():
        sums(6, nearer)

    pass_on(2, 2)
    pass_on(3, 2)
    piece_total(6)
    f_start(6)
    f_wait(5)
    spread(5)
    pass_on(4, 2)

    for d in range(1, n_f):
        f_rows(2, d, S1, R1).wait_recv()
    S2[...] = jnp.zeros_like(S2)
    S2[0:1, 0:qc] = ES[4:5, 0:qc]
    S2[1:2, :] = SMALL[0:1, :]
    S2[2:3, 0:tile] = SMALL[1:2, pl.ds(pl.multiple_of(me_f * tile, tile), tile)]
    vec = S1[me_f, 0:4, :]
    for d in range(1, n_f):
        vec = vec + R1[d - 1, 0:4, :]
    S2[3:7, 0:tile] = vec

    def s2_send(k):
        dest = (me_c + k) % n_c
        return remote(S2, R2.at[k], as_.at[4, k], ar.at[4, k], (me_f, dest))

    for k in range(1, n_c):
        s2_send(k).start()

    for d in range(1, n_f):
        f_rows(0, d, PT, OR).wait_recv()
    v = X[me_f].astype(f32)
    acc = v + PT[me_f].astype(f32)
    for d in range(1, n_f):
        acc = acc + OR[d - 1].astype(f32)
    out_ref[...] = acc.astype(bf16)
    f_wait(6)
    spread(6)
    pass_on(2, 3)
    pass_on(3, 3)
    pass_on(5, 1)
    pass_on(4, 3)
    pass_on(6, 1)

    for d in range(1, n_f):
        f_rows(1, d, H2, HR).wait_recv()
    h = H2[me_f].astype(f32)
    for d in range(1, n_f):
        h = h + HR[d - 1].astype(f32)
    center = v - jnp.mean(v, axis=-1, keepdims=True)
    rstd = lax.rsqrt(jnp.mean(center * center, axis=-1, keepdims=True) + norm_eps)
    xhat = center * rstd
    grad = rstd * (h - jnp.mean(h, axis=-1, keepdims=True) - xhat * jnp.mean(h * xhat, axis=-1, keepdims=True))
    gx_ref[...] = (DY[me_f].astype(f32) + grad).astype(bf16)
    pass_on(5, 2)
    pass_on(6, 2)
    pass_on(5, 3)
    pass_on(6, 3)
    tot = S2[...]
    for k in range(1, n_c):
        s2_send(k).wait_recv()
        tot = tot + R2[k]
    sum_ref[...] = tot

    for kind in range(5):
        for d in range(1, n_f):
            if kind < 2 and d % 2 == 1 and d > 1:
                forward(kind, d - 1).wait_send()
            else:
                copy_of(kind, d).wait_send()
            if kind in (2, 3) and d > 1:
                for way in range(3):
                    share(kind, d, way).wait_send()
    for kind, src in ((0, SQ.at[0, 0]), (1, SG.at[0, 0]), (2, PK.at[0, pl.ds(ROT, 8)])):
        for k in range(1, n_c):
            to_heads(kind, k, src, src).wait_send()
    for k in range(1, n_c):
        for kind in range(4):
            back(kind // 2, kind % 2, k, (me_c + k) % n_c).wait_send()
        s2_send(k).wait_send()
    for d in range(1, n_f):
        f_rows(0, d, PT, OR).wait_send()
        f_rows(1, d, H2, HR).wait_send()
        f_rows(2, d, S1, R1).wait_send()
        for item in UP + QKV:
            f_send(item, d).wait_send()
    for item in range(len(G)):
        for z in range(n_z):
            y_send(item, z).wait_send()

            @pl.when(my_z != z)
            def _(item=item, z=z):
                line_copy(item, toward(z), z, YR[item].at[z]).wait_send()

        spread_wait(item)


def call_m(n_f, n_c, n_y, x, dy, wq, wu, wd, wn, pk, vectors):
    rows, width = x.shape
    qc, uc = wq.shape[1] // n_f, wu.shape[1] // n_f
    n_z, group, cut, n = n_c // n_y, n_c // n_f, width // n_f, n_c * rows
    S, V, D = jax.ShapeDtypeStruct, pltpu.VMEM, pltpu.SemaphoreType.DMA
    pat = jnp.asarray(rotary_pattern(), bf16)
    shapes = [(uc // n_c // 2, width), (n_f, cut // n_c // 2, uc), (cut // n_c, width), (n_f, cut // n_c // 2, qc)]
    wides = [shapes[0], (cut // n_c // 2, n_f * uc), shapes[2], (cut // n_c // 2, n_f * qc)]
    act = V((n_f, rows, width), bf16)
    scratch = [
        act, act, V((n_f, cut, qc), bf16), V((n_f, cut, uc), bf16), V((uc, width), bf16), V((cut, width), bf16),
        V((n_f,) + pk.shape, f32), act, act, act, V((n_f, group, 3, rows, 128), bf16), V((n_f, group, rows, 128), bf16),
        V((n_f, rows, uc), bf16), V((n_f, rows, uc), bf16), act, act, V((8, width), f32), V((8, max(uc, width)), f32),
    ]
    scratch += [
        V((n_f, group, 2, rows, 128), bf16), V((n_f, group, 2, rows, 128), bf16),
        V((n_f - 1, rows, width), bf16), V((n_f - 1, rows, width), bf16), V((8, width), f32),
    ]
    parts = [(2,), (2,), (), (2,)]
    scratch += [V(p + (n_c,) + s, bf16) for p, s in zip(parts, shapes)]
    scratch += [V(p + (n_z,) + s, bf16) for p, s in zip(parts, shapes)]
    scratch += [V(p + (2, n_z) + s, bf16) for p, s in zip(parts, shapes)]
    scratch += [V(p + s, bf16) for p, s in zip(parts, shapes)]
    scratch += [V((2,) + wides[1], bf16), V((2,) + wides[3], bf16)]
    scratch += [V((n_f, 8, cut), f32), V((n_f - 1, 8, cut), f32), V((8, uc), f32), V((n_c, 8, uc), f32), V((8, width), f32)]
    scratch += [
        V((n_c, 3, rows, 128), bf16), V((n_c, rows, 128), bf16), V((n_c, 8, rows), f32), V((128, n), bf16), V((128, n), bf16),
        V((128, n), f32), V((n, rows), f32), V((n, 128), f32), V((128, rows), f32), V((rows, rows), f32),
        V((n_f, rows, cut), bf16),
    ]
    scratch += [
        D((7,)), D((5, n_f)), D((5, n_f)), D((2, 3, n_f)), D((2, 3, n_f)), D((3, n_c)), D((3, n_c)),
        D((8, n_f)), D((8, n_f)), D((5, n_c)), D((5, n_c)),
        D((7, n_z)), D((7, n_z)), D((7, n_z)), D((7, 2, n_z)), D((7, 2, n_z)), D((7, n_z)), D((7, n_z)), D((7, n_z)), D((7,)),
    ]
    return pl.pallas_call(
        functools.partial(kernel_m, n_f, n_c, n_y),
        out_shape=(S((rows, width), bf16), S((rows, width), bf16))
        + tuple(S((n_c,) + p + s, bf16) for p, s in zip(parts, wides)) + (S((8, uc), f32),),
        in_specs=[hbm] * 7 + [vmem] * 2,
        out_specs=(vmem, vmem) + (hbm,) * 4 + (vmem,),
        scratch_shapes=scratch,
        compiler_params=pltpu.CompilerParams(collective_id=0, has_side_effects=True, vmem_limit_bytes=63 * 2**20),
        name="layer",
    )(x, dy, wq, wu, wd, wn, pk, pat, vectors)


def kernel_d(od, ou, on, oq, out, gx, vec, fd, fu, fn, fq, o1, o2, bq, b1, b2, bu, n1g, n1b, n2g, n2b):
    for src, dst in ((od, fd), (ou, fu), (on, fn), (oq, fq)):
        dst[...] = src[...].astype(f32)
    o1[...] = out[...]
    o2[...] = gx[...]

    @pl.when(pl.program_id(0) == 0)
    def _():
        for ref, row in ((bq, 0), (bu, 1), (b1, 2), (b2, 2), (n1g, 3), (n1b, 4), (n2g, 5), (n2b, 6)):
            ref[...] = vec[row, 0 : ref.shape[0]]


def call_d(od, ou, on, oq, out, gx, vec, qc):
    steps, cut = 2, on.shape[0]
    S = jax.ShapeDtypeStruct

    def whole(n):
        return pl.BlockSpec((n,), lambda i: (0,))

    def block(a):
        return pl.BlockSpec((a.shape[0] // steps, a.shape[1]), lambda i: (i, 0))

    grads = (od, ou, on, oq)
    sizes = (qc, cut, cut, vec.shape[1], cut, cut, cut, cut)
    return pl.pallas_call(
        kernel_d,
        grid=(steps,),
        out_shape=tuple(S(a.shape, f32) for a in grads)
        + (S(out.shape, bf16), S(out.shape, bf16)) + tuple(S((n,), f32) for n in sizes),
        in_specs=[block(a) for a in grads + (out, gx)] + [pl.BlockSpec(vec.shape, lambda i: (0, 0))],
        out_specs=tuple(block(a) for a in grads + (out, gx)) + tuple(whole(n) for n in sizes),
        compiler_params=pltpu.CompilerParams(vmem_limit_bytes=62 * 2**20),
        name="widen",
    )(od, ou, on, oq, out, gx, vec)


def low(v):
    return v.astype(bf16)


def rotate_back(grad_part, cosine_table, sine_table):
    half_rot = ROT // 2
    g = grad_part[..., :ROT]
    b = g * sine_table[:, None, :]
    turned = jnp.concatenate([b[..., half_rot:], -b[..., :half_rot]], axis=-1)
    return jnp.concatenate([g * cosine_table[:, None, :] + turned, grad_part[..., ROT:]], axis=-1)


def body(
    tokens, segments, positions, cotangent, qkv_weight, qkv_bias, dense_weight, dense_bias,
    up_weight, up_bias, down_weight, down_bias, norm1_gain, norm1_bias, norm2_gain, norm2_bias,
):
    n_f, n_c = lax.axis_size("fsdp"), lax.axis_size("ctx")
    n_y = 2
    pk, vectors = call_p(positions, segments, norm1_gain, norm1_bias, norm2_gain, norm2_bias,
                         dense_bias, down_bias, qkv_bias, up_bias)
    out, gx, od, ou, on, oq, vec = call_m(
        n_f, n_c, n_y, tokens, cotangent, qkv_weight, up_weight, down_weight, dense_weight, pk, vectors)
    od, ou, on, oq = (a.reshape(-1, a.shape[-1]) for a in (od, ou, on, oq))
    gd, gu, gn, gq, out, gx, bq, b1, b2, bu, n1g, n1b, n2g, n2b = call_d(
        od, ou, on, oq, out, gx, vec, qkv_bias.shape[0])
    return out, gx, gq, bq, gn, b1, gu, bu, gd, b2, n1g, n1b, n2g, n2b


def rotary_tables(places):
    half_rot = ROT // 2
    inverse = 10000.0 ** (-2.0 * jnp.arange(half_rot, dtype=jnp.float32) / ROT)
    angles = places.astype(jnp.float32)[:, None] * inverse[None, :]
    angles = jnp.concatenate([angles, angles], axis=1)
    return (jnp.cos(angles), jnp.sin(angles))


def rotate(head_part, cosine_table, sine_table):
    half_rot = ROT // 2
    rotated_part = head_part[..., :ROT]
    turned = jnp.concatenate([-rotated_part[..., half_rot:], rotated_part[..., :half_rot]], axis=-1)
    rotated_part = rotated_part * cosine_table[:, None, :] + turned * sine_table[:, None, :]
    return jnp.concatenate([rotated_part, head_part[..., ROT:]], axis=-1)


def attention_pair(q, k, v, gc, doc):
    length = q.shape[0]
    place = jnp.arange(length, dtype=jnp.int32)
    visible = (place[None, :] <= place[:, None]) & (doc[None, :] == doc[:, None])
    scores = nt(q, k) * (1.0 / math.sqrt(HD))
    row_max = jnp.max(jnp.where(visible, scores, masked_fill), axis=-1, keepdims=True)
    terms = jnp.where(visible, jnp.exp(jnp.where(visible, scores - row_max, 0.0)), 0.0)
    total = jnp.sum(terms, axis=-1, keepdims=True)
    context = nn(low(terms), v) / total
    correction = jnp.sum(gc * context, axis=-1, keepdims=True) / total
    gw = low(gc / total)
    gv = tn(low(terms), gw)
    gs = low(terms * (nt(gw, v) - correction))
    gq = nn(gs, k) * (1.0 / math.sqrt(HD))
    gk = tn(gs, q) * (1.0 / math.sqrt(HD))
    return context, gq, gk, gv


def plain_body(
    tokens, segments, positions, cotangent, qkv_weight, qkv_bias, dense_weight, dense_bias,
    up_weight, up_bias, down_weight, down_bias, norm1_gain, norm1_bias, norm2_gain, norm2_bias,
):
    f32 = jnp.float32
    n_f, n_c = lax.axis_size("fsdp"), lax.axis_size("ctx")
    rows, width = tokens.shape
    heads = width // HD
    pairs = heads // n_c
    group = n_c // n_f
    me_c = lax.axis_index("ctx")
    me_f = lax.axis_index("fsdp")

    x = lax.all_gather(tokens, "fsdp", axis=0, tiled=True).astype(f32)
    dy = lax.all_gather(cotangent, "fsdp", axis=0, tiled=True)
    pos = lax.all_gather(positions, "fsdp", axis=0, tiled=True)
    docs = lax.all_gather(segments, ("fsdp", "ctx"), axis=0, tiled=True)
    w_qkv = lax.all_to_all(qkv_weight, "fsdp", 1, 0, tiled=True)
    w_up = lax.all_to_all(up_weight, "fsdp", 1, 0, tiled=True)
    norms = lax.all_gather(
        jnp.stack([norm1_gain, norm1_bias, norm2_gain, norm2_bias]), "fsdp", axis=1, tiled=True
    ).astype(f32)

    center = x - jnp.mean(x, axis=-1, keepdims=True)
    rstd = lax.rsqrt(jnp.mean(center * center, axis=-1, keepdims=True) + norm_eps)
    xhat = center * rstd
    normed_one = low(xhat * norms[0] + norms[1])
    normed_two = low(xhat * norms[2] + norms[3])

    mixed = nn(normed_one, w_qkv) + qkv_bias.astype(f32)
    total_rows = x.shape[0]
    cos, sin = rotary_tables(pos)
    mixed = mixed.reshape(total_rows, heads // n_f, 3, HD)
    mixed = jnp.stack(
        [rotate(mixed[:, :, 0], cos, sin), rotate(mixed[:, :, 1], cos, sin), mixed[:, :, 2]], axis=2
    )

    def to_heads(a, cols):
        a = a.reshape(n_f, rows, group, cols).transpose(0, 2, 1, 3).reshape(n_c, rows, cols)
        return lax.all_to_all(a, "ctx", 0, 0, tiled=True).reshape(n_c * rows, cols)

    def to_tokens(a, cols):
        a = lax.all_to_all(a.reshape(n_c, rows, cols), "ctx", 0, 0, tiled=True)
        return a.reshape(n_f, group, rows, cols).transpose(0, 2, 1, 3).reshape(total_rows, group * cols)

    qkv = to_heads(low(mixed).reshape(total_rows, -1), pairs * 3 * HD).reshape(-1, pairs, 3, HD)
    grad_context = nt(dy, dense_weight)
    gc = to_heads(low(grad_context), pairs * HD).reshape(-1, pairs, HD).astype(f32)
    seq_doc = lax.dynamic_slice_in_dim(docs, (me_c // group) * (n_c * rows), n_c * rows, 0)

    results = [
        attention_pair(qkv[:, i, 0], qkv[:, i, 1], qkv[:, i, 2], gc[:, i], seq_doc) for i in range(pairs)
    ]
    context = to_tokens(low(jnp.concatenate([r[0] for r in results], axis=1)), pairs * HD)
    grads = jnp.stack([jnp.stack(r[1:], axis=1) for r in results], axis=1)
    grads = to_tokens(low(grads).reshape(n_c * rows, -1), pairs * 3 * HD).astype(f32)
    grads = grads.reshape(total_rows, heads // n_f, 3, HD)
    grad_mixed = low(
        jnp.stack(
            [rotate_back(grads[:, :, 0], cos, sin), rotate_back(grads[:, :, 1], cos, sin), grads[:, :, 2]],
            axis=2,
        )
    ).reshape(total_rows, -1)

    up = nn(normed_two, w_up) + up_bias.astype(f32)
    active, pull = jax.vjp(lambda v: jax.nn.gelu(v, approximate=False), up)
    active = low(active)
    grad_up = low(pull(nt(dy, down_weight))[0])
    g_up_w = tn(normed_two, grad_up)
    g_up_b = jnp.sum(grad_up.astype(f32), axis=0)
    g_down_w = tn(active, dy)
    e_two = nt(grad_up, w_up)

    part = nn(context, dense_weight) + nn(active, down_weight)
    bias = lax.dynamic_update_slice_in_dim(
        jnp.zeros((width,), f32), dense_bias.astype(f32) + down_bias.astype(f32), me_f * (width // n_f), 0
    )
    part = low(part + bias)
    out = lax.psum_scatter(part, "fsdp", scatter_dimension=0, tiled=True).astype(f32)
    layer_out = low(tokens.astype(f32) + out)

    g_dense_w = tn(context, dy)
    g_qkv_w = tn(normed_one, grad_mixed)
    g_qkv_b = jnp.sum(grad_mixed.astype(f32), axis=0)
    e_one = nt(grad_mixed, w_qkv)
    h = low(e_one * norms[0] + e_two * norms[2])
    h = lax.psum_scatter(h, "fsdp", scatter_dimension=0, tiled=True).astype(f32)
    own_xhat = lax.dynamic_slice_in_dim(xhat, me_f * rows, rows, 0)
    own_rstd = lax.dynamic_slice_in_dim(rstd, me_f * rows, rows, 0)
    grad_in = own_rstd * (
        h - jnp.mean(h, axis=-1, keepdims=True) - own_xhat * jnp.mean(h * own_xhat, axis=-1, keepdims=True)
    )
    grad_tokens = low(cotangent.astype(f32) + grad_in)
    vecs = jnp.stack(
        [jnp.sum(e_one * xhat, 0), jnp.sum(e_one, 0), jnp.sum(e_two * xhat, 0), jnp.sum(e_two, 0)]
    )
    vecs = lax.psum(lax.psum_scatter(vecs, "fsdp", scatter_dimension=1, tiled=True), "ctx")
    dy_sum = jnp.sum(cotangent.astype(f32), axis=0)
    dy_sum = lax.psum(lax.psum_scatter(dy_sum, "fsdp", scatter_dimension=0, tiled=True), "ctx")
    g_qkv_b = lax.psum(g_qkv_b, "ctx")
    g_up_b = lax.psum(g_up_b, "ctx")

    def reduced(g, columns):
        if columns:
            g = lax.psum_scatter(low(g).reshape(n_f, -1, g.shape[1]), "ctx", scatter_dimension=1, tiled=True)
            g = lax.all_to_all(g, "fsdp", 0, 0, tiled=True)
            g = g.transpose(1, 0, 2).reshape(g.shape[1], -1)
            return lax.all_gather(g, "ctx", axis=0, tiled=True).astype(f32)
        g = lax.psum_scatter(low(g), "ctx", scatter_dimension=0, tiled=True)
        return lax.all_gather(g, "ctx", axis=0, tiled=True).astype(f32)

    return (
        layer_out, grad_tokens,
        reduced(g_qkv_w, True), g_qkv_b, reduced(g_dense_w, False), dy_sum,
        reduced(g_up_w, True), g_up_b, reduced(g_down_w, False), dy_sum,
        vecs[0], vecs[1], vecs[2], vecs[3],
    )


def solution(mesh):
    n_f, n_c = mesh.shape["fsdp"], mesh.shape["ctx"]
    fits = n_c % n_f == 0 and n_c == 8 and n_f == 4
    row, flat, w, b = P(("fsdp", "ctx"), None), P(("fsdp", "ctx")), P("fsdp", None), P("fsdp")
    return jax.shard_map(
        body if fits else plain_body,
        mesh=mesh,
        in_specs=(row, flat, flat, row, w, b, w, b, w, b, w, b, b, b, b, b),
        out_specs=(row, row, w, b, w, b, w, b, w, b, b, b, b, b),
        check_vma=False,
    )
```
